512 devices in a mesh: centres: 128 (over x, z, core), rep: 4 (over y).
Axes of the slice: x: 4, y: 4, z: 16, core: 2. Of those that a mesh axis runs over, the one named last changes fastest.
Arguments:
- embeddings: bfloat16 [4096, 512], P(('centres', 'rep'))
- bn_gain: float32 [512], replicated, may hold values from 0.5 to 2
- bn_bias: float32 [512], replicated, may hold values from -3 to 3
- centres: bfloat16 [262144, 512], P('centres'), may hold values from -6 to 6
- sample_rows: int32 [128, 768], P('centres'), may hold values from 0 to 2047, as said below
- label_shard: int32 [128, 4, 8], P(None, 'rep'), may hold values from 0 to 127
- label_slot: int32 [128, 4, 8], P(None, 'rep'), may hold values from 0 to 767
Outputs:
- row_loss: float32 [4096], P(('centres', 'rep'))
- emb_grad: float32 [4096, 512], P(('centres', 'rep'))
- centre_grad: bfloat16 [98304, 512], P('centres')
- gain_grad: float32 [512], replicated
- bias_grad: float32 [512], replicated
The draws below stay inside these ranges and needn't reach their ends.
Inputs may be any that keep to these rules, and one draw needn't show every extreme that they name: `sample_rows`: within each shard's row the entries are distinct.
All inputs are finite; a program needn't handle non-finite values.
Results may differ from the reference program's by a relative error of at most 0.0059.
Values may be sent and summed in bfloat16 or wider, within the bound.
No kernel may reach another device: no remote copies, remote signals or barrier semaphores. Data moves between devices by JAX's collectives and lax.ppermute only.
A program may use at most 64 MiB of HBM per device.

```python
import math
import jax
import jax.numpy as jnp
from jax import lax

D = 512
S_DEV = 768
CLS_DEV = 2048
B_DEV = 8
BATCH = 4096
CLASSES = 262144
N_CENTRES = 128
N_REP = 4


def draw_embeddings(key, part):
    key = jax.random.fold_in(key, 1)
    key_list = jax.random.split(key, 4)
    noise_field = jax.random.normal(key_list[0], (BATCH, D), jnp.float32)
    col_scale = jnp.exp(jax.random.uniform(key_list[1], (1, D), jnp.float32) * math.log(10.0))
    col_shift = jax.random.normal(key_list[2], (1, D), jnp.float32)
    rising = jnp.exp(jnp.arange(BATCH, dtype=jnp.float32)[:, None] * (math.log(3.0) / BATCH))
    row_scale = jnp.exp(jax.random.uniform(key_list[3], (BATCH, 1), jnp.float32) * math.log(10.0))
    return ((noise_field * col_scale + col_shift) * row_scale * rising).astype(jnp.bfloat16)


def draw_sample_rows(key, part):
    key = jax.random.fold_in(key, 2)
    shard_keys = jax.random.split(key, N_CENTRES)
    chosen = jax.vmap(lambda one_key: jax.random.permutation(one_key, CLS_DEV)[:S_DEV])(shard_keys)
    return chosen.astype(jnp.int32)


def touch_ends(entries, key, smallest, high):
    longest = entries.shape.index(max(entries.shape))
    spots = []
    for shift in (0, 1):
        where = [jax.random.randint(jax.random.fold_in(key, axis), (), 0, length) for axis, length in enumerate(entries.shape)]
        where[longest] = (where[longest] + shift) % entries.shape[longest]
        spots.append(tuple(where))
    return entries.at[spots[0]].set(smallest).at[spots[1]].set(high)


def steps_of(rng, extent, pieces, least, top_value):
    def one(position, shards_of):
        heights = jax.random.uniform(jax.random.fold_in(jax.random.fold_in(rng, 6), position), (shards_of,), jnp.float32, least / len(pieces), top_value / len(pieces))
        return jnp.repeat(jnp.exp(heights), extent[position] // shards_of).reshape((-1,) + (1,) * (len(extent) - position - 1))

    factor_of = one(*pieces[0])
    for cut in pieces[1:]:
        factor_of = factor_of * one(*cut)
    return factor_of


def scatter_about(key, dims, deviation, reach, cuts=(), held_as=jnp.bfloat16):
    array = jax.random.normal(key, dims, jnp.float32) * deviation
    if len(cuts) > 0:
        array = steps_of(key, dims, cuts, -0.22, 0.18) * array
    return jnp.clip(array, min=-reach, max=reach).astype(held_as)


def setup_inputs(seed: int = 0) -> dict:
    keys = jax.random.split(jax.random.key(seed), 8)
    embeddings = draw_embeddings(jax.random.fold_in(keys[7], 71), 0)
    bn_gain = jnp.clip(jnp.exp(jax.random.uniform(keys[1], (D,), jnp.float32, math.log(0.5), math.log(2.0))), 0.5, 2.0)
    bn_bias = scatter_about(keys[2], (D,), 0.5, 3.0, (), jnp.float32)
    centres = scatter_about(keys[3], (CLASSES, D), 1.0, 6.0, ((0, 128),))
    sample_rows = draw_sample_rows(jax.random.fold_in(keys[7], 71), 0)
    label_shard = touch_ends(jax.random.randint(keys[5], (N_CENTRES, N_REP, B_DEV), 0, N_CENTRES), jax.random.fold_in(keys[5], 1), 0, N_CENTRES - 1).astype(jnp.int32)
    label_slot = touch_ends(jax.random.randint(keys[6], (N_CENTRES, N_REP, B_DEV), 0, S_DEV), jax.random.fold_in(keys[6], 1), 0, S_DEV - 1).astype(jnp.int32)
    return {"embeddings": embeddings, "bn_gain": bn_gain, "bn_bias": bn_bias, "centres": centres, "sample_rows": sample_rows, "label_shard": label_shard, "label_slot": label_slot}


LOGIT_SCALE = 64.0
MARGIN = 0.4
EPSILON = 1e-05

def reference(embeddings, bn_gain, bn_bias, centres, sample_rows, label_shard, label_slot):
    batch_total = BATCH
    inputs = embeddings.astype(jnp.float32)
    col_mean = lax.optimization_barrier(jnp.sum(inputs, 0)) / batch_total
    col_var = lax.optimization_barrier(jnp.sum(inputs * inputs, 0)) / batch_total - col_mean * col_mean
    inv_std = lax.rsqrt(col_var + EPSILON)
    normed = (inputs - col_mean) * inv_std
    shifted = normed * bn_gain + bn_bias
    row_scale = lax.rsqrt(lax.optimization_barrier(jnp.sum(shifted * shifted, 1, keepdims=True)) + EPSILON)
    unit_f = shifted * row_scale
    unit = unit_f.astype(jnp.bfloat16)
    table = centres.reshape(N_CENTRES, CLS_DEV, D)
    picked = jnp.take_along_axis(table, sample_rows[:, :, None], axis=1).astype(jnp.float32)
    inv_norm = lax.rsqrt(lax.optimization_barrier(jnp.sum(picked * picked, 2, keepdims=True)) + EPSILON)
    w_unit = picked * inv_norm
    w_hat = w_unit.astype(jnp.bfloat16)
    shard_ids = jnp.arange(N_CENTRES, dtype=jnp.int32)
    columns = jnp.arange(S_DEV, dtype=jnp.int32)
    unit_groups = unit.reshape(N_CENTRES, N_REP, B_DEV, D)
    loss_parts = []
    grad_parts = []
    raw_grad = jnp.zeros((N_CENTRES, S_DEV, D), jnp.float32)
    for replica in range(N_REP):
        group_rows = unit_groups[:, replica].reshape(N_CENTRES * B_DEV, D)
        owners = label_shard[:, replica].reshape(-1)
        slot_ids = label_slot[:, replica].reshape(-1)

        def logits_of(shard_at, w_shard):
            cosine = jnp.dot(group_rows, w_shard.T, preferred_element_type=jnp.float32)
            targets = (owners[:, None] == shard_at) & (slot_ids[:, None] == columns[None, :])
            logits = LOGIT_SCALE * cosine - jnp.where(targets, LOGIT_SCALE * MARGIN, 0.0)
            return (logits, targets)

        def first_pass(carry, scan_item):
            logits, targets = logits_of(scan_item[0], scan_item[1])
            local_sum = lax.optimization_barrier(jnp.sum(jnp.exp(logits), 1))
            target_logit = lax.optimization_barrier(jnp.sum(jnp.where(targets, logits, 0.0), 1))
            return ((carry[0] + local_sum, carry[1] + target_logit), None)
        rows_count = N_CENTRES * B_DEV
        start_stats = (jnp.zeros((rows_count,), jnp.float32), jnp.zeros((rows_count,), jnp.float32))
        (row_total, target_logit), _ = lax.scan(first_pass, start_stats, (shard_ids, w_hat))

        def second_pass(running, scan_item):
            logits, targets = logits_of(scan_item[0], scan_item[1])
            probability = jnp.exp(logits) / row_total[:, None]
            grad_cos = (probability - targets.astype(jnp.float32)).astype(jnp.bfloat16)
            running = running + jnp.dot(grad_cos, scan_item[1], preferred_element_type=jnp.float32)
            grad_rows = lax.dot_general(grad_cos, group_rows, (((0,), (0,)), ((), ())), preferred_element_type=jnp.float32)
            return (running, grad_rows)
        grad_unit_r, grad_rows_all = lax.scan(second_pass, jnp.zeros((rows_count, D), jnp.float32), (shard_ids, w_hat))
        raw_grad = raw_grad + grad_rows_all
        loss_parts.append(jnp.log(row_total) - target_logit)
        grad_parts.append(grad_unit_r)
    row_loss = jnp.stack(loss_parts).reshape(N_REP, N_CENTRES, B_DEV).transpose(1, 0, 2).reshape(BATCH)
    grad_unit = jnp.stack(grad_parts).reshape(N_REP, N_CENTRES, B_DEV, D).transpose(1, 0, 2, 3).reshape(BATCH, D)
    radial_c = lax.optimization_barrier(jnp.sum(w_unit * raw_grad, 2, keepdims=True))
    centre_grad = ((raw_grad - w_unit * radial_c) * inv_norm).astype(jnp.bfloat16).reshape(N_CENTRES * S_DEV, D)
    radial = lax.optimization_barrier(jnp.sum(unit_f * grad_unit, 1, keepdims=True))
    grad_shift = (grad_unit - unit_f * radial) * row_scale
    bias_grad = lax.optimization_barrier(jnp.sum(grad_shift, 0))
    gain_grad = lax.optimization_barrier(jnp.sum(grad_shift * normed, 0))
    emb_grad = inv_std * (grad_shift * bn_gain - bn_gain * bias_grad / batch_total - normed * (bn_gain * gain_grad / batch_total))
    return (row_loss, emb_grad, centre_grad, gain_grad, bias_grad)
```

```python
import jax
import jax.numpy as jnp
from jax import lax
from jax.sharding import Mesh, PartitionSpec as P

LOGIT_SCALE = 64.0
MARGIN = 0.4
EPSILON = 1e-05
F32 = jnp.float32
BF16 = jnp.bfloat16


def spread(block, axes):
    copies = jnp.broadcast_to(block[None], (lax.axis_size(axes),) + block.shape)
    return lax.all_to_all(copies, axes, 0, 0)


def swap_cores(block):
    return lax.ppermute(block, "core", [(0, 1), (1, 0)])


def body(embeddings, bn_gain, bn_bias, centres, sample_rows, label_shard, label_slot):
    nx, nz, nc, nr = (lax.axis_size(a) for a in ("x", "z", "core", "rep"))
    ix, iz, ic, ir = (lax.axis_index(a) for a in ("x", "z", "core", "rep"))
    rows_dev, width = embeddings.shape
    slots = sample_rows.shape[1]
    batch_total = rows_dev * nx * nz * nc * nr
    group = nx * nz * rows_dev

    line = spread(embeddings, "z").reshape(nz * rows_dev, width)
    line_f = line.astype(F32)
    line_sums = jnp.stack([jnp.sum(line_f, 0), jnp.sum(line_f * line_f, 0)])
    sums = jnp.sum(spread(line_sums, ("x", "core", "rep")), 0)
    rows = spread(line, "x").reshape(group, width)

    picked = jnp.take(centres, sample_rows[0], axis=0).astype(F32)
    inv_norm = lax.rsqrt(jnp.sum(picked * picked, 1, keepdims=True) + EPSILON)
    w_unit = picked * inv_norm
    w_own = w_unit.astype(BF16)
    w_hat = jnp.concatenate([w_own, swap_cores(w_own)], 0)

    def mine(labels):
        return jnp.take(labels.reshape(nx * nz, nc, rows_dev), ic, axis=1).reshape(group)

    owner = mine(label_shard)
    slot = mine(label_slot)
    chip = (ix * nz + iz) * nc
    place = jnp.where(
        owner == chip + ic, slot, jnp.where(owner == chip + 1 - ic, slot + slots, -1)
    )
    columns = jnp.arange(nc * slots, dtype=jnp.int32)
    targets = place[:, None] == columns[None, :]

    hit = jnp.dot(targets.astype(BF16), w_hat, preferred_element_type=F32).astype(BF16)
    hit = lax.all_to_all(hit.reshape(nx, nz * rows_dev, width), "x", 0, 0)
    hit = jnp.sum(hit.astype(F32), 0).astype(BF16)
    hit = lax.all_to_all(hit.reshape(nz, rows_dev, width), "z", 0, 0)
    w_target = jnp.sum(hit.astype(F32), 0)

    col_mean = sums[0] / batch_total
    col_var = sums[1] / batch_total - col_mean * col_mean
    inv_std = lax.rsqrt(col_var + EPSILON)

    def head(inputs):
        normed = (inputs.astype(F32) - col_mean) * inv_std
        shifted = normed * bn_gain + bn_bias
        row_scale = lax.rsqrt(jnp.sum(shifted * shifted, 1, keepdims=True) + EPSILON)
        return normed, shifted * row_scale, row_scale

    unit = head(rows)[1].astype(BF16)
    cosine = jnp.dot(unit, w_hat.T, preferred_element_type=F32)
    exp_logits = jnp.exp(
        LOGIT_SCALE * cosine - jnp.where(targets, LOGIT_SCALE * MARGIN, 0.0)
    )
    part = jnp.sum(exp_logits, 1)
    part = jnp.sum(spread(part, "x"), 0)
    row_total = jnp.sum(spread(part, "z"), 0)

    others = jnp.where(targets, 0.0, exp_logits).astype(BF16)
    pull = jnp.dot(others, w_hat, preferred_element_type=F32).astype(BF16)
    pull = lax.all_to_all(pull.reshape(nx, nz * rows_dev, width), "x", 0, 0)
    pull = jnp.sum(pull.astype(F32), 0).astype(BF16)
    pull = lax.all_to_all(pull.reshape(nz, rows_dev, width), "z", 0, 0)
    pull = jnp.sum(pull.astype(F32), 0)

    normed, unit_f, row_scale = head(embeddings)
    own_total = lax.dynamic_slice_in_dim(
        row_total, (ix * nz + iz) * rows_dev, rows_dev, 0
    )[:, None]
    own_unit = unit_f.astype(BF16).astype(F32)
    target_logit = LOGIT_SCALE * jnp.sum(own_unit * w_target, 1, keepdims=True) - (
        LOGIT_SCALE * MARGIN
    )
    row_loss = (jnp.log(own_total) - target_logit)[:, 0]
    weight = (jnp.exp(target_logit) / own_total - 1.0).astype(BF16).astype(F32)
    grad_unit = pull / own_total + weight * w_target
    radial = jnp.sum(unit_f * grad_unit, 1, keepdims=True)
    grad_shift = (grad_unit - unit_f * radial) * row_scale
    ends = jnp.stack([jnp.sum(grad_shift, 0), jnp.sum(grad_shift * normed, 0)])
    ends = jnp.sum(spread(ends, "z"), 0)
    ends = jnp.sum(spread(ends, ("x", "core", "rep")), 0)
    bias_grad, gain_grad = ends[0], ends[1]
    emb_grad = inv_std * (
        grad_shift * bn_gain
        - bn_gain * bias_grad / batch_total
        - normed * (bn_gain * gain_grad / batch_total)
    )

    grad_cos = (exp_logits / row_total[:, None] - targets.astype(F32)).astype(BF16)
    raw = lax.dot_general(
        grad_cos, unit, (((0,), (0,)), ((), ())), preferred_element_type=F32
    )
    raw = raw[:slots] + swap_cores(raw[slots:].astype(BF16)).astype(F32)
    quarter = slots // nr
    raw = lax.all_to_all(raw.astype(BF16).reshape(nr, quarter, width), "rep", 0, 0)
    raw = jnp.sum(raw.astype(F32), 0)
    w_part = lax.dynamic_slice_in_dim(w_unit, ir * quarter, quarter, 0)
    n_part = lax.dynamic_slice_in_dim(inv_norm, ir * quarter, quarter, 0)
    along = jnp.sum(w_part * raw, 1, keepdims=True)
    grad = ((raw - w_part * along) * n_part).astype(BF16)
    centre_grad = spread(grad, "rep").reshape(slots, width)
    return (row_loss, emb_grad, centre_grad, gain_grad, bias_grad)


def solution(mesh):
    shards, replicas = mesh.devices.shape
    split = (4, shards // 8, 2, replicas)
    fine = Mesh(mesh.devices.reshape(split), ("x", "z", "core", "rep"))
    cen = ("x", "z", "core")
    every = cen + ("rep",)
    return jax.shard_map(
        body,
        mesh=fine,
        in_specs=(
            P(every, None),
            P(),
            P(),
            P(cen, None),
            P(cen, None),
            P(None, "rep", None),
            P(None, "rep", None),
        ),
        out_specs=(P(every), P(every, None), P(cen, None), P(), P()),
        check_vma=False,
    )
```

```python
import jax
import jax.numpy as jnp
from jax import lax
from jax.experimental import pallas as pl
from jax.experimental.pallas import tpu as pltpu
from jax.sharding import Mesh, PartitionSpec as P

LOGIT_SCALE = 64.0
MARGIN = 0.4
EPSILON = 1e-05
F32 = jnp.float32
BF16 = jnp.bfloat16
VMEM = 48 * 1024 * 1024
PAD = 16


def spread(block, axes):
    copies = jnp.broadcast_to(block[None], (lax.axis_size(axes),) + block.shape)
    return lax.all_to_all(copies, axes, 0, 0)


def shift(block, axis, by):
    n = lax.axis_size(axis)
    return lax.ppermute(block, axis, [(i, (i + by) % n) for i in range(n)])


def head(inputs, sums, gain, bias, batch_total):
    mean = sums[0:1] / batch_total
    inv_std = lax.rsqrt(sums[1:2] / batch_total - mean * mean + EPSILON)
    normed = (inputs.astype(F32) - mean) * inv_std
    shifted = normed * gain + bias
    scale = lax.rsqrt(jnp.sum(shifted * shifted, 1, keepdims=True) + EPSILON)
    return normed, shifted * scale, scale, inv_std


def call(kernel, grid, ins, outs, shapes, scratch, flops, size, exps=0):
    return pl.pallas_call(
        kernel,
        grid=(grid,),
        in_specs=ins,
        out_specs=outs,
        out_shape=shapes,
        scratch_shapes=scratch,
        compiler_params=pltpu.CompilerParams(vmem_limit_bytes=VMEM),
        cost_estimate=pl.CostEstimate(
            flops=flops, bytes_accessed=size, transcendentals=exps
        ),
    )


def whole(*shape):
    return pl.BlockSpec(shape, lambda i: (0,) * len(shape))


def rows_of(block, width):
    return pl.BlockSpec((block, width), lambda i: (i, 0))


def hits(place, block, count, first):
    return place == lax.broadcasted_iota(jnp.int32, (block, count), 0) + first


def exp_kernel(batch, rows, sums, gain, bias, place, w_hat, unit, expo, stats):
    i = pl.program_id(0)
    block, count = expo.shape

    @pl.when(i == 0)
    def _():
        total = jnp.sum(sums[...], 0)
        unit[...] = head(rows[...], total, gain[...], bias[...], batch)[1].astype(BF16)
        stats[...] = jnp.zeros_like(stats)

    cosine = lax.dot_general(
        w_hat[...], unit[...], (((1,), (1,)), ((), ())), preferred_element_type=F32
    )
    target = hits(place[...], block, count, i * block)
    logits = LOGIT_SCALE * cosine - jnp.where(target, LOGIT_SCALE * MARGIN, 0.0)
    exps = jnp.exp(logits)
    expo[...] = exps
    stats[0:1] += jnp.sum(exps, 0, keepdims=True)
    stats[1:2] += jnp.sum(jnp.where(target, logits, 0.0), 0, keepdims=True)


def grad_of(expo, total, place, first):
    block, count = expo.shape
    target = hits(place, block, count, first)
    return (expo / total - target.astype(F32)).astype(BF16)


def pull_kernel(
    batch, parts, rows, sums, gain, bias, place, totals, w_hat, expo, packed, acc
):
    i = pl.program_id(0)
    block = expo.shape[0]
    grad = grad_of(expo[...], totals[0:1], place[...], i * block)
    term = lax.dot_general(
        grad, w_hat[...], (((0,), (0,)), ((), ())), preferred_element_type=F32
    )

    @pl.when(i == 0)
    def _():
        acc[...] = term

    @pl.when(i > 0)
    def _():
        acc[...] += term

    @pl.when(i == pl.num_programs(0) - 1)
    def _():
        total = jnp.sum(sums[...], 0)
        normed, unit_f, scale, _ = head(rows[...], total, gain[...], bias[...], batch)
        pull = acc[...]
        radial = jnp.sum(unit_f * pull, 1, keepdims=True)
        shifts = (pull - unit_f * radial) * scale
        bias_part = jnp.sum(shifts, 0, keepdims=True)
        gain_part = jnp.sum(shifts * normed, 0, keepdims=True)
        tail = pack_ends(bias_part, gain_part)
        n = pull.shape[0] // parts
        for p in range(parts):
            packed[p, :n] = pull[p * n : (p + 1) * n].astype(BF16)
            packed[p, n:] = tail


def pack_ends(bias_part, gain_part):
    pieces = []
    for value in (bias_part, gain_part):
        for _ in range(3):
            piece = value.astype(BF16)
            value = value - piece.astype(F32)
            pieces.append(piece.astype(F32))
    fill = jnp.zeros((PAD - 6, bias_part.shape[1]), F32)
    return jnp.concatenate(pieces + [fill], 0).astype(BF16)


def unpack_ends(tail):
    tail = tail.astype(F32)
    return jnp.concatenate(
        [
            jnp.sum(tail[0:3], 0, keepdims=True),
            jnp.sum(tail[3:6], 0, keepdims=True),
        ],
        0,
    )


def mid_kernel(lines, rows_dev, arrived, packed):
    total = jnp.sum(arrived[...].astype(F32), 0)
    n = lines * rows_dev
    ends = unpack_ends(total[n:])
    tail = pack_ends(ends[0:1], ends[1:2]).astype(F32)
    both = PAD // rows_dev
    for p in range(lines):
        piece = total[p * rows_dev : (p + 1) * rows_dev]
        fill = [tail[: PAD - rows_dev]]
        packed[p] = jnp.concatenate([piece] + fill, 0).astype(BF16)


def raw_kernel(place, totals, unit, expo, own, other):
    i = pl.program_id(0)
    block = expo.shape[0]
    half = pl.num_programs(0) // 2
    grad = grad_of(expo[...], totals[0:1], place[...], i * block)
    term = jnp.dot(grad, unit[...], preferred_element_type=F32)

    @pl.when(i < half)
    def _():
        own[...] = term

    @pl.when(i >= half)
    def _():
        other[...] = term.astype(BF16)


def body(embeddings, bn_gain, bn_bias, centres, sample_rows, label_shard, label_slot):
    nx, nz, nc, nr = (lax.axis_size(a) for a in ("x", "z", "core", "rep"))
    ix, iz, ic, ir = (lax.axis_index(a) for a in ("x", "z", "core", "rep"))
    rows_dev, width = embeddings.shape
    slots = sample_rows.shape[1]
    batch = rows_dev * nx * nz * nc * nr
    line_rows = nz * rows_dev
    group = nx * line_rows
    held = nc * slots
    gain, bias = bn_gain[None], bn_bias[None]

    line = spread(embeddings, "z").reshape(line_rows, width)
    rows = spread(line, "x").reshape(group, width)
    rows_f = rows.astype(F32)
    sums = spread(
        jnp.stack([jnp.sum(rows_f, 0), jnp.sum(rows_f * rows_f, 0)]), ("core", "rep")
    )
    peers = nc * nr

    picked = jnp.take(centres, sample_rows[0], axis=0).astype(F32)
    inv_norm = lax.rsqrt(jnp.sum(picked * picked, 1, keepdims=True) + EPSILON)
    w_unit = picked * inv_norm
    w_own = w_unit.astype(BF16)
    w_hat = jnp.concatenate([w_own, shift(w_own, "core", 1)], 0)

    def mine(labels):
        return jnp.take(labels.reshape(nx * nz, nc, rows_dev), ic, axis=1).reshape(
            1, group
        )

    owner = mine(label_shard)
    slot = mine(label_slot)
    chip = (ix * nz + iz) * nc
    place = jnp.where(
        owner == chip + ic, slot, jnp.where(owner == chip + 1 - ic, slot + slots, -1)
    )

    def exp_call():
        block = held // 3
        return call(
            lambda *refs: exp_kernel(batch, *refs),
            3,
            [
                whole(group, width),
                whole(peers, 2, width),
                whole(1, width),
                whole(1, width),
                whole(1, group),
                rows_of(block, width),
            ],
            [whole(group, width), rows_of(block, group), whole(2, group)],
            [
                jax.ShapeDtypeStruct((group, width), BF16),
                jax.ShapeDtypeStruct((held, group), F32),
                jax.ShapeDtypeStruct((2, group), F32),
            ],
            [],
            2 * held * group * width,
            4 * held * group + 2 * held * width,
            held * group,
        )(rows, sums, gain, bias, place, w_hat)

    unit, expo, stats = exp_call()
    stats = jnp.sum(spread(stats, "x"), 0)
    stats = jnp.sum(spread(stats, "z"), 0)

    pull = call(
        lambda *refs: pull_kernel(batch, nx, *refs),
        3,
        [
            whole(group, width),
            whole(peers, 2, width),
            whole(1, width),
            whole(1, width),
            whole(1, group),
            whole(2, group),
            rows_of(held // 3, width),
            rows_of(held // 3, group),
        ],
        whole(nx, line_rows + PAD, width),
        jax.ShapeDtypeStruct((nx, line_rows + PAD, width), BF16),
        [pltpu.VMEM((group, width), F32)],
        2 * held * group * width,
        4 * held * group + 2 * held * width,
    )(rows, sums, gain, bias, place, stats, w_hat, expo)
    pull = lax.all_to_all(pull, "x", 0, 0)
    pull = call(
        lambda *refs: mid_kernel(nz, rows_dev, *refs),
        1,
        [whole(nx, line_rows + PAD, width)],
        whole(nz, PAD, width),
        jax.ShapeDtypeStruct((nz, PAD, width), BF16),
        [],
        nx * line_rows * width,
        2 * nx * line_rows * width,
    )(pull)
    pull = jnp.sum(lax.all_to_all(pull, "z", 0, 0).astype(F32), 0)
    grad_unit = pull[:rows_dev]
    ends = jnp.sum(spread(unpack_ends(pull[rows_dev:]), ("core", "rep")), 0)

    own_stats = lax.dynamic_slice_in_dim(
        stats, (ix * nz + iz) * rows_dev, rows_dev, 1
    )
    row_loss = jnp.log(own_stats[0]) - own_stats[1]
    normed, unit_f, row_scale, inv_std = head(
        embeddings, jnp.sum(sums, 0), gain, bias, batch
    )
    radial = jnp.sum(unit_f * grad_unit, 1, keepdims=True)
    grad_shift = (grad_unit - unit_f * radial) * row_scale
    bias_grad, gain_grad = ends[0], ends[1]
    emb_grad = inv_std * (
        grad_shift * bn_gain
        - bn_gain * bias_grad / batch
        - normed * (bn_gain * gain_grad / batch)
    )

    raw_block = slots // 2
    own, other = call(
        raw_kernel,
        4,
        [
            whole(1, group),
            whole(2, group),
            whole(group, width),
            rows_of(raw_block, group),
        ],
        [
            pl.BlockSpec((raw_block, width), lambda i: (jnp.minimum(i, 1), 0)),
            pl.BlockSpec((raw_block, width), lambda i: (jnp.maximum(i - 2, 0), 0)),
        ],
        [
            jax.ShapeDtypeStruct((slots, width), F32),
            jax.ShapeDtypeStruct((slots, width), BF16),
        ],
        [],
        2 * held * group * width,
        4 * held * group + 6 * slots * width,
    )(place, stats, unit, expo)
    raw = own + shift(other, "core", 1).astype(F32)
    quarter = slots // nr
    sent = raw.astype(BF16).reshape(nr, quarter, width)

    def piece(whole_array, at):
        return lax.dynamic_index_in_dim(whole_array, at, 0, keepdims=False)

    mine_raw = piece(raw.reshape(nr, quarter, width), ir)
    for by in range(1, nr):
        mine_raw = mine_raw + shift(
            piece(sent, lax.rem(ir + by, nr)), "rep", by
        ).astype(F32)
    w_part = piece(w_unit.reshape(nr, quarter, width), ir)
    n_part = piece(inv_norm.reshape(nr, quarter, 1), ir)
    along = jnp.sum(w_part * mine_raw, 1, keepdims=True)
    grad = ((mine_raw - w_part * along) * n_part).astype(BF16)
    found = jnp.stack([grad] + [shift(grad, "rep", by) for by in range(1, nr)])
    order = lax.rem(ir - jnp.arange(nr, dtype=jnp.int32) + nr, nr)
    centre_grad = jnp.take(found, order, axis=0).reshape(slots, width)
    return (row_loss, emb_grad, centre_grad, ends[1], ends[0])


def solution(mesh):
    shards, replicas = mesh.devices.shape
    split = (4, shards // 8, 2, replicas)
    fine = Mesh(mesh.devices.reshape(split), ("x", "z", "core", "rep"))
    cen = ("x", "z", "core")
    every = cen + ("rep",)
    return jax.shard_map(
        body,
        mesh=fine,
        in_specs=(
            P(every, None),
            P(),
            P(),
            P(cen, None),
            P(cen, None),
            P(None, "rep", None),
            P(None, "rep", None),
        ),
        out_specs=(P(every), P(every, None), P(cen, None), P(), P()),
        check_vma=False,
    )
```

```python
import jax
import jax.numpy as jnp
from jax import lax
from jax.experimental import pallas as pl
from jax.experimental.pallas import tpu as pltpu
from jax.sharding import Mesh, PartitionSpec as P

LOGIT_SCALE = 64.0
MARGIN = 0.4
EPSILON = 1e-05
F32 = jnp.float32
BF16 = jnp.bfloat16
VMEM = 60 * 1024 * 1024
PAD = 16


def spread(block, axes):
    copies = jnp.broadcast_to(block[None], (lax.axis_size(axes),) + block.shape)
    return lax.all_to_all(copies, axes, 0, 0)


def shift(block, axis, by):
    n = lax.axis_size(axis)
    return lax.ppermute(block, axis, [(i, (i + by) % n) for i in range(n)])


def head(inputs, sums, gain, bias, batch_total):
    mean = sums[0:1] / batch_total
    inv_std = lax.rsqrt(sums[1:2] / batch_total - mean * mean + EPSILON)
    normed = (inputs.astype(F32) - mean) * inv_std
    shifted = normed * gain + bias
    scale = lax.rsqrt(jnp.sum(shifted * shifted, 1, keepdims=True) + EPSILON)
    return normed, shifted * scale, scale, inv_std


def call(kernel, grid, ins, outs, shapes, scratch, flops, size, exps=0):
    return pl.pallas_call(
        kernel,
        grid=(grid,),
        in_specs=ins,
        out_specs=outs,
        out_shape=shapes,
        scratch_shapes=scratch,
        compiler_params=pltpu.CompilerParams(vmem_limit_bytes=VMEM),
        cost_estimate=pl.CostEstimate(
            flops=flops, bytes_accessed=size, transcendentals=exps
        ),
    )


def whole(*shape):
    return pl.BlockSpec(shape, lambda i: (0,) * len(shape))


def rows_of(block, width):
    return pl.BlockSpec((block, width), lambda i: (i, 0))


def hits(place, block, count, first):
    return place == lax.broadcasted_iota(jnp.int32, (block, count), 0) + first


def exp_kernel(
    batch, rows, sums, gain, bias, place, w_own, w_other, unit, expo, stats, acc
):
    i = pl.program_id(0)
    half = pl.num_programs(0) // 2
    block, count = expo.shape

    @pl.when(i == 0)
    def _():
        total = jnp.sum(sums[...], 0)
        unit[...] = head(rows[...], total, gain[...], bias[...], batch)[1].astype(BF16)
        acc[...] = jnp.zeros_like(acc)

    w_hat = jnp.where(i < half, w_own[...], w_other[...])
    cosine = lax.dot_general(
        w_hat, unit[...], (((1,), (1,)), ((), ())), preferred_element_type=F32
    )
    target = hits(place[...], block, count, i * block)
    logits = LOGIT_SCALE * cosine - jnp.where(target, LOGIT_SCALE * MARGIN, 0.0)
    exps = jnp.exp(logits)
    expo[...] = exps
    acc[0:1] += jnp.sum(exps, 0, keepdims=True)
    acc[1:2] += jnp.sum(jnp.where(target, logits, 0.0), 0, keepdims=True)

    @pl.when(i == pl.num_programs(0) - 1)
    def _():
        for p in range(stats.shape[0]):
            stats[p] = acc[...]


def pull_kernel(
    batch,
    parts,
    rows,
    sums,
    gain,
    bias,
    place,
    totals,
    w_own,
    w_other,
    expo,
    packed,
    acc,
):
    i = pl.program_id(0)
    half = pl.num_programs(0) // 2
    block, count = expo.shape
    target = hits(place[...], block, count, i * block)
    grad = (expo[...] / totals[0:1] - target.astype(F32)).astype(BF16)
    w_hat = jnp.where(i < half, w_own[...], w_other[...])
    term = lax.dot_general(
        grad, w_hat, (((0,), (0,)), ((), ())), preferred_element_type=F32
    )

    @pl.when(i == 0)
    def _():
        acc[...] = term

    @pl.when(i > 0)
    def _():
        acc[...] += term

    @pl.when(i == pl.num_programs(0) - 1)
    def _():
        total = jnp.sum(sums[...], 0)
        normed, unit_f, scale, _ = head(rows[...], total, gain[...], bias[...], batch)
        pull = acc[...]
        radial = jnp.sum(unit_f * pull, 1, keepdims=True)
        shifts = (pull - unit_f * radial) * scale
        bias_part = jnp.sum(shifts, 0, keepdims=True)
        gain_part = jnp.sum(shifts * normed, 0, keepdims=True)
        tail = pack_ends(bias_part, gain_part).astype(BF16)
        n = pull.shape[0] // parts
        for p in range(parts):
            packed[p, :n] = pull[p * n : (p + 1) * n].astype(BF16)
            packed[p, n:] = tail


def pack_ends(bias_part, gain_part):
    pieces = []
    for value in (bias_part, gain_part):
        for _ in range(3):
            piece = value.astype(BF16).astype(F32)
            value = value - piece
            pieces.append(piece)
    fill = jnp.zeros((PAD - 6, bias_part.shape[1]), F32)
    return jnp.concatenate(pieces + [fill], 0)


def unpack_ends(tail):
    return jnp.concatenate(
        [jnp.sum(tail[0:3], 0, keepdims=True), jnp.sum(tail[3:6], 0, keepdims=True)], 0
    )


def mid_kernel(lines, rows_dev, arrived, packed):
    total = jnp.sum(arrived[...].astype(F32), 0)
    ends = unpack_ends(total[lines * rows_dev :])
    tail = pack_ends(ends[0:1], ends[1:2])[: PAD - rows_dev]
    for p in range(lines):
        piece = total[p * rows_dev : (p + 1) * rows_dev]
        packed[p] = jnp.concatenate([piece, tail], 0).astype(BF16)


def raw_kernel(
    at, place, place_2, totals, unit, unit_2, w_own, after, mine, *sent
):
    i = pl.program_id(0)
    parts = pl.num_programs(0)
    block = w_own.shape[0]
    first = lax.rem(at[0] + i, parts) * block
    raw = None
    for units, places, row in ((unit, place, 0), (unit_2, place_2, 2)):
        cosine = lax.dot_general(
            w_own[...], units[...], (((1,), (1,)), ((), ())), preferred_element_type=F32
        )
        target = hits(places[...], block, units.shape[0], first)
        logits = LOGIT_SCALE * cosine - jnp.where(target, LOGIT_SCALE * MARGIN, 0.0)
        share = jnp.exp(logits) / totals[row : row + 1]
        grad = (share - target.astype(F32)).astype(BF16)
        term = jnp.dot(grad, units[...], preferred_element_type=F32)
        raw = term if raw is None else raw + term

    @pl.when(i == 0)
    def _():
        mine[...] = raw

    for by, out in enumerate(sent):

        @pl.when(i == by + 1)
        def _(out=out):
            out[...] = raw.astype(BF16)


def project_kernel(at, picked, mine, *rest):
    arrived, out = rest[:-1], rest[-1]
    raw = mine[...]
    for piece in arrived:
        raw = raw + piece[...].astype(F32)
    picks = picked[...].astype(F32)
    inv_norm = lax.rsqrt(jnp.sum(picks * picks, 1, keepdims=True) + EPSILON)
    w_unit = picks * inv_norm
    along = jnp.sum(w_unit * raw, 1, keepdims=True)
    out[...] = ((raw - w_unit * along) * inv_norm).astype(BF16)


def order_kernel(at, *refs):
    found, out = refs[:-1], refs[-1]
    parts = len(found)
    source = lax.rem(at[0] - pl.program_id(0) + parts, parts)
    for by, piece in enumerate(found):

        @pl.when(source == by)
        def _(piece=piece):
            out[...] = piece[...]


def fixed(*shape):
    return pl.BlockSpec(shape, lambda i, at: (0,) * len(shape))


def call_at(kernel, grid, ins, outs, shapes, flops, size, exps=0):
    return pl.pallas_call(
        kernel,
        grid_spec=pltpu.PrefetchScalarGridSpec(
            num_scalar_prefetch=1, grid=(grid,), in_specs=ins, out_specs=outs
        ),
        out_shape=shapes,
        compiler_params=pltpu.CompilerParams(vmem_limit_bytes=VMEM),
        cost_estimate=pl.CostEstimate(
            flops=flops, bytes_accessed=size, transcendentals=exps
        ),
    )


def body(embeddings, bn_gain, bn_bias, centres, sample_rows, label_shard, label_slot):
    nx, nz, nc, nr = (lax.axis_size(a) for a in ("x", "z", "core", "rep"))
    ix, iz, ic, ir = (lax.axis_index(a) for a in ("x", "z", "core", "rep"))
    rows_dev, width = embeddings.shape
    slots = sample_rows.shape[1]
    batch = rows_dev * nx * nz * nc * nr
    line_rows = nz * rows_dev
    group = nx * line_rows
    held = nc * slots
    quarter = slots // nr
    at = ir.astype(jnp.int32).reshape(1)
    gain, bias = bn_gain[None], bn_bias[None]

    line = spread(embeddings, "z").reshape(line_rows, width)
    rows = spread(line, "x").reshape(group, width)
    rows_f = rows.astype(F32)
    sums = spread(
        jnp.stack([jnp.sum(rows_f, 0), jnp.sum(rows_f * rows_f, 0)]), ("core", "rep")
    )
    peers = nc * nr

    picked = jnp.take(centres, sample_rows[0], axis=0)
    picks = picked.astype(F32)
    inv_norm = lax.rsqrt(jnp.sum(picks * picks, 1, keepdims=True) + EPSILON)
    w_own = (picks * inv_norm).astype(BF16)
    w_other = shift(w_own, "core", 1)

    def of_core(labels, core):
        lines = labels.reshape(nx * nz, nc, rows_dev)
        return lax.dynamic_index_in_dim(lines, core, 1).reshape(1, group)

    owner, slot = of_core(label_shard, ic), of_core(label_slot, ic)
    chip = (ix * nz + iz) * nc
    place = jnp.where(
        owner == chip + ic, slot, jnp.where(owner == chip + 1 - ic, slot + slots, -1)
    )
    place_2 = jnp.where(
        of_core(label_shard, 1 - ic) == chip + ic, of_core(label_slot, 1 - ic), -1
    )

    block = slots // 2
    near = pl.BlockSpec((block, width), lambda i: (jnp.minimum(i, 1), 0))
    far = pl.BlockSpec((block, width), lambda i: (jnp.maximum(i - 2, 0), 0))
    unit, expo, stats = call(
        lambda *refs: exp_kernel(batch, *refs),
        4,
        [
            whole(group, width),
            whole(peers, 2, width),
            whole(1, width),
            whole(1, width),
            whole(1, group),
            near,
            far,
        ],
        [whole(group, width), rows_of(block, group), whole(nx * nc, 2, group)],
        [
            jax.ShapeDtypeStruct((group, width), BF16),
            jax.ShapeDtypeStruct((held, group), F32),
            jax.ShapeDtypeStruct((nx * nc, 2, group), F32),
        ],
        [pltpu.VMEM((2, group), F32)],
        2 * held * group * width,
        4 * held * group + 2 * held * width,
        held * group,
    )(rows, sums, gain, bias, place, w_own, w_other)
    unit_2 = shift(unit, "core", 1)

    stats = lax.all_to_all(stats, ("x", "core"), 0, 0).reshape(nx, nc, 2, group)
    stats = jnp.sum(stats, 0)
    stats = jnp.where(ic == 0, stats, stats[::-1]).reshape(2 * nc, group)
    stats = jnp.sum(spread(stats, "z"), 0)

    pull = call(
        lambda *refs: pull_kernel(batch, nx, *refs),
        4,
        [
            whole(group, width),
            whole(peers, 2, width),
            whole(1, width),
            whole(1, width),
            whole(1, group),
            whole(2 * nc, group),
            near,
            far,
            rows_of(block, group),
        ],
        whole(nx, line_rows + PAD, width),
        jax.ShapeDtypeStruct((nx, line_rows + PAD, width), BF16),
        [pltpu.VMEM((group, width), F32)],
        2 * held * group * width,
        4 * held * group + 2 * held * width,
    )(rows, sums, gain, bias, place, stats, w_own, w_other, expo)

    piece = jax.ShapeDtypeStruct((quarter, width), BF16)
    mine, *sent = call_at(
        raw_kernel,
        nr,
        [
            fixed(1, group),
            fixed(1, group),
            fixed(2 * nc, group),
            fixed(group, width),
            fixed(group, width),
            pl.BlockSpec((quarter, width), lambda i, at: (lax.rem(at[0] + i, nr), 0)),
            pl.BlockSpec(memory_space=pl.ANY),
        ],
        [fixed(quarter, width)] * nr,
        [jax.ShapeDtypeStruct((quarter, width), F32)] + [piece] * (nr - 1),
        4 * held * group * width,
        2 * held * width,
        held * group,
    )(at, place, place_2, stats, unit, unit_2, w_own, pull)
    came = [shift(sent[by - 1], "rep", by) for by in range(1, nr)]
    grad = call_at(
        project_kernel,
        1,
        [pl.BlockSpec((quarter, width), lambda i, at: (at[0], 0))]
        + [fixed(quarter, width)] * nr,
        fixed(quarter, width),
        piece,
        20 * quarter * width,
        14 * quarter * width,
    )(at, picked, mine, *came)
    found = [grad] + [shift(grad, "rep", by) for by in range(1, nr)]
    centre_grad = call_at(
        order_kernel,
        nr,
        [fixed(quarter, width)] * nr,
        pl.BlockSpec((quarter, width), lambda i, at: (i, 0)),
        jax.ShapeDtypeStruct((slots, width), BF16),
        slots * width,
        4 * slots * width,
    )(at, *found)

    pull = lax.all_to_all(pull, "x", 0, 0)
    pull = call(
        lambda *refs: mid_kernel(nz, rows_dev, *refs),
        1,
        [whole(nx, line_rows + PAD, width)],
        whole(nz, PAD, width),
        jax.ShapeDtypeStruct((nz, PAD, width), BF16),
        [],
        nx * line_rows * width,
        2 * nx * line_rows * width,
    )(pull)
    pull = jnp.sum(lax.all_to_all(pull, "z", 0, 0).astype(F32), 0)
    grad_unit = pull[:rows_dev]
    ends = jnp.sum(spread(unpack_ends(pull[rows_dev:]), ("core", "rep")), 0)

    own_stats = lax.dynamic_slice_in_dim(
        stats, (ix * nz + iz) * rows_dev, rows_dev, 1
    )
    row_loss = jnp.log(own_stats[0]) - own_stats[1]
    normed, unit_f, row_scale, inv_std = head(
        embeddings, jnp.sum(sums, 0), gain, bias, batch
    )
    radial = jnp.sum(unit_f * grad_unit, 1, keepdims=True)
    grad_shift = (grad_unit - unit_f * radial) * row_scale
    bias_grad, gain_grad = ends[0], ends[1]
    emb_grad = inv_std * (
        grad_shift * bn_gain
        - bn_gain * bias_grad / batch
        - normed * (bn_gain * gain_grad / batch)
    )
    return (row_loss, emb_grad, centre_grad, gain_grad, bias_grad)


def solution(mesh):
    shards, replicas = mesh.devices.shape
    split = (4, shards // 8, 2, replicas)
    fine = Mesh(mesh.devices.reshape(split), ("x", "z", "core", "rep"))
    cen = ("x", "z", "core")
    every = cen + ("rep",)
    return jax.shard_map(
        body,
        mesh=fine,
        in_specs=(
            P(every, None),
            P(),
            P(),
            P(cen, None),
            P(cen, None),
            P(None, "rep", None),
            P(None, "rep", None),
        ),
        out_specs=(P(every), P(every, None), P(cen, None), P(), P()),
        check_vma=False,
    )
```

```python
import jax
import jax.numpy as jnp
from jax import lax
from jax.experimental import pallas as pl
from jax.experimental.pallas import tpu as pltpu
from jax.sharding import Mesh, PartitionSpec as P

LOGIT_SCALE = 64.0
MARGIN = 0.4
EPSILON = 1e-05
F32 = jnp.float32
BF16 = jnp.bfloat16
VMEM = 20 * 1024 * 1024
PAD = 16


def spread(block, axes):
    copies = jnp.broadcast_to(block[None], (lax.axis_size(axes),) + block.shape)
    return lax.all_to_all(copies, axes, 0, 0)


def shift(block, axis, by):
    n = lax.axis_size(axis)
    return lax.ppermute(block, axis, [(i, (i + by) % n) for i in range(n)])


def head(inputs, sums, gain, bias, batch_total):
    mean = sums[0:1] / batch_total
    inv_std = lax.rsqrt(sums[1:2] / batch_total - mean * mean + EPSILON)
    normed = (inputs.astype(F32) - mean) * inv_std
    shifted = normed * gain + bias
    scale = lax.rsqrt(jnp.sum(shifted * shifted, 1, keepdims=True) + EPSILON)
    return normed, shifted * scale, scale, inv_std


def call(kernel, shapes, flops, size, exps=0, scalars=0, skipped=0):
    vmem = pl.BlockSpec(memory_space=pltpu.VMEM)
    smem = pl.BlockSpec(memory_space=pltpu.SMEM)
    left = pl.BlockSpec(memory_space=pl.ANY)

    def run(*args):
        inner = len(args) - scalars - skipped
        return pl.pallas_call(
            kernel,
            in_specs=[smem] * scalars + [vmem] * inner + [left] * skipped,
            out_specs=jax.tree.map(lambda _: vmem, shapes),
            out_shape=shapes,
            compiler_params=pltpu.CompilerParams(vmem_limit_bytes=VMEM),
            cost_estimate=pl.CostEstimate(
                flops=flops, bytes_accessed=size, transcendentals=exps
            ),
        )(*args)

    return run


def hits(place, block, count, first):
    return place == lax.broadcasted_iota(jnp.int32, (block, count), 0) + first


def logits_of(w_hat, unit, place, first):
    cosine = lax.dot_general(
        w_hat, unit, (((1,), (1,)), ((), ())), preferred_element_type=F32
    )
    target = hits(place, w_hat.shape[0], unit.shape[0], first)
    return LOGIT_SCALE * cosine - jnp.where(target, LOGIT_SCALE * MARGIN, 0.0), target


def grad_of(w_hat, unit, place, first, total):
    logits, target = logits_of(w_hat, unit, place, first)
    return (jnp.exp(logits) / total - target.astype(F32)).astype(BF16)


def blocks_of(w_own, w_other):
    block = w_own.shape[0] // 2
    for i in range(4):
        source = w_own if i < 2 else w_other
        yield source[(i % 2) * block : (i % 2 + 1) * block], i * block


def exp_kernel(batch, rows, sums, gain, bias, place, w_own, w_other, unit, stats):
    total = jnp.sum(sums[...], 0)
    units = head(rows[...], total, gain[...], bias[...], batch)[1].astype(BF16)
    unit[...] = units
    exps = hit = None
    for w_hat, first in blocks_of(w_own, w_other):
        logits, target = logits_of(w_hat, units, place[...], first)
        term = jnp.sum(jnp.exp(logits), 0, keepdims=True)
        other = jnp.sum(jnp.where(target, logits, 0.0), 0, keepdims=True)
        exps = term if exps is None else exps + term
        hit = other if hit is None else hit + other
    both = jnp.concatenate([exps, hit], 0)
    for p in range(stats.shape[0]):
        stats[p] = both


def pull_kernel(
    batch, rows, sums, gain, bias, place, totals, unit, w_own, w_other, packed
):
    units = unit[...]
    pull = None
    for w_hat, first in blocks_of(w_own, w_other):
        grad = grad_of(w_hat, units, place[...], first, totals[0:1])
        term = lax.dot_general(
            grad, w_hat, (((0,), (0,)), ((), ())), preferred_element_type=F32
        )
        pull = term if pull is None else pull + term
    total = jnp.sum(sums[...], 0)
    normed, unit_f, scale, _ = head(rows[...], total, gain[...], bias[...], batch)
    radial = jnp.sum(unit_f * pull, 1, keepdims=True)
    shifts = (pull - unit_f * radial) * scale
    bias_part = jnp.sum(shifts, 0, keepdims=True)
    gain_part = jnp.sum(shifts * normed, 0, keepdims=True)
    tail = pack_ends(bias_part, gain_part).astype(BF16)
    parts = packed.shape[0]
    n = pull.shape[0] // parts
    for p in range(parts):
        packed[p, :n] = pull[p * n : (p + 1) * n].astype(BF16)
        packed[p, n:] = tail


def pack_ends(bias_part, gain_part):
    pieces = []
    for value in (bias_part, gain_part):
        for _ in range(3):
            piece = value.astype(BF16).astype(F32)
            value = value - piece
            pieces.append(piece)
    fill = jnp.zeros((PAD - 6, bias_part.shape[1]), F32)
    return jnp.concatenate(pieces + [fill], 0)


def unpack_ends(tail):
    return jnp.concatenate(
        [jnp.sum(tail[0:3], 0, keepdims=True), jnp.sum(tail[3:6], 0, keepdims=True)], 0
    )


def mid_kernel(rows_dev, arrived, packed):
    lines = packed.shape[0]
    total = jnp.sum(arrived[...].astype(F32), 0)
    ends = unpack_ends(total[lines * rows_dev :])
    tail = pack_ends(ends[0:1], ends[1:2])[: PAD - rows_dev]
    for p in range(lines):
        piece = total[p * rows_dev : (p + 1) * rows_dev]
        packed[p] = jnp.concatenate([piece, tail], 0).astype(BF16)


def raw_kernel(
    at, place, place_2, totals, unit, unit_2, w_own, _, mine, *sent
):
    parts = len(sent) + 1
    block = mine.shape[0]
    for i in range(parts):
        first = pl.multiple_of(lax.rem(at[0] + i, parts) * block, 64)
        w_hat = w_own[pl.ds(first, block)]
        raw = None
        for units, places, row in ((unit, place, 0), (unit_2, place_2, 2)):
            grad = grad_of(
                w_hat, units[...], places[...], first, totals[row : row + 1]
            )
            term = jnp.dot(grad, units[...], preferred_element_type=F32)
            raw = term if raw is None else raw + term
        if i == 0:
            mine[...] = raw
        else:
            sent[i - 1][...] = raw.astype(BF16)


def project_kernel(at, picked, mine, *rest):
    arrived, out = rest[:-1], rest[-1]
    block = mine.shape[0]
    raw = mine[...]
    for piece in arrived:
        raw = raw + piece[...].astype(F32)
    picks = picked[pl.ds(pl.multiple_of(at[0] * block, 64), block)].astype(F32)
    inv_norm = lax.rsqrt(jnp.sum(picks * picks, 1, keepdims=True) + EPSILON)
    w_unit = picks * inv_norm
    along = jnp.sum(w_unit * raw, 1, keepdims=True)
    out[...] = ((raw - w_unit * along) * inv_norm).astype(BF16)


def order_kernel(at, *refs):
    found, out = refs[:-1], refs[-1]
    parts = len(found)
    block = found[0].shape[0]
    for by, piece in enumerate(found):
        where = lax.rem(at[0] - by + parts, parts) * block
        out[pl.ds(pl.multiple_of(where, 64), block)] = piece[...]


def body(embeddings, bn_gain, bn_bias, centres, sample_rows, label_shard, label_slot):
    nx, nz, nc, nr = (lax.axis_size(a) for a in ("x", "z", "core", "rep"))
    ix, iz, ic, ir = (lax.axis_index(a) for a in ("x", "z", "core", "rep"))
    rows_dev, width = embeddings.shape
    slots = sample_rows.shape[1]
    batch = rows_dev * nx * nz * nc * nr
    line_rows = nz * rows_dev
    group = nx * line_rows
    held = nc * slots
    quarter = slots // nr
    at = ir.astype(jnp.int32).reshape(1)
    gain, bias = bn_gain[None], bn_bias[None]

    line = spread(embeddings, "z").reshape(line_rows, width)
    rows = spread(line, "x").reshape(group, width)
    rows_f = rows.astype(F32)
    sums = spread(
        jnp.stack([jnp.sum(rows_f, 0), jnp.sum(rows_f * rows_f, 0)]), ("core", "rep")
    )

    picked = jnp.take(centres, sample_rows[0], axis=0)
    picks = picked.astype(F32)
    inv_norm = lax.rsqrt(jnp.sum(picks * picks, 1, keepdims=True) + EPSILON)
    w_own = (picks * inv_norm).astype(BF16)
    w_other = shift(w_own, "core", 1)

    def of_core(labels, core):
        lines = labels.reshape(nx * nz, nc, rows_dev)
        return lax.dynamic_index_in_dim(lines, core, 1).reshape(1, group)

    owner, slot = of_core(label_shard, ic), of_core(label_slot, ic)
    chip = (ix * nz + iz) * nc
    place = jnp.where(
        owner == chip + ic, slot, jnp.where(owner == chip + 1 - ic, slot + slots, -1)
    )
    place_2 = jnp.where(
        of_core(label_shard, 1 - ic) == chip + ic, of_core(label_slot, 1 - ic), -1
    )

    unit, stats = call(
        lambda *refs: exp_kernel(batch, *refs),
        [
            jax.ShapeDtypeStruct((group, width), BF16),
            jax.ShapeDtypeStruct((nx * nc, 2, group), F32),
        ],
        2 * held * group * width,
        2 * held * width,
        held * group,
    )(rows, sums, gain, bias, place, w_own, w_other)
    unit_2 = shift(unit, "core", 1)

    stats = lax.all_to_all(stats, ("x", "core"), 0, 0).reshape(nx, nc, 2, group)
    stats = jnp.sum(stats, 0)
    stats = jnp.where(ic == 0, stats, stats[::-1]).reshape(2 * nc, group)
    stats, unit_2 = lax.optimization_barrier((stats, unit_2))
    stats = jnp.sum(spread(stats, "z"), 0)

    pull = call(
        lambda *refs: pull_kernel(batch, *refs),
        jax.ShapeDtypeStruct((nx, line_rows + PAD, width), BF16),
        4 * held * group * width,
        2 * held * width,
        held * group,
    )(rows, sums, gain, bias, place, stats, unit, w_own, w_other)

    piece = jax.ShapeDtypeStruct((quarter, width), BF16)
    mine, *sent = call(
        raw_kernel,
        [jax.ShapeDtypeStruct((quarter, width), F32)] + [piece] * (nr - 1),
        4 * held * group * width,
        2 * held * width,
        held * group,
        scalars=1,
        skipped=1,
    )(at, place, place_2, stats, unit, unit_2, w_own, pull)
    came = [shift(sent[by - 1], "rep", by) for by in range(1, nr)]
    grad = call(
        project_kernel, piece, 20 * quarter * width, 14 * quarter * width, scalars=1
    )(at, picked, mine, *came)
    found = [grad] + [shift(grad, "rep", by) for by in range(1, nr)]
    centre_grad = call(
        order_kernel,
        jax.ShapeDtypeStruct((slots, width), BF16),
        slots * width,
        4 * slots * width,
        scalars=1,
    )(at, *found)

    pull = lax.all_to_all(pull, "x", 0, 0)
    pull, mine = lax.optimization_barrier((pull, mine))
    pull = call(
        lambda *refs: mid_kernel(rows_dev, *refs),
        jax.ShapeDtypeStruct((nz, PAD, width), BF16),
        nx * line_rows * width,
        2 * nx * line_rows * width,
    )(pull)
    pull = jnp.sum(lax.all_to_all(pull, "z", 0, 0).astype(F32), 0)
    grad_unit = pull[:rows_dev]
    ends = jnp.sum(spread(unpack_ends(pull[rows_dev:]), ("core", "rep")), 0)

    own_stats = lax.dynamic_slice_in_dim(
        stats, (ix * nz + iz) * rows_dev, rows_dev, 1
    )
    row_loss = jnp.log(own_stats[0]) - own_stats[1]
    normed, unit_f, row_scale, inv_std = head(
        embeddings, jnp.sum(sums, 0), gain, bias, batch
    )
    radial = jnp.sum(unit_f * grad_unit, 1, keepdims=True)
    grad_shift = (grad_unit - unit_f * radial) * row_scale
    bias_grad, gain_grad = ends[0], ends[1]
    emb_grad = inv_std * (
        grad_shift * bn_gain
        - bn_gain * bias_grad / batch
        - normed * (bn_gain * gain_grad / batch)
    )
    return (row_loss, emb_grad, centre_grad, gain_grad, bias_grad)


def solution(mesh):
    shards, replicas = mesh.devices.shape
    split = (4, shards // 8, 2, replicas)
    fine = Mesh(mesh.devices.reshape(split), ("x", "z", "core", "rep"))
    cen = ("x", "z", "core")
    every = cen + ("rep",)
    return jax.shard_map(
        body,
        mesh=fine,
        in_specs=(
            P(every, None),
            P(),
            P(),
            P(cen, None),
            P(cen, None),
            P(None, "rep", None),
            P(None, "rep", None),
        ),
        out_specs=(P(every), P(every, None), P(cen, None), P(), P()),
        check_vma=False,
    )
```

```python
import jax
import jax.numpy as jnp
from jax import lax
from jax.experimental import pallas as pl
from jax.experimental.pallas import tpu as pltpu
from jax.sharding import Mesh, PartitionSpec as P

LOGIT_SCALE = 64.0
MARGIN = 0.4
EPSILON = 1e-05
F32 = jnp.float32
BF16 = jnp.bfloat16
VMEM = 20 * 1024 * 1024
PAD = 16


def spread(block, axes):
    copies = jnp.broadcast_to(block[None], (lax.axis_size(axes),) + block.shape)
    return lax.all_to_all(copies, axes, 0, 0)


def shift(block, axis, by):
    n = lax.axis_size(axis)
    return lax.ppermute(block, axis, [(i, (i + by) % n) for i in range(n)])


def head(inputs, sums, gain, bias, batch_total):
    mean = sums[0:1] / batch_total
    inv_std = lax.rsqrt(sums[1:2] / batch_total - mean * mean + EPSILON)
    normed = (inputs.astype(F32) - mean) * inv_std
    shifted = normed * gain + bias
    scale = lax.rsqrt(jnp.sum(shifted * shifted, 1, keepdims=True) + EPSILON)
    return normed, shifted * scale, scale, inv_std


VM = pl.BlockSpec(memory_space=pltpu.VMEM)
SM = pl.BlockSpec(memory_space=pltpu.SMEM)
HB = pl.BlockSpec(memory_space=pl.ANY)


def call(kernel, ins, outs, shapes, flops, size, exps=0, scratch=()):
    return pl.pallas_call(
        kernel,
        in_specs=ins,
        out_specs=outs,
        out_shape=shapes,
        scratch_shapes=list(scratch),
        compiler_params=pltpu.CompilerParams(vmem_limit_bytes=VMEM),
        cost_estimate=pl.CostEstimate(
            flops=flops, bytes_accessed=size, transcendentals=exps
        ),
    )


def hits(place, block, count, first):
    return place == lax.broadcasted_iota(jnp.int32, (block, count), 0) + first


def logits_of(w_hat, unit, place, first):
    cosine = lax.dot_general(
        w_hat, unit, (((1,), (1,)), ((), ())), preferred_element_type=F32
    )
    target = hits(place, w_hat.shape[0], unit.shape[0], first)
    return LOGIT_SCALE * cosine - jnp.where(target, LOGIT_SCALE * MARGIN, 0.0), target


def grad_of(w_hat, unit, place, first, total):
    logits, target = logits_of(w_hat, unit, place, first)
    return (jnp.exp(logits) / total - target.astype(F32)).astype(BF16)


def blocks_of(w_own, w_other):
    block = w_own.shape[0] // 2
    for i in range(4):
        source = w_own if i < 2 else w_other
        yield source[(i % 2) * block : (i % 2 + 1) * block], i * block


def place_of(at, by, parts, block):
    return pl.multiple_of(lax.rem(at[0] - by + parts, parts) * block, block)


def exp_kernel(
    batch, lines, at, sums, gain, bias, place, w_own, w_other, *refs
):
    found, (unit, stats) = refs[:lines], refs[lines:]
    n = found[0].shape[0]
    total = jnp.sum(sums[...], 0)
    for by, piece in enumerate(found):
        part = head(piece[...], total, gain[...], bias[...], batch)[1].astype(BF16)
        unit[pl.ds(place_of(at, by, lines, n), n)] = part
    units = unit[...]
    exps = hit = None
    for w_hat, first in blocks_of(w_own, w_other):
        logits, target = logits_of(w_hat, units, place[...], first)
        term = jnp.sum(jnp.exp(logits), 0, keepdims=True)
        other = jnp.sum(jnp.where(target, logits, 0.0), 0, keepdims=True)
        exps = term if exps is None else exps + term
        hit = other if hit is None else hit + other
    both = jnp.concatenate([exps, hit], 0)
    for p in range(stats.shape[0]):
        stats[p] = both


def pull_kernel(
    batch, lines, at, sums, gain, bias, place, totals, unit, w_own, w_other, *refs
):
    found, (packed, acc) = refs[:lines], refs[lines:]
    n = found[0].shape[0]
    units = unit[...]
    pull = None
    for w_hat, first in blocks_of(w_own, w_other):
        grad = grad_of(w_hat, units, place[...], first, totals[0:1])
        term = lax.dot_general(
            grad, w_hat, (((0,), (0,)), ((), ())), preferred_element_type=F32
        )
        pull = term if pull is None else pull + term
    acc[...] = pull
    total = jnp.sum(sums[...], 0)
    bias_part = gain_part = 0.0
    for by, piece in enumerate(found):
        where = place_of(at, by, lines, n)
        part = acc[pl.ds(where, n)]
        normed, unit_f, scale, _ = head(piece[...], total, gain[...], bias[...], batch)
        radial = jnp.sum(unit_f * part, 1, keepdims=True)
        shifts = (part - unit_f * radial) * scale
        bias_part = bias_part + jnp.sum(shifts, 0, keepdims=True)
        gain_part = gain_part + jnp.sum(shifts * normed, 0, keepdims=True)
    tail = pack_ends(bias_part, gain_part).astype(BF16)
    for p in range(lines):
        packed[p, :n] = acc[p * n : (p + 1) * n].astype(BF16)
        packed[p, n:] = tail


def pack_ends(bias_part, gain_part):
    pieces = []
    for value in (bias_part, gain_part):
        for _ in range(3):
            piece = value.astype(BF16).astype(F32)
            value = value - piece
            pieces.append(piece)
    fill = jnp.zeros((PAD - 6, bias_part.shape[1]), F32)
    return jnp.concatenate(pieces + [fill], 0)


def unpack_ends(tail):
    return jnp.concatenate(
        [jnp.sum(tail[0:3], 0, keepdims=True), jnp.sum(tail[3:6], 0, keepdims=True)], 0
    )


def mid_kernel(rows_dev, arrived, packed):
    lines = packed.shape[0]
    total = jnp.sum(arrived[...].astype(F32), 0)
    ends = unpack_ends(total[lines * rows_dev :])
    tail = pack_ends(ends[0:1], ends[1:2])[: PAD - rows_dev]
    for p in range(lines):
        piece = total[p * rows_dev : (p + 1) * rows_dev]
        packed[p] = jnp.concatenate([piece, tail], 0).astype(BF16)


def raw_kernel(parts, at, place, place_2, totals, unit, unit_2, w_own, _, *refs):
    outs, (mine, sent, sems) = refs[:parts], refs[parts:]
    block = mine.shape[0]
    copies = []
    for i in range(parts):
        first = pl.multiple_of(lax.rem(at[0] + i, parts) * block, 64)
        w_hat = w_own[pl.ds(first, block)]
        raw = None
        for units, places, row in ((unit, place, 0), (unit_2, place_2, 2)):
            grad = grad_of(
                w_hat, units[...], places[...], first, totals[row : row + 1]
            )
            term = jnp.dot(grad, units[...], preferred_element_type=F32)
            raw = term if raw is None else raw + term
        if i == 0:
            mine[...] = raw
            source = mine
        else:
            sent[i - 1] = raw.astype(BF16)
            source = sent.at[i - 1]
        copies.append(pltpu.make_async_copy(source, outs[i], sems.at[i]))
        copies[-1].start()
    for copy in copies:
        copy.wait()


def project_kernel(parts, at, picked, *refs):
    found, (out, picks_ref, sem) = refs[:parts], refs[parts:]
    block = out.shape[0]
    rows = pl.ds(pl.multiple_of(at[0] * block, 64), block)
    copy = pltpu.make_async_copy(picked.at[rows], picks_ref, sem)
    copy.start()
    raw = found[0][...]
    for piece in found[1:]:
        raw = raw + piece[...].astype(F32)
    copy.wait()
    picks = picks_ref[...].astype(F32)
    inv_norm = lax.rsqrt(jnp.sum(picks * picks, 1, keepdims=True) + EPSILON)
    w_unit = picks * inv_norm
    along = jnp.sum(w_unit * raw, 1, keepdims=True)
    out[...] = ((raw - w_unit * along) * inv_norm).astype(BF16)


def order_kernel(parts, at, *refs):
    found, (out, sems) = refs[:parts], refs[parts:]
    block = found[0].shape[0]
    copies = []
    for by, piece in enumerate(found):
        where = pl.multiple_of(lax.rem(at[0] - by + parts, parts) * block, 64)
        copies.append(
            pltpu.make_async_copy(piece, out.at[pl.ds(where, block)], sems.at[by])
        )
        copies[-1].start()
    for copy in copies:
        copy.wait()


def body(embeddings, bn_gain, bn_bias, centres, sample_rows, label_shard, label_slot):
    nx, nz, nc, nr = (lax.axis_size(a) for a in ("x", "z", "core", "rep"))
    ix, iz, ic, ir = (lax.axis_index(a) for a in ("x", "z", "core", "rep"))
    rows_dev, width = embeddings.shape
    slots = sample_rows.shape[1]
    batch = rows_dev * nx * nz * nc * nr
    line_rows = nz * rows_dev
    group = nx * line_rows
    held = nc * slots
    quarter = slots // nr
    at = ir.astype(jnp.int32).reshape(1)
    at_x = ix.astype(jnp.int32).reshape(1)
    gain, bias = bn_gain[None], bn_bias[None]

    line = spread(embeddings, "z").reshape(line_rows, width)
    line_f = line.astype(F32)
    sums = spread(
        jnp.stack([jnp.sum(line_f, 0), jnp.sum(line_f * line_f, 0)]),
        ("x", "core", "rep"),
    )
    lines = [line] + [shift(line, "x", by) for by in range(1, nx)]

    picked = jnp.take(centres, sample_rows[0], axis=0)
    picks = picked.astype(F32)
    inv_norm = lax.rsqrt(jnp.sum(picks * picks, 1, keepdims=True) + EPSILON)
    w_own = (picks * inv_norm).astype(BF16)
    w_other = shift(w_own, "core", 1)

    def of_core(labels, core):
        lines = labels.reshape(nx * nz, nc, rows_dev)
        return lax.dynamic_index_in_dim(lines, core, 1).reshape(1, group)

    owner, slot = of_core(label_shard, ic), of_core(label_slot, ic)
    chip = (ix * nz + iz) * nc
    place = jnp.where(
        owner == chip + ic, slot, jnp.where(owner == chip + 1 - ic, slot + slots, -1)
    )
    place_2 = jnp.where(
        of_core(label_shard, 1 - ic) == chip + ic, of_core(label_slot, 1 - ic), -1
    )

    unit, stats = call(
        lambda *refs: exp_kernel(batch, nx, *refs),
        [SM] + [VM] * (6 + nx),
        [VM] * 2,
        [
            jax.ShapeDtypeStruct((group, width), BF16),
            jax.ShapeDtypeStruct((nx * nc, 2, group), F32),
        ],
        2 * held * group * width,
        2 * held * width,
        held * group,
    )(at_x, sums, gain, bias, place, w_own, w_other, *lines)
    unit_2 = shift(unit, "core", 1)

    stats = lax.all_to_all(stats, ("x", "core"), 0, 0).reshape(nx, nc, 2, group)
    stats = jnp.sum(stats, 0)
    stats = jnp.where(ic == 0, stats, stats[::-1]).reshape(2 * nc, group)
    stats, unit_2 = lax.optimization_barrier((stats, unit_2))
    stats = jnp.sum(spread(stats, "z"), 0)

    pull = call(
        lambda *refs: pull_kernel(batch, nx, *refs),
        [SM] + [VM] * (8 + nx),
        VM,
        jax.ShapeDtypeStruct((nx, line_rows + PAD, width), BF16),
        4 * held * group * width,
        2 * held * width,
        held * group,
        [pltpu.VMEM((group, width), F32)],
    )(at_x, sums, gain, bias, place, stats, unit, w_own, w_other, *lines)

    piece = jax.ShapeDtypeStruct((quarter, width), BF16)
    mine, *sent = call(
        lambda *refs: raw_kernel(nr, *refs),
        [SM] + [VM] * 6 + [HB],
        [HB] * nr,
        [jax.ShapeDtypeStruct((quarter, width), F32)] + [piece] * (nr - 1),
        4 * held * group * width,
        2 * held * width,
        held * group,
        [
            pltpu.VMEM((quarter, width), F32),
            pltpu.VMEM((nr - 1, quarter, width), BF16),
            pltpu.SemaphoreType.DMA((nr,)),
        ],
    )(at, place, place_2, stats, unit, unit_2, w_own, pull)
    came = [shift(sent[by - 1], "rep", by) for by in range(1, nr)]
    grad = call(
        lambda *refs: project_kernel(nr, *refs),
        [SM, HB] + [VM] * nr,
        VM,
        piece,
        20 * quarter * width,
        14 * quarter * width,
        0,
        [pltpu.VMEM((quarter, width), BF16), pltpu.SemaphoreType.DMA],
    )(at, picked, mine, *came)

    pull = lax.all_to_all(pull, "x", 0, 0)
    pull, mine = lax.optimization_barrier((pull, mine))
    pull = call(
        lambda *refs: mid_kernel(rows_dev, *refs),
        [VM],
        VM,
        jax.ShapeDtypeStruct((nz, PAD, width), BF16),
        nx * line_rows * width,
        2 * nx * line_rows * width,
    )(pull)
    pull = jnp.sum(lax.all_to_all(pull, "z", 0, 0).astype(F32), 0)
    grad_unit = pull[:rows_dev]
    ends = unpack_ends(pull[rows_dev:])
    ends = jnp.broadcast_to(ends[None], (nc * nr,) + ends.shape)
    ends, grad = lax.optimization_barrier((ends, grad))
    ends = jnp.sum(lax.all_to_all(ends, ("core", "rep"), 0, 0), 0)
    found = [grad] + [shift(grad, "rep", by) for by in range(1, nr)]
    centre_grad = call(
        lambda *refs: order_kernel(nr, *refs),
        [SM] + [HB] * nr,
        HB,
        jax.ShapeDtypeStruct((slots, width), BF16),
        slots * width,
        4 * slots * width,
        0,
        [pltpu.SemaphoreType.DMA((nr,))],
    )(at, *found)

    own_stats = lax.dynamic_slice_in_dim(
        stats, (ix * nz + iz) * rows_dev, rows_dev, 1
    )
    row_loss = jnp.log(own_stats[0]) - own_stats[1]
    normed, unit_f, row_scale, inv_std = head(
        embeddings, jnp.sum(sums, 0), gain, bias, batch
    )
    radial = jnp.sum(unit_f * grad_unit, 1, keepdims=True)
    grad_shift = (grad_unit - unit_f * radial) * row_scale
    bias_grad, gain_grad = ends[0], ends[1]
    emb_grad = inv_std * (
        grad_shift * bn_gain
        - bn_gain * bias_grad / batch
        - normed * (bn_gain * gain_grad / batch)
    )
    return (row_loss, emb_grad, centre_grad, gain_grad, bias_grad)


def solution(mesh):
    shards, replicas = mesh.devices.shape
    split = (4, shards // 8, 2, replicas)
    fine = Mesh(mesh.devices.reshape(split), ("x", "z", "core", "rep"))
    cen = ("x", "z", "core")
    every = cen + ("rep",)
    return jax.shard_map(
        body,
        mesh=fine,
        in_specs=(
            P(every, None),
            P(),
            P(),
            P(cen, None),
            P(cen, None),
            P(None, "rep", None),
            P(None, "rep", None),
        ),
        out_specs=(P(every), P(every, None), P(cen, None), P(), P()),
        check_vma=False,
    )
```

```python
import jax
import jax.numpy as jnp
from jax import lax
from jax.experimental import pallas as pl
from jax.experimental.pallas import tpu as pltpu
from jax.sharding import Mesh, PartitionSpec as P

LOGIT_SCALE = 64.0
MARGIN = 0.4
EPSILON = 1e-05
F32 = jnp.float32
BF16 = jnp.bfloat16
LARGE = 60 * 1024 * 1024
SMALL = 20 * 1024 * 1024
PAD = 16


def spread(block, axes):
    copies = jnp.broadcast_to(block[None], (lax.axis_size(axes),) + block.shape)
    return lax.all_to_all(copies, axes, 0, 0)


def shift(block, axis, by):
    n = lax.axis_size(axis)
    return lax.ppermute(block, axis, [(i, (i + by) % n) for i in range(n)])


def head(inputs, sums, gain, bias, batch_total):
    mean = sums[0:1] / batch_total
    inv_std = lax.rsqrt(sums[1:2] / batch_total - mean * mean + EPSILON)
    normed = (inputs.astype(F32) - mean) * inv_std
    shifted = normed * gain + bias
    scale = lax.rsqrt(jnp.sum(shifted * shifted, 1, keepdims=True) + EPSILON)
    return normed, shifted * scale, scale, inv_std


VM = pl.BlockSpec(memory_space=pltpu.VMEM)
SM = pl.BlockSpec(memory_space=pltpu.SMEM)
HB = pl.BlockSpec(memory_space=pl.ANY)
HO = pl.BlockSpec(memory_space=pltpu.HBM)


def call(kernel, ins, outs, shapes, flops, size, exps=0, scratch=(), grant=LARGE):
    return pl.pallas_call(
        kernel,
        in_specs=ins,
        out_specs=outs,
        out_shape=shapes,
        scratch_shapes=list(scratch),
        compiler_params=pltpu.CompilerParams(vmem_limit_bytes=grant),
        cost_estimate=pl.CostEstimate(
            flops=flops, bytes_accessed=size, transcendentals=exps
        ),
    )


def hits(place, block, count, first):
    return place == lax.broadcasted_iota(jnp.int32, (block, count), 0) + first


def logits_of(w_hat, unit, place, first):
    cosine = lax.dot_general(
        w_hat, unit, (((1,), (1,)), ((), ())), preferred_element_type=F32
    )
    target = hits(place, w_hat.shape[0], unit.shape[0], first)
    return LOGIT_SCALE * cosine - jnp.where(target, LOGIT_SCALE * MARGIN, 0.0), target


def grad_of(w_hat, unit, place, first, total):
    logits, target = logits_of(w_hat, unit, place, first)
    return (jnp.exp(logits) / total - target.astype(F32)).astype(BF16)


def blocks_of(w_own, w_other):
    block = w_own.shape[0] // 2
    for i in range(4):
        source = w_own if i < 2 else w_other
        yield source[(i % 2) * block : (i % 2 + 1) * block], i * block


def exp_kernel(batch, rows, sums, gain, bias, place, w_own, w_other, unit, stats):
    total = jnp.sum(sums[...], 0)
    units = head(rows[...], total, gain[...], bias[...], batch)[1].astype(BF16)
    unit[...] = units
    exps = hit = None
    for w_hat, first in blocks_of(w_own, w_other):
        logits, target = logits_of(w_hat, units, place[...], first)
        term = jnp.sum(jnp.exp(logits), 0, keepdims=True)
        other = jnp.sum(jnp.where(target, logits, 0.0), 0, keepdims=True)
        exps = term if exps is None else exps + term
        hit = other if hit is None else hit + other
    both = jnp.concatenate([exps, hit], 0)
    for p in range(stats.shape[0]):
        stats[p] = both


def pull_kernel(
    batch, rows, sums, gain, bias, place, totals, unit, w_own, w_other, packed
):
    units = unit[...]
    row_total = jnp.sum(totals[...], 0)[0:1, : units.shape[0]]
    pull = None
    for w_hat, first in blocks_of(w_own, w_other):
        grad = grad_of(w_hat, units, place[...], first, row_total)
        term = lax.dot_general(
            grad, w_hat, (((0,), (0,)), ((), ())), preferred_element_type=F32
        )
        pull = term if pull is None else pull + term
    total = jnp.sum(sums[...], 0)
    normed, unit_f, scale, _ = head(rows[...], total, gain[...], bias[...], batch)
    radial = jnp.sum(unit_f * pull, 1, keepdims=True)
    shifts = (pull - unit_f * radial) * scale
    bias_part = jnp.sum(shifts, 0, keepdims=True)
    gain_part = jnp.sum(shifts * normed, 0, keepdims=True)
    tail = tail_of(bias_part, gain_part)
    parts = packed.shape[0]
    n = pull.shape[0] // parts
    for p in range(parts):
        packed[p, :n] = pull[p * n : (p + 1) * n].astype(BF16)
        packed[p, n:] = tail


def tail_of(bias_part, gain_part):
    pieces = split(bias_part, 3) + split(gain_part, 3)
    fill = jnp.zeros((PAD - 6, bias_part.shape[1]), F32)
    return jnp.concatenate(pieces + [fill], 0).astype(BF16)


def sums_of(tail):
    return jnp.concatenate(
        [jnp.sum(tail[k : k + 3], 0, keepdims=True) for k in (0, 3)], 0
    )


def split(value, count):
    pieces = []
    for _ in range(count):
        piece = value.astype(BF16).astype(F32)
        value = value - piece
        pieces.append(piece)
    return pieces


def total_kernel(lines, at, arrived, out):
    group = arrived.shape[2]
    n = group // lines
    place = at[0] * n if n % 128 else pl.multiple_of(at[0] * n, 128)
    own = other = hit = 0.0
    for x in range(lines):
        own = own + arrived[2 * x + at[1], 0:1]
        other = other + arrived[2 * x + 1 - at[1], 0:1]
        hit = hit + arrived[2 * x + at[1], 1:2, pl.ds(place, n)]
    both = jnp.concatenate(
        [
            jnp.concatenate([own, hit], 1),
            jnp.concatenate([other, jnp.zeros_like(hit)], 1),
        ],
        0,
    )
    for p in range(out.shape[0]):
        out[p] = both


def mid_kernel(rows_dev, arrived, packed):
    lines, _, lane = packed.shape
    total = jnp.sum(arrived[...].astype(F32), 0)
    width = total.shape[1]
    cuts = [slice(k, k + lane) for k in range(0, width, lane)]
    ends = sums_of(total[lines * rows_dev :])
    rows = split(ends[0:1], 2) + split(ends[1:2], 2)
    tail = [row[:, cut] for row in rows for cut in cuts]
    for p in range(lines):
        piece = total[p * rows_dev : (p + 1) * rows_dev]
        packed[p] = jnp.concatenate([piece[:, c] for c in cuts] + tail, 0).astype(BF16)


def home_kernel(rows_dev, arrived, grad, ends):
    total = jnp.sum(arrived[...].astype(F32), 0)
    lane = total.shape[1]
    n = grad.shape[1] // lane
    grad[...] = jnp.concatenate(
        [total[k * rows_dev : (k + 1) * rows_dev] for k in range(n)], 1
    )
    tail = total[n * rows_dev :]
    rows = []
    for v in range(2):
        both = tail[2 * v * n : (2 * v + 1) * n] + tail[(2 * v + 1) * n : (2 * v + 2) * n]
        rows.append(jnp.concatenate([both[k : k + 1] for k in range(n)], 1))
    ends[...] = jnp.concatenate(rows, 0)


def raw_kernel(parts, at, place, place_2, totals, unit, unit_2, w_own, _, *refs):
    outs, (mine, sent, sems) = refs[:parts], refs[parts:]
    block = mine.shape[0]
    copies = []
    group = unit.shape[0]
    total = jnp.sum(totals[...], 0)
    for i in range(parts):
        first = pl.multiple_of(lax.rem(at[0] + i, parts) * block, 64)
        w_hat = w_own[pl.ds(first, block)]
        raw = None
        for units, places, row in ((unit, place, 0), (unit_2, place_2, 1)):
            grad = grad_of(
                w_hat, units[...], places[...], first, total[row : row + 1, :group]
            )
            term = jnp.dot(grad, units[...], preferred_element_type=F32)
            raw = term if raw is None else raw + term
        if i == 0:
            mine[...] = raw
            source = mine
        else:
            sent[i - 1] = raw.astype(BF16)
            source = sent.at[i - 1]
        copies.append(pltpu.make_async_copy(source, outs[i], sems.at[i]))
        copies[-1].start()
    for copy in copies:
        copy.wait()


def project_kernel(parts, at, picked, ends, ends_2, *refs):
    found, (packed, picks_ref, sem) = refs[:parts], refs[parts:]
    block = picks_ref.shape[0]
    rows = pl.ds(pl.multiple_of(at[0] * block, 64), block)
    copy = pltpu.make_async_copy(picked.at[rows], picks_ref, sem)
    copy.start()
    raw = found[0][...]
    for piece in found[1:]:
        raw = raw + piece[...].astype(F32)
    both = ends[...] + ends_2[...]
    tail = tail_of(both[0:1], both[1:2])
    copy.wait()
    picks = picks_ref[...].astype(F32)
    inv_norm = lax.rsqrt(jnp.sum(picks * picks, 1, keepdims=True) + EPSILON)
    w_unit = picks * inv_norm
    along = jnp.sum(w_unit * raw, 1, keepdims=True)
    grad = ((raw - w_unit * along) * inv_norm).astype(BF16)
    for p in range(parts):
        packed[p, :block] = grad
        packed[p, block:] = tail


def final_kernel(
    batch, at, arrived, inputs, sums, gain, bias, grad_unit, totals, loss, emb, grad, ends
):
    parts, tall, _ = arrived.shape
    block = tall - PAD
    tail = 0.0
    for p in range(parts):
        grad[p * block : (p + 1) * block] = arrived[p, :block]
        tail = tail + arrived[p, block:].astype(F32)
    both = sums_of(tail)
    ends[...] = both
    bias_grad, gain_grad = both[0:1], both[1:2]
    total = jnp.sum(sums[...], 0)
    normed, unit_f, scale, inv_std = head(
        inputs[...], total, gain[...], bias[...], batch
    )
    pull = grad_unit[...]
    radial = jnp.sum(unit_f * pull, 1, keepdims=True)
    shifts = (pull - unit_f * radial) * scale
    emb[...] = inv_std * (
        shifts * gain[...]
        - gain[...] * bias_grad / batch
        - normed * (gain[...] * gain_grad / batch)
    )
    own = jnp.sum(totals[...], 0)[0:1]
    n = inputs.shape[0]
    shape = (n, own.shape[1])
    ahead = lax.broadcasted_iota(jnp.int32, shape, 1) - lax.broadcasted_iota(
        jnp.int32, shape, 0
    )
    found = [
        jnp.sum(jnp.where(ahead == at[k], own, 0.0), 1, keepdims=True) for k in (0, 1)
    ]
    values = jnp.log(found[0]) - found[1]
    square = (n, n)
    same = lax.broadcasted_iota(jnp.int32, square, 0) == lax.broadcasted_iota(
        jnp.int32, square, 1
    )
    loss[...] = jnp.sum(jnp.where(same, values, 0.0), 0, keepdims=True)


def body(embeddings, bn_gain, bn_bias, centres, sample_rows, label_shard, label_slot):
    nx, nz, nc, nr = (lax.axis_size(a) for a in ("x", "z", "core", "rep"))
    ix, iz, ic, ir = (lax.axis_index(a) for a in ("x", "z", "core", "rep"))
    rows_dev, width = embeddings.shape
    slots = sample_rows.shape[1]
    batch = rows_dev * nx * nz * nc * nr
    line_rows = nz * rows_dev
    group = nx * line_rows
    held = nc * slots
    quarter = slots // nr
    at = ir.astype(jnp.int32).reshape(1)
    gain, bias = bn_gain[None], bn_bias[None]

    line = spread(embeddings, "z").reshape(line_rows, width)
    rows = spread(line, "x").reshape(group, width)
    rows_f = rows.astype(F32)
    sums = spread(
        jnp.stack([jnp.sum(rows_f, 0), jnp.sum(rows_f * rows_f, 0)]), ("core", "rep")
    )

    picked = centres.at[sample_rows[0]].get(mode="promise_in_bounds")
    picks = picked.astype(F32)
    inv_norm = lax.rsqrt(jnp.sum(picks * picks, 1, keepdims=True) + EPSILON)
    w_own = (picks * inv_norm).astype(BF16)
    w_other = shift(w_own, "core", 1)

    def of_core(labels, core):
        lines = labels.reshape(nx * nz, nc, rows_dev)
        return lax.dynamic_index_in_dim(lines, core, 1).reshape(1, group)

    owner, slot = of_core(label_shard, ic), of_core(label_slot, ic)
    chip = (ix * nz + iz) * nc
    place = jnp.where(
        owner == chip + ic, slot, jnp.where(owner == chip + 1 - ic, slot + slots, -1)
    )
    place_2 = jnp.where(
        of_core(label_shard, 1 - ic) == chip + ic, of_core(label_slot, 1 - ic), -1
    )

    unit, stats = call(
        lambda *refs: exp_kernel(batch, *refs),
        [VM] * 7,
        [VM] * 2,
        [
            jax.ShapeDtypeStruct((group, width), BF16),
            jax.ShapeDtypeStruct((nx * nc, 2, group), F32),
        ],
        2 * held * group * width,
        2 * held * width,
        held * group,
    )(rows, sums, gain, bias, place, w_own, w_other)
    unit_2 = shift(unit, "core", 1)

    stats = lax.all_to_all(stats, ("x", "core"), 0, 0)
    totals = call(
        lambda *refs: total_kernel(nx, *refs),
        [SM, VM],
        VM,
        jax.ShapeDtypeStruct((nz, nc, group + line_rows), F32),
        16 * group,
        64 * group,
        grant=SMALL,
    )(jnp.stack([ix, ic]).astype(jnp.int32), stats)
    totals, unit_2, place_2 = lax.optimization_barrier((totals, unit_2, place_2))
    totals = lax.all_to_all(totals, "z", 0, 0)

    pull = call(
        lambda *refs: pull_kernel(batch, *refs),
        [VM] * 9,
        VM,
        jax.ShapeDtypeStruct((nx, line_rows + PAD, width), BF16),
        4 * held * group * width,
        2 * held * width,
        held * group,
    )(rows, sums, gain, bias, place, totals, unit, w_own, w_other)

    piece = jax.ShapeDtypeStruct((quarter, width), BF16)
    mine, *sent = call(
        lambda *refs: raw_kernel(nr, *refs),
        [SM] + [VM] * 6 + [HB],
        [HO] * nr,
        [jax.ShapeDtypeStruct((quarter, width), F32)] + [piece] * (nr - 1),
        4 * held * group * width,
        2 * held * width,
        held * group,
        [
            pltpu.VMEM((quarter, width), F32),
            pltpu.VMEM((nr - 1, quarter, width), BF16),
            pltpu.SemaphoreType.DMA((nr,)),
        ],
    )(at, place, place_2, totals, unit, unit_2, w_own, pull)
    came = [shift(sent[by - 1], "rep", by) for by in range(1, nr)]
    pull = lax.all_to_all(pull, "x", 0, 0)
    pull, mine = lax.optimization_barrier((pull, mine))
    lanes = min(width, 128)
    tall = (rows_dev + 4) * (width // lanes)
    pull = call(
        lambda *refs: mid_kernel(rows_dev, *refs),
        [VM],
        VM,
        jax.ShapeDtypeStruct((nz, tall, lanes), BF16),
        nx * line_rows * width,
        2 * nx * line_rows * width,
        grant=SMALL,
    )(pull)
    pull = lax.all_to_all(pull, "z", 0, 0)
    grad_unit, ends = call(
        lambda *refs: home_kernel(rows_dev, *refs),
        [VM],
        [VM] * 2,
        [
            jax.ShapeDtypeStruct((rows_dev, width), F32),
            jax.ShapeDtypeStruct((2, width), F32),
        ],
        nz * tall * lanes,
        2 * nz * tall * lanes,
        grant=SMALL,
    )(pull)
    last = call(
        lambda *refs: project_kernel(nr, *refs),
        [SM, HB] + [VM] * (2 + nr),
        VM,
        jax.ShapeDtypeStruct((nr, quarter + PAD, width), BF16),
        20 * quarter * width,
        14 * quarter * width,
        0,
        [pltpu.VMEM((quarter, width), BF16), pltpu.SemaphoreType.DMA],
        grant=SMALL,
    )(at, picked, ends, shift(ends, "core", 1), mine, *came)
    last = lax.all_to_all(last, "rep", 0, 0)

    own = jnp.stack([(ix * nz + iz) * rows_dev, group + iz * rows_dev])
    row_loss, emb_grad, centre_grad, ends = call(
        lambda *refs: final_kernel(batch, *refs),
        [SM] + [VM] * 7,
        [VM] * 4,
        [
            jax.ShapeDtypeStruct((1, rows_dev), F32),
            jax.ShapeDtypeStruct((rows_dev, width), F32),
            jax.ShapeDtypeStruct((slots, width), BF16),
            jax.ShapeDtypeStruct((2, width), F32),
        ],
        slots * width,
        4 * slots * width,
        grant=SMALL,
    )(own.astype(jnp.int32), last, embeddings, sums, gain, bias, grad_unit, totals)
    return (row_loss[0], emb_grad, centre_grad, ends[1], ends[0])


def solution(mesh):
    shards, replicas = mesh.devices.shape
    split = (4, shards // 8, 2, replicas)
    fine = Mesh(mesh.devices.reshape(split), ("x", "z", "core", "rep"))
    cen = ("x", "z", "core")
    every = cen + ("rep",)
    return jax.shard_map(
        body,
        mesh=fine,
        in_specs=(
            P(every, None),
            P(),
            P(),
            P(cen, None),
            P(cen, None),
            P(None, "rep", None),
            P(None, "rep", None),
        ),
        out_specs=(P(every), P(every, None), P(cen, None), P(), P()),
        check_vma=False,
    )
```

```python
import jax
import jax.numpy as jnp
from jax import lax
from jax.experimental import pallas as pl
from jax.experimental.pallas import tpu as pltpu
from jax.sharding import Mesh, PartitionSpec as P

LOGIT_SCALE = 64.0
MARGIN = 0.4
EPSILON = 1e-05
F32 = jnp.float32
BF16 = jnp.bfloat16
LARGE = 60 * 1024 * 1024
SMALL = 20 * 1024 * 1024
PAD = 16


def spread(block, axes):
    copies = jnp.broadcast_to(block[None], (lax.axis_size(axes),) + block.shape)
    return lax.all_to_all(copies, axes, 0, 0)


def shift(block, axis, by):
    n = lax.axis_size(axis)
    return lax.ppermute(block, axis, [(i, (i + by) % n) for i in range(n)])


def head(inputs, sums, gain, bias, batch_total):
    mean = sums[0:1] / batch_total
    inv_std = lax.rsqrt(sums[1:2] / batch_total - mean * mean + EPSILON)
    normed = (inputs.astype(F32) - mean) * inv_std
    shifted = normed * gain + bias
    scale = lax.rsqrt(jnp.sum(shifted * shifted, 1, keepdims=True) + EPSILON)
    return normed, shifted * scale, scale, inv_std


VM = pl.BlockSpec(memory_space=pltpu.VMEM)
SM = pl.BlockSpec(memory_space=pltpu.SMEM)
HB = pl.BlockSpec(memory_space=pl.ANY)
HO = pl.BlockSpec(memory_space=pltpu.HBM)


def call(kernel, ins, outs, shapes, flops, size, exps=0, scratch=(), grant=LARGE):
    return pl.pallas_call(
        kernel,
        in_specs=ins,
        out_specs=outs,
        out_shape=shapes,
        scratch_shapes=list(scratch),
        compiler_params=pltpu.CompilerParams(vmem_limit_bytes=grant),
        cost_estimate=pl.CostEstimate(
            flops=flops, bytes_accessed=size, transcendentals=exps
        ),
    )


def hits(place, block, count, first):
    return place == lax.broadcasted_iota(jnp.int32, (block, count), 0) + first


def logits_of(w_hat, unit, place, first):
    cosine = lax.dot_general(
        w_hat, unit, (((1,), (1,)), ((), ())), preferred_element_type=F32
    )
    target = hits(place, w_hat.shape[0], unit.shape[0], first)
    return LOGIT_SCALE * cosine - jnp.where(target, LOGIT_SCALE * MARGIN, 0.0), target


def grad_of(w_hat, unit, place, first, total):
    logits, target = logits_of(w_hat, unit, place, first)
    return (jnp.exp(logits) / total - target.astype(F32)).astype(BF16)


def blocks_of(w_own, w_other):
    block = w_own.shape[0] // 2
    for i in range(4):
        source = w_own if i < 2 else w_other
        yield source[(i % 2) * block : (i % 2 + 1) * block], i * block


def exp_kernel(batch, rows, sums, gain, bias, place, w_own, w_other, unit, stats):
    total = jnp.sum(sums[...], 0)
    units = head(rows[...], total, gain[...], bias[...], batch)[1].astype(BF16)
    unit[...] = units
    exps = hit = None
    for w_hat, first in blocks_of(w_own, w_other):
        logits, target = logits_of(w_hat, units, place[...], first)
        term = jnp.sum(jnp.exp(logits), 0, keepdims=True)
        other = jnp.sum(jnp.where(target, logits, 0.0), 0, keepdims=True)
        exps = term if exps is None else exps + term
        hit = other if hit is None else hit + other
    both = jnp.concatenate([exps, hit], 0)
    for p in range(stats.shape[0]):
        stats[p] = both


def pull_kernel(
    batch, rows, sums, gain, bias, place, totals, unit, w_own, w_other, packed
):
    units = unit[...]
    row_total = jnp.sum(totals[...], 0)[0:1, : units.shape[0]]
    pull = None
    for w_hat, first in blocks_of(w_own, w_other):
        grad = grad_of(w_hat, units, place[...], first, row_total)
        term = lax.dot_general(
            grad, w_hat, (((0,), (0,)), ((), ())), preferred_element_type=F32
        )
        pull = term if pull is None else pull + term
    total = jnp.sum(sums[...], 0)
    normed, unit_f, scale, _ = head(rows[...], total, gain[...], bias[...], batch)
    radial = jnp.sum(unit_f * pull, 1, keepdims=True)
    shifts = (pull - unit_f * radial) * scale
    bias_part = jnp.sum(shifts, 0, keepdims=True)
    gain_part = jnp.sum(shifts * normed, 0, keepdims=True)
    tail = tail_of(bias_part, gain_part)
    parts = packed.shape[0]
    n = pull.shape[0] // parts
    for p in range(parts):
        packed[p, :n] = pull[p * n : (p + 1) * n].astype(BF16)
        packed[p, n:] = tail


def tail_of(bias_part, gain_part):
    pieces = split(bias_part, 3) + split(gain_part, 3)
    fill = jnp.zeros((PAD - 6, bias_part.shape[1]), F32)
    return jnp.concatenate(pieces + [fill], 0).astype(BF16)


def sums_of(tail):
    return jnp.concatenate(
        [jnp.sum(tail[k : k + 3], 0, keepdims=True) for k in (0, 3)], 0
    )


def split(value, count):
    pieces = []
    for _ in range(count):
        piece = value.astype(BF16).astype(F32)
        value = value - piece
        pieces.append(piece)
    return pieces


def total_kernel(lines, at, arrived, out):
    group = arrived.shape[2]
    n = group // lines
    place = at[0] * n if n % 128 else pl.multiple_of(at[0] * n, 128)
    own = other = hit = 0.0
    for x in range(lines):
        own = own + arrived[2 * x + at[1], 0:1]
        other = other + arrived[2 * x + 1 - at[1], 0:1]
        hit = hit + arrived[2 * x + at[1], 1:2, pl.ds(place, n)]
    both = jnp.concatenate(
        [
            jnp.concatenate([own, hit], 1),
            jnp.concatenate([other, jnp.zeros_like(hit)], 1),
        ],
        0,
    )
    for p in range(out.shape[0]):
        out[p] = both


def mid_kernel(rows_dev, arrived, packed):
    lines, _, lane = packed.shape
    total = jnp.sum(arrived[...].astype(F32), 0)
    width = total.shape[1]
    cuts = [slice(k, k + lane) for k in range(0, width, lane)]
    ends = sums_of(total[lines * rows_dev :])
    rows = split(ends[0:1], 2) + split(ends[1:2], 2)
    tail = [row[:, cut] for row in rows for cut in cuts]
    for p in range(lines):
        piece = total[p * rows_dev : (p + 1) * rows_dev]
        packed[p] = jnp.concatenate([piece[:, c] for c in cuts] + tail, 0).astype(BF16)


def home_kernel(rows_dev, arrived, grad, ends):
    total = jnp.sum(arrived[...].astype(F32), 0)
    lane = total.shape[1]
    n = grad.shape[1] // lane
    grad[...] = jnp.concatenate(
        [total[k * rows_dev : (k + 1) * rows_dev] for k in range(n)], 1
    )
    tail = total[n * rows_dev :]
    rows = []
    for v in range(2):
        both = tail[2 * v * n : (2 * v + 1) * n] + tail[(2 * v + 1) * n : (2 * v + 2) * n]
        rows.append(jnp.concatenate([both[k : k + 1] for k in range(n)], 1))
    both = jnp.concatenate(rows, 0)
    for p in range(ends.shape[0]):
        ends[p] = both


def raw_kernel(parts, at, place, place_2, totals, unit, unit_2, w_own, _, *refs):
    outs, (mine, sent, sems) = refs[:parts], refs[parts:]
    block = mine.shape[0]
    copies = []
    group = unit.shape[0]
    total = jnp.sum(totals[...], 0)
    for i in range(parts):
        first = pl.multiple_of(lax.rem(at[0] + i, parts) * block, 64)
        w_hat = w_own[pl.ds(first, block)]
        raw = None
        for units, places, row in ((unit, place, 0), (unit_2, place_2, 1)):
            grad = grad_of(
                w_hat, units[...], places[...], first, total[row : row + 1, :group]
            )
            term = jnp.dot(grad, units[...], preferred_element_type=F32)
            raw = term if raw is None else raw + term
        if i == 0:
            mine[...] = raw
            source = mine
        else:
            sent[i - 1] = raw.astype(BF16)
            source = sent.at[i - 1]
        copies.append(pltpu.make_async_copy(source, outs[i], sems.at[i]))
        copies[-1].start()
    for copy in copies:
        copy.wait()


def project_kernel(parts, at, picked, *refs):
    found, (out, picks_ref, sem) = refs[:parts], refs[parts:]
    block = out.shape[0]
    rows = pl.ds(pl.multiple_of(at[0] * block, 64), block)
    copy = pltpu.make_async_copy(picked.at[rows], picks_ref, sem)
    copy.start()
    raw = found[0][...]
    for piece in found[1:]:
        raw = raw + piece[...].astype(F32)
    copy.wait()
    picks = picks_ref[...].astype(F32)
    inv_norm = lax.rsqrt(jnp.sum(picks * picks, 1, keepdims=True) + EPSILON)
    w_unit = picks * inv_norm
    along = jnp.sum(w_unit * raw, 1, keepdims=True)
    out[...] = ((raw - w_unit * along) * inv_norm).astype(BF16)


def own_kernel(batch, at, inputs, sums, gain, bias, grad_unit, totals, terms, loss):
    n = inputs.shape[0]
    total = jnp.sum(sums[...], 0)
    normed, unit_f, scale, inv_std = head(
        inputs[...], total, gain[...], bias[...], batch
    )
    pull = grad_unit[...]
    radial = jnp.sum(unit_f * pull, 1, keepdims=True)
    shifts = (pull - unit_f * radial) * scale
    share = inv_std * gain[...]
    terms[0:n] = shifts * share
    terms[n : 2 * n] = normed * (share / batch)
    terms[2 * n : 3 * n] = jnp.broadcast_to(share / batch, (n, share.shape[1]))
    own = jnp.sum(totals[...], 0)[0:1]
    shape = (n, own.shape[1])
    ahead = lax.broadcasted_iota(jnp.int32, shape, 1) - lax.broadcasted_iota(
        jnp.int32, shape, 0
    )
    found = [
        jnp.sum(jnp.where(ahead == at[k], own, 0.0), 1, keepdims=True) for k in (0, 1)
    ]
    values = jnp.log(found[0]) - found[1]
    square = (n, n)
    same = lax.broadcasted_iota(jnp.int32, square, 0) == lax.broadcasted_iota(
        jnp.int32, square, 1
    )
    loss[...] = jnp.sum(jnp.where(same, values, 0.0), 0, keepdims=True)


def final_kernel(parts, at, terms, ends, *refs):
    found, (emb, grad, gain_grad, bias_grad) = refs[:parts], refs[parts:]
    block = found[0].shape[0]
    n = emb.shape[0]
    both = jnp.sum(ends[...], 0)
    bias_grad[...] = both[0:1]
    gain_grad[...] = both[1:2]
    emb[...] = (
        terms[0:n] - terms[2 * n : 3 * n] * both[0:1] - terms[n : 2 * n] * both[1:2]
    )
    for by, piece in enumerate(found):
        where = lax.rem(at[0] - by + parts, parts) * block
        grad[pl.ds(pl.multiple_of(where, 64), block)] = piece[...]


def body(embeddings, bn_gain, bn_bias, centres, sample_rows, label_shard, label_slot):
    nx, nz, nc, nr = (lax.axis_size(a) for a in ("x", "z", "core", "rep"))
    ix, iz, ic, ir = (lax.axis_index(a) for a in ("x", "z", "core", "rep"))
    rows_dev, width = embeddings.shape
    slots = sample_rows.shape[1]
    batch = rows_dev * nx * nz * nc * nr
    line_rows = nz * rows_dev
    group = nx * line_rows
    held = nc * slots
    quarter = slots // nr
    at = ir.astype(jnp.int32).reshape(1)
    gain, bias = bn_gain[None], bn_bias[None]

    picked = centres.at[sample_rows[0]].get(mode="promise_in_bounds")
    picks = picked.astype(F32)
    inv_norm = lax.rsqrt(jnp.sum(picks * picks, 1, keepdims=True) + EPSILON)
    w_own = (picks * inv_norm).astype(BF16)

    line = spread(embeddings, "z").reshape(line_rows, width)
    line, w_own = lax.optimization_barrier((line, w_own))
    rows = spread(line, "x").reshape(group, width)
    rows_f = rows.astype(F32)
    sums = spread(
        jnp.stack([jnp.sum(rows_f, 0), jnp.sum(rows_f * rows_f, 0)]), ("core", "rep")
    )
    w_other = shift(w_own, "core", 1)

    def of_core(labels, core):
        lines = labels.reshape(nx * nz, nc, rows_dev)
        return lax.dynamic_index_in_dim(lines, core, 1).reshape(1, group)

    owner, slot = of_core(label_shard, ic), of_core(label_slot, ic)
    chip = (ix * nz + iz) * nc
    place = jnp.where(
        owner == chip + ic, slot, jnp.where(owner == chip + 1 - ic, slot + slots, -1)
    )
    place_2 = jnp.where(
        of_core(label_shard, 1 - ic) == chip + ic, of_core(label_slot, 1 - ic), -1
    )

    unit, stats = call(
        lambda *refs: exp_kernel(batch, *refs),
        [VM] * 7,
        [VM] * 2,
        [
            jax.ShapeDtypeStruct((group, width), BF16),
            jax.ShapeDtypeStruct((nx * nc, 2, group), F32),
        ],
        2 * held * group * width,
        2 * held * width,
        held * group,
    )(rows, sums, gain, bias, place, w_own, w_other)
    unit_2 = shift(unit, "core", 1)

    stats = lax.all_to_all(stats, ("x", "core"), 0, 0)
    totals = call(
        lambda *refs: total_kernel(nx, *refs),
        [SM, VM],
        VM,
        jax.ShapeDtypeStruct((nz, nc, group + line_rows), F32),
        16 * group,
        64 * group,
        grant=SMALL,
    )(jnp.stack([ix, ic]).astype(jnp.int32), stats)
    totals, unit_2, place_2 = lax.optimization_barrier((totals, unit_2, place_2))
    totals = lax.all_to_all(totals, "z", 0, 0)

    pull = call(
        lambda *refs: pull_kernel(batch, *refs),
        [VM] * 9,
        VM,
        jax.ShapeDtypeStruct((nx, line_rows + PAD, width), BF16),
        4 * held * group * width,
        2 * held * width,
        held * group,
    )(rows, sums, gain, bias, place, totals, unit, w_own, w_other)

    piece = jax.ShapeDtypeStruct((quarter, width), BF16)
    mine, *sent = call(
        lambda *refs: raw_kernel(nr, *refs),
        [SM] + [VM] * 6 + [HB],
        [HO] * nr,
        [jax.ShapeDtypeStruct((quarter, width), F32)] + [piece] * (nr - 1),
        4 * held * group * width,
        2 * held * width,
        held * group,
        [
            pltpu.VMEM((quarter, width), F32),
            pltpu.VMEM((nr - 1, quarter, width), BF16),
            pltpu.SemaphoreType.DMA((nr,)),
        ],
    )(at, place, place_2, totals, unit, unit_2, w_own, pull)
    came = [shift(sent[by - 1], "rep", by) for by in range(1, nr)]
    grad = call(
        lambda *refs: project_kernel(nr, *refs),
        [SM, HB] + [VM] * nr,
        VM,
        piece,
        20 * quarter * width,
        14 * quarter * width,
        0,
        [pltpu.VMEM((quarter, width), BF16), pltpu.SemaphoreType.DMA],
        grant=SMALL,
    )(at, picked, mine, *came)
    pull = lax.all_to_all(pull, "x", 0, 0)
    pull, mine = lax.optimization_barrier((pull, mine))
    lanes = min(width, 128)
    tall = (rows_dev + 4) * (width // lanes)
    pull = call(
        lambda *refs: mid_kernel(rows_dev, *refs),
        [VM],
        VM,
        jax.ShapeDtypeStruct((nz, tall, lanes), BF16),
        nx * line_rows * width,
        2 * nx * line_rows * width,
        grant=SMALL,
    )(pull)
    pull = lax.all_to_all(pull, "z", 0, 0)
    grad_unit, ends = call(
        lambda *refs: home_kernel(rows_dev, *refs),
        [VM],
        [VM] * 2,
        [
            jax.ShapeDtypeStruct((rows_dev, width), F32),
            jax.ShapeDtypeStruct((nc * nr, 2, width), F32),
        ],
        nz * tall * lanes,
        2 * nz * tall * lanes,
        grant=SMALL,
    )(pull)
    ends = lax.all_to_all(ends, ("core", "rep"), 0, 0)

    own = jnp.stack([(ix * nz + iz) * rows_dev, group + iz * rows_dev])
    terms, row_loss = call(
        lambda *refs: own_kernel(batch, *refs),
        [SM] + [VM] * 6,
        [VM] * 2,
        [
            jax.ShapeDtypeStruct((3 * rows_dev, width), F32),
            jax.ShapeDtypeStruct((1, rows_dev), F32),
        ],
        40 * rows_dev * width,
        40 * rows_dev * width,
        grant=SMALL,
    )(own.astype(jnp.int32), embeddings, sums, gain, bias, grad_unit, totals)
    emb_grad, centre_grad, gain_grad, bias_grad = call(
        lambda *refs: final_kernel(nr, *refs),
        [SM] + [VM] * (2 + nr),
        [VM] * 4,
        [
            jax.ShapeDtypeStruct((rows_dev, width), F32),
            jax.ShapeDtypeStruct((slots, width), BF16),
            jax.ShapeDtypeStruct((1, width), F32),
            jax.ShapeDtypeStruct((1, width), F32),
        ],
        slots * width,
        4 * slots * width,
        grant=SMALL,
    )(at, terms, ends, grad, *[shift(grad, "rep", by) for by in range(1, nr)])
    return (row_loss[0], emb_grad, centre_grad, gain_grad[0], bias_grad[0])


def solution(mesh):
    shards, replicas = mesh.devices.shape
    split = (4, shards // 8, 2, replicas)
    fine = Mesh(mesh.devices.reshape(split), ("x", "z", "core", "rep"))
    cen = ("x", "z", "core")
    every = cen + ("rep",)
    return jax.shard_map(
        body,
        mesh=fine,
        in_specs=(
            P(every, None),
            P(),
            P(),
            P(cen, None),
            P(cen, None),
            P(None, "rep", None),
            P(None, "rep", None),
        ),
        out_specs=(P(every), P(every, None), P(cen, None), P(), P()),
        check_vma=False,
    )
```

```python
import jax
import jax.numpy as jnp
from jax import lax
from jax.experimental import pallas as pl
from jax.experimental.pallas import tpu as pltpu
from jax.sharding import Mesh, PartitionSpec as P

LOGIT_SCALE = 64.0
MARGIN = 0.4
EPSILON = 1e-05
F32 = jnp.float32
BF16 = jnp.bfloat16
LARGE = 60 * 1024 * 1024
SMALL = 20 * 1024 * 1024
PAD = 16


def spread(block, axes):
    copies = jnp.broadcast_to(block[None], (lax.axis_size(axes),) + block.shape)
    return lax.all_to_all(copies, axes, 0, 0)


def shift(block, axis, by):
    n = lax.axis_size(axis)
    return lax.ppermute(block, axis, [(i, (i + by) % n) for i in range(n)])


def head(inputs, sums, gain, bias, batch_total):
    mean = sums[0:1] / batch_total
    inv_std = lax.rsqrt(sums[1:2] / batch_total - mean * mean + EPSILON)
    normed = (inputs.astype(F32) - mean) * inv_std
    shifted = normed * gain + bias
    scale = lax.rsqrt(jnp.sum(shifted * shifted, 1, keepdims=True) + EPSILON)
    return normed, shifted * scale, scale, inv_std


VM = pl.BlockSpec(memory_space=pltpu.VMEM)
SM = pl.BlockSpec(memory_space=pltpu.SMEM)
HB = pl.BlockSpec(memory_space=pl.ANY)
HO = pl.BlockSpec(memory_space=pltpu.HBM)


def call(kernel, ins, outs, shapes, flops, size, exps=0, scratch=(), grant=LARGE):
    return pl.pallas_call(
        kernel,
        in_specs=ins,
        out_specs=outs,
        out_shape=shapes,
        scratch_shapes=list(scratch),
        compiler_params=pltpu.CompilerParams(vmem_limit_bytes=grant),
        cost_estimate=pl.CostEstimate(
            flops=flops, bytes_accessed=size, transcendentals=exps
        ),
    )


def hits(place, block, count, first):
    return place == lax.broadcasted_iota(jnp.int32, (block, count), 0) + first


def logits_of(w_hat, unit, place, first):
    cosine = lax.dot_general(
        w_hat, unit, (((1,), (1,)), ((), ())), preferred_element_type=F32
    )
    target = hits(place, w_hat.shape[0], unit.shape[0], first)
    return LOGIT_SCALE * cosine - jnp.where(target, LOGIT_SCALE * MARGIN, 0.0), target


def grad_of(w_hat, unit, place, first, total):
    logits, target = logits_of(w_hat, unit, place, first)
    return (jnp.exp(logits) / total - target.astype(F32)).astype(BF16)


def blocks_of(w_own, w_other):
    block = w_own.shape[0] // 2
    for i in range(4):
        source = w_own if i < 2 else w_other
        yield source[(i % 2) * block : (i % 2 + 1) * block], i * block


def exp_kernel(batch, rows, sums, gain, bias, place, w_own, w_other, unit, stats):
    total = jnp.sum(sums[...], 0)
    units = head(rows[...], total, gain[...], bias[...], batch)[1].astype(BF16)
    unit[...] = units
    exps = hit = None
    for w_hat, first in blocks_of(w_own, w_other):
        logits, target = logits_of(w_hat, units, place[...], first)
        term = jnp.sum(jnp.exp(logits), 0, keepdims=True)
        other = jnp.sum(jnp.where(target, logits, 0.0), 0, keepdims=True)
        exps = term if exps is None else exps + term
        hit = other if hit is None else hit + other
    both = jnp.concatenate([exps, hit], 0)
    for p in range(stats.shape[0]):
        stats[p] = both


def pull_kernel(
    batch, rows, sums, gain, bias, place, totals, unit, w_own, w_other, packed
):
    units = unit[...]
    row_total = jnp.sum(totals[...], 0)[0:1, : units.shape[0]]
    pull = None
    for w_hat, first in blocks_of(w_own, w_other):
        grad = grad_of(w_hat, units, place[...], first, row_total)
        term = lax.dot_general(
            grad, w_hat, (((0,), (0,)), ((), ())), preferred_element_type=F32
        )
        pull = term if pull is None else pull + term
    total = jnp.sum(sums[...], 0)
    normed, unit_f, scale, _ = head(rows[...], total, gain[...], bias[...], batch)
    radial = jnp.sum(unit_f * pull, 1, keepdims=True)
    shifts = (pull - unit_f * radial) * scale
    bias_part = jnp.sum(shifts, 0, keepdims=True)
    gain_part = jnp.sum(shifts * normed, 0, keepdims=True)
    tail = tail_of(bias_part, gain_part)
    parts = packed.shape[0]
    n = pull.shape[0] // parts
    for p in range(parts):
        packed[p, :n] = pull[p * n : (p + 1) * n].astype(BF16)
        packed[p, n:] = tail


def tail_of(bias_part, gain_part):
    pieces = split(bias_part, 3) + split(gain_part, 3)
    fill = jnp.zeros((PAD - 6, bias_part.shape[1]), F32)
    return jnp.concatenate(pieces + [fill], 0).astype(BF16)


def sums_of(tail):
    return jnp.concatenate(
        [jnp.sum(tail[k : k + 3], 0, keepdims=True) for k in (0, 3)], 0
    )


def split(value, count):
    pieces = []
    for _ in range(count):
        piece = value.astype(BF16).astype(F32)
        value = value - piece
        pieces.append(piece)
    return pieces


def total_kernel(lines, at, arrived, out):
    group = arrived.shape[2]
    n = group // lines
    place = at[0] * n if n % 128 else pl.multiple_of(at[0] * n, 128)
    own = other = hit = 0.0
    for x in range(lines):
        own = own + arrived[2 * x + at[1], 0:1]
        other = other + arrived[2 * x + 1 - at[1], 0:1]
        hit = hit + arrived[2 * x + at[1], 1:2, pl.ds(place, n)]
    both = jnp.concatenate(
        [
            jnp.concatenate([own, hit], 1),
            jnp.concatenate([other, jnp.zeros_like(hit)], 1),
        ],
        0,
    )
    for p in range(out.shape[0]):
        out[p] = both


def mid_kernel(rows_dev, arrived, packed):
    lines, _, lane = packed.shape
    total = jnp.sum(arrived[...].astype(F32), 0)
    width = total.shape[1]
    cuts = [slice(k, k + lane) for k in range(0, width, lane)]
    ends = sums_of(total[lines * rows_dev :])
    rows = split(ends[0:1], 2) + split(ends[1:2], 2)
    tail = [row[:, cut] for row in rows for cut in cuts]
    for p in range(lines):
        piece = total[p * rows_dev : (p + 1) * rows_dev]
        packed[p] = jnp.concatenate([piece[:, c] for c in cuts] + tail, 0).astype(BF16)


def home_kernel(rows_dev, arrived, grad, ends):
    total = jnp.sum(arrived[...].astype(F32), 0)
    lane = total.shape[1]
    n = grad.shape[1] // lane
    grad[...] = jnp.concatenate(
        [total[k * rows_dev : (k + 1) * rows_dev] for k in range(n)], 1
    )
    tail = total[n * rows_dev :]
    rows = []
    for v in range(2):
        both = tail[2 * v * n : (2 * v + 1) * n] + tail[(2 * v + 1) * n : (2 * v + 2) * n]
        rows.append(jnp.concatenate([both[k : k + 1] for k in range(n)], 1))
    both = jnp.concatenate(rows, 0)
    for p in range(ends.shape[0]):
        ends[p] = both


def raw_kernel(parts, at, place, place_2, totals, unit, unit_2, w_own, _, *refs):
    outs, (mine, sent, sems) = refs[:parts], refs[parts:]
    block = mine.shape[0]
    copies = []
    group = unit.shape[0]
    total = jnp.sum(totals[...], 0)
    for i in range(parts):
        first = pl.multiple_of(lax.rem(at[0] + i, parts) * block, 64)
        w_hat = w_own[pl.ds(first, block)]
        raw = None
        for units, places, row in ((unit, place, 0), (unit_2, place_2, 1)):
            grad = grad_of(
                w_hat, units[...], places[...], first, total[row : row + 1, :group]
            )
            term = jnp.dot(grad, units[...], preferred_element_type=F32)
            raw = term if raw is None else raw + term
        if i == 0:
            mine[...] = raw
            source = mine
        else:
            sent[i - 1] = raw.astype(BF16)
            source = sent.at[i - 1]
        copies.append(pltpu.make_async_copy(source, outs[i], sems.at[i]))
        copies[-1].start()
    for copy in copies:
        copy.wait()


def project_kernel(parts, at, picked, *refs):
    found, (out, picks_ref, sem) = refs[:parts], refs[parts:]
    block = out.shape[0]
    rows = pl.ds(pl.multiple_of(at[0] * block, 64), block)
    copy = pltpu.make_async_copy(picked.at[rows], picks_ref, sem)
    copy.start()
    raw = found[0][...]
    for piece in found[1:]:
        raw = raw + piece[...].astype(F32)
    copy.wait()
    picks = picks_ref[...].astype(F32)
    inv_norm = lax.rsqrt(jnp.sum(picks * picks, 1, keepdims=True) + EPSILON)
    w_unit = picks * inv_norm
    along = jnp.sum(w_unit * raw, 1, keepdims=True)
    out[...] = ((raw - w_unit * along) * inv_norm).astype(BF16)


def own_kernel(batch, at, inputs, sums, gain, bias, grad_unit, totals, terms, loss):
    n = inputs.shape[0]
    total = jnp.sum(sums[...], 0)
    normed, unit_f, scale, inv_std = head(
        inputs[...], total, gain[...], bias[...], batch
    )
    pull = grad_unit[...]
    radial = jnp.sum(unit_f * pull, 1, keepdims=True)
    shifts = (pull - unit_f * radial) * scale
    share = inv_std * gain[...]
    terms[0:n] = shifts * share
    terms[n : 2 * n] = normed * (share / batch)
    terms[2 * n : 3 * n] = jnp.broadcast_to(share / batch, (n, share.shape[1]))
    own = jnp.sum(totals[...], 0)[0:1]
    shape = (n, own.shape[1])
    ahead = lax.broadcasted_iota(jnp.int32, shape, 1) - lax.broadcasted_iota(
        jnp.int32, shape, 0
    )
    found = [
        jnp.sum(jnp.where(ahead == at[k], own, 0.0), 1, keepdims=True) for k in (0, 1)
    ]
    values = jnp.log(found[0]) - found[1]
    square = (n, n)
    same = lax.broadcasted_iota(jnp.int32, square, 0) == lax.broadcasted_iota(
        jnp.int32, square, 1
    )
    loss[...] = jnp.sum(jnp.where(same, values, 0.0), 0, keepdims=True)


def final_kernel(parts, at, terms, ends, *refs):
    found, (emb, grad, gain_grad, bias_grad, sems) = refs[:parts], refs[parts:]
    block = found[0].shape[0]
    n = emb.shape[0]
    copies = []
    for by, piece in enumerate(found):
        where = pl.multiple_of(lax.rem(at[0] - by + parts, parts) * block, 64)
        copies.append(
            pltpu.make_async_copy(piece, grad.at[pl.ds(where, block)], sems.at[by])
        )
        copies[-1].start()
    both = jnp.sum(ends[...], 0)
    bias_grad[...] = both[0:1]
    gain_grad[...] = both[1:2]
    emb[...] = (
        terms[0:n] - terms[2 * n : 3 * n] * both[0:1] - terms[n : 2 * n] * both[1:2]
    )
    for copy in copies:
        copy.wait()


def body(embeddings, bn_gain, bn_bias, centres, sample_rows, label_shard, label_slot):
    nx, nz, nc, nr = (lax.axis_size(a) for a in ("x", "z", "core", "rep"))
    ix, iz, ic, ir = (lax.axis_index(a) for a in ("x", "z", "core", "rep"))
    rows_dev, width = embeddings.shape
    slots = sample_rows.shape[1]
    batch = rows_dev * nx * nz * nc * nr
    line_rows = nz * rows_dev
    group = nx * line_rows
    held = nc * slots
    quarter = slots // nr
    at = ir.astype(jnp.int32).reshape(1)
    gain, bias = bn_gain[None], bn_bias[None]

    picked = centres.at[sample_rows[0]].get(mode="promise_in_bounds")
    picks = picked.astype(F32)
    inv_norm = lax.rsqrt(jnp.sum(picks * picks, 1, keepdims=True) + EPSILON)
    w_own = (picks * inv_norm).astype(BF16)

    def of_core(labels, core):
        lines = labels.reshape(nx * nz, nc, rows_dev)
        return lax.dynamic_index_in_dim(lines, core, 1).reshape(1, group)

    owner, slot = of_core(label_shard, ic), of_core(label_slot, ic)
    chip = (ix * nz + iz) * nc
    place = jnp.where(
        owner == chip + ic, slot, jnp.where(owner == chip + 1 - ic, slot + slots, -1)
    )
    place_2 = jnp.where(
        of_core(label_shard, 1 - ic) == chip + ic, of_core(label_slot, 1 - ic), -1
    )

    line = spread(embeddings, "z").reshape(line_rows, width)
    line, w_own = lax.optimization_barrier((line, w_own))
    rows = spread(line, "x").reshape(group, width)
    rows_f = rows.astype(F32)
    sums = spread(
        jnp.stack([jnp.sum(rows_f, 0), jnp.sum(rows_f * rows_f, 0)]), ("core", "rep")
    )
    w_other = shift(w_own, "core", 1)

    unit, stats = call(
        lambda *refs: exp_kernel(batch, *refs),
        [VM] * 7,
        [VM] * 2,
        [
            jax.ShapeDtypeStruct((group, width), BF16),
            jax.ShapeDtypeStruct((nx * nc, 2, group), F32),
        ],
        2 * held * group * width,
        2 * held * width,
        held * group,
    )(rows, sums, gain, bias, place, w_own, w_other)
    unit_2 = shift(unit, "core", 1)

    stats = lax.all_to_all(stats, ("x", "core"), 0, 0)
    totals = call(
        lambda *refs: total_kernel(nx, *refs),
        [SM, VM],
        VM,
        jax.ShapeDtypeStruct((nz, nc, group + line_rows), F32),
        16 * group,
        64 * group,
        grant=SMALL,
    )(jnp.stack([ix, ic]).astype(jnp.int32), stats)
    totals, unit_2, place_2 = lax.optimization_barrier((totals, unit_2, place_2))
    totals = lax.all_to_all(totals, "z", 0, 0)

    pull = call(
        lambda *refs: pull_kernel(batch, *refs),
        [VM] * 9,
        VM,
        jax.ShapeDtypeStruct((nx, line_rows + PAD, width), BF16),
        4 * held * group * width,
        2 * held * width,
        held * group,
    )(rows, sums, gain, bias, place, totals, unit, w_own, w_other)

    piece = jax.ShapeDtypeStruct((quarter, width), BF16)
    mine, *sent = call(
        lambda *refs: raw_kernel(nr, *refs),
        [SM] + [VM] * 6 + [HB],
        [HO] * nr,
        [jax.ShapeDtypeStruct((quarter, width), F32)] + [piece] * (nr - 1),
        4 * held * group * width,
        2 * held * width,
        held * group,
        [
            pltpu.VMEM((quarter, width), F32),
            pltpu.VMEM((nr - 1, quarter, width), BF16),
            pltpu.SemaphoreType.DMA((nr,)),
        ],
    )(at, place, place_2, totals, unit, unit_2, w_own, pull)
    came = [shift(sent[by - 1], "rep", by) for by in range(1, nr)]

    pull = lax.all_to_all(pull, "x", 0, 0)
    pull, came = lax.optimization_barrier((pull, came))
    grad = call(
        lambda *refs: project_kernel(nr, *refs),
        [SM, HB] + [VM] * nr,
        VM,
        piece,
        20 * quarter * width,
        14 * quarter * width,
        0,
        [pltpu.VMEM((quarter, width), BF16), pltpu.SemaphoreType.DMA],
        grant=SMALL,
    )(at, picked, mine, *came)
    lanes = min(width, 128)
    tall = (rows_dev + 4) * (width // lanes)
    pull = call(
        lambda *refs: mid_kernel(rows_dev, *refs),
        [VM],
        VM,
        jax.ShapeDtypeStruct((nz, tall, lanes), BF16),
        nx * line_rows * width,
        2 * nx * line_rows * width,
        grant=SMALL,
    )(pull)
    pull = lax.all_to_all(pull, "z", 0, 0)
    grad_unit, ends = call(
        lambda *refs: home_kernel(rows_dev, *refs),
        [VM],
        [VM] * 2,
        [
            jax.ShapeDtypeStruct((rows_dev, width), F32),
            jax.ShapeDtypeStruct((nc * nr, 2, width), F32),
        ],
        nz * tall * lanes,
        2 * nz * tall * lanes,
        grant=SMALL,
    )(pull)
    ends = lax.all_to_all(ends, ("core", "rep"), 0, 0)

    own = jnp.stack([(ix * nz + iz) * rows_dev, group + iz * rows_dev])
    terms, row_loss = call(
        lambda *refs: own_kernel(batch, *refs),
        [SM] + [VM] * 6,
        [VM] * 2,
        [
            jax.ShapeDtypeStruct((3 * rows_dev, width), F32),
            jax.ShapeDtypeStruct((1, rows_dev), F32),
        ],
        40 * rows_dev * width,
        40 * rows_dev * width,
        grant=SMALL,
    )(own.astype(jnp.int32), embeddings, sums, gain, bias, grad_unit, totals)
    emb_grad, centre_grad, gain_grad, bias_grad = call(
        lambda *refs: final_kernel(nr, *refs),
        [SM] + [VM] * 2 + [HB] * nr,
        [VM] * 4,
        [
            jax.ShapeDtypeStruct((rows_dev, width), F32),
            jax.ShapeDtypeStruct((slots, width), BF16),
            jax.ShapeDtypeStruct((1, width), F32),
            jax.ShapeDtypeStruct((1, width), F32),
        ],
        slots * width,
        4 * slots * width,
        0,
        [pltpu.SemaphoreType.DMA((nr,))],
        grant=SMALL,
    )(at, terms, ends, grad, *[shift(grad, "rep", by) for by in range(1, nr)])
    return (row_loss[0], emb_grad, centre_grad, gain_grad[0], bias_grad[0])


def solution(mesh):
    shards, replicas = mesh.devices.shape
    split = (4, shards // 8, 2, replicas)
    fine = Mesh(mesh.devices.reshape(split), ("x", "z", "core", "rep"))
    cen = ("x", "z", "core")
    every = cen + ("rep",)
    return jax.shard_map(
        body,
        mesh=fine,
        in_specs=(
            P(every, None),
            P(),
            P(),
            P(cen, None),
            P(cen, None),
            P(None, "rep", None),
            P(None, "rep", None),
        ),
        out_specs=(P(every), P(every, None), P(cen, None), P(), P()),
        check_vma=False,
    )
```

```python
import math

import jax
import jax.numpy as jnp
from jax import lax
from jax.experimental import pallas as pl
from jax.experimental.pallas import tpu as pltpu
from jax.sharding import Mesh, PartitionSpec as P

LOGIT_SCALE = 64.0
MARGIN = 0.4
EPSILON = 1e-05
SHRINK = math.exp(-LOGIT_SCALE * MARGIN)
F32 = jnp.float32
BF16 = jnp.bfloat16
LARGE = 60 * 1024 * 1024
SMALL = 20 * 1024 * 1024
PAD = 16


def spread(block, axes):
    copies = jnp.broadcast_to(block[None], (lax.axis_size(axes),) + block.shape)
    return lax.all_to_all(copies, axes, 0, 0)


def shift(block, axis, by):
    n = lax.axis_size(axis)
    return lax.ppermute(block, axis, [(i, (i + by) % n) for i in range(n)])


def head(inputs, sums, gain, bias, batch_total):
    mean = sums[0:1] / batch_total
    inv_std = lax.rsqrt(sums[1:2] / batch_total - mean * mean + EPSILON)
    normed = (inputs.astype(F32) - mean) * inv_std
    shifted = normed * gain + bias
    scale = lax.rsqrt(jnp.sum(shifted * shifted, 1, keepdims=True) + EPSILON)
    return normed, shifted * scale, scale, inv_std


VM = pl.BlockSpec(memory_space=pltpu.VMEM)
SM = pl.BlockSpec(memory_space=pltpu.SMEM)
HB = pl.BlockSpec(memory_space=pl.ANY)
HO = pl.BlockSpec(memory_space=pltpu.HBM)


def call(kernel, ins, outs, shapes, flops, size, exps=0, scratch=(), grant=LARGE):
    return pl.pallas_call(
        kernel,
        in_specs=ins,
        out_specs=outs,
        out_shape=shapes,
        scratch_shapes=list(scratch),
        compiler_params=pltpu.CompilerParams(vmem_limit_bytes=grant),
        cost_estimate=pl.CostEstimate(
            flops=flops, bytes_accessed=size, transcendentals=exps
        ),
    )


def hits(place, block, count, first):
    return place == lax.broadcasted_iota(jnp.int32, (block, count), 0) + first


def cosine_of(w_hat, unit, place, first):
    cosine = lax.dot_general(
        w_hat, unit, (((1,), (1,)), ((), ())), preferred_element_type=F32
    )
    return cosine, hits(place, w_hat.shape[0], unit.shape[0], first)


def grad_of(w_hat, unit, place, first, inverse):
    cosine, target = cosine_of(w_hat, unit, place, first)
    share = jnp.exp(LOGIT_SCALE * cosine) * inverse
    return jnp.where(target, share * SHRINK - 1.0, share).astype(BF16)


def blocks_of(w_own, w_other):
    block = w_own.shape[0] // 2
    for i in range(4):
        source = w_own if i < 2 else w_other
        yield source[(i % 2) * block : (i % 2 + 1) * block], i * block


def exp_kernel(batch, rows, sums, gain, bias, place, w_own, w_other, unit, stats):
    total = jnp.sum(sums[...], 0)
    units = head(rows[...], total, gain[...], bias[...], batch)[1].astype(BF16)
    unit[...] = units
    exps = hit = None
    for w_hat, first in blocks_of(w_own, w_other):
        cosine, target = cosine_of(w_hat, units, place[...], first)
        term = jnp.exp(LOGIT_SCALE * cosine)
        term = jnp.sum(jnp.where(target, term * SHRINK, term), 0, keepdims=True)
        other = jnp.sum(jnp.where(target, cosine, 0.0), 0, keepdims=True)
        exps = term if exps is None else exps + term
        hit = other if hit is None else hit + other
    hit = jnp.where(place[...] >= 0, LOGIT_SCALE * hit - LOGIT_SCALE * MARGIN, 0.0)
    both = jnp.concatenate([exps, hit], 0)
    for p in range(stats.shape[0]):
        stats[p] = both


def pull_kernel(
    batch, rows, sums, gain, bias, place, totals, unit, w_own, w_other, packed
):
    units = unit[...]
    inverse = 1.0 / jnp.sum(totals[...], 0)[0:1, : units.shape[0]]
    pull = None
    for w_hat, first in blocks_of(w_own, w_other):
        grad = grad_of(w_hat, units, place[...], first, inverse)
        term = lax.dot_general(
            grad, w_hat, (((0,), (0,)), ((), ())), preferred_element_type=F32
        )
        pull = term if pull is None else pull + term
    total = jnp.sum(sums[...], 0)
    normed, unit_f, scale, _ = head(rows[...], total, gain[...], bias[...], batch)
    radial = jnp.sum(unit_f * pull, 1, keepdims=True)
    shifts = (pull - unit_f * radial) * scale
    bias_part = jnp.sum(shifts, 0, keepdims=True)
    gain_part = jnp.sum(shifts * normed, 0, keepdims=True)
    tail = tail_of(bias_part, gain_part)
    parts = packed.shape[0]
    n = pull.shape[0] // parts
    for p in range(parts):
        packed[p, :n] = pull[p * n : (p + 1) * n].astype(BF16)
        packed[p, n:] = tail


def tail_of(bias_part, gain_part):
    pieces = split(bias_part, 3) + split(gain_part, 3)
    fill = jnp.zeros((PAD - 6, bias_part.shape[1]), F32)
    return jnp.concatenate(pieces + [fill], 0).astype(BF16)


def sums_of(tail):
    return jnp.concatenate(
        [jnp.sum(tail[k : k + 3], 0, keepdims=True) for k in (0, 3)], 0
    )


def split(value, count):
    pieces = []
    for _ in range(count):
        piece = value.astype(BF16).astype(F32)
        value = value - piece
        pieces.append(piece)
    return pieces


def total_kernel(lines, at, arrived, out):
    group = arrived.shape[2]
    n = group // lines
    place = at[0] * n if n % 128 else pl.multiple_of(at[0] * n, 128)
    own = other = hit = 0.0
    for x in range(lines):
        own = own + arrived[2 * x + at[1], 0:1]
        other = other + arrived[2 * x + 1 - at[1], 0:1]
        hit = hit + arrived[2 * x + at[1], 1:2, pl.ds(place, n)]
    both = jnp.concatenate(
        [
            jnp.concatenate([own, hit], 1),
            jnp.concatenate([other, jnp.zeros_like(hit)], 1),
        ],
        0,
    )
    for p in range(out.shape[0]):
        out[p] = both


def mid_kernel(rows_dev, arrived, packed):
    lines, _, lane = packed.shape
    total = jnp.sum(arrived[...].astype(F32), 0)
    width = total.shape[1]
    cuts = [slice(k, k + lane) for k in range(0, width, lane)]
    ends = sums_of(total[lines * rows_dev :])
    rows = split(ends[0:1], 2) + split(ends[1:2], 2)
    tail = [row[:, cut] for row in rows for cut in cuts]
    for p in range(lines):
        piece = total[p * rows_dev : (p + 1) * rows_dev]
        packed[p] = jnp.concatenate([piece[:, c] for c in cuts] + tail, 0).astype(BF16)


def home_kernel(rows_dev, arrived, grad, ends):
    total = jnp.sum(arrived[...].astype(F32), 0)
    lane = total.shape[1]
    n = grad.shape[1] // lane
    grad[...] = jnp.concatenate(
        [total[k * rows_dev : (k + 1) * rows_dev] for k in range(n)], 1
    )
    tail = total[n * rows_dev :]
    rows = []
    for v in range(2):
        both = tail[2 * v * n : (2 * v + 1) * n] + tail[(2 * v + 1) * n : (2 * v + 2) * n]
        rows.append(jnp.concatenate([both[k : k + 1] for k in range(n)], 1))
    both = jnp.concatenate(rows, 0)
    for p in range(ends.shape[0]):
        ends[p] = both


def raw_kernel(parts, at, place, place_2, totals, unit, unit_2, w_own, _, *refs):
    outs, (mine, sent, sems) = refs[:parts], refs[parts:]
    block = mine.shape[0]
    copies = []
    group = unit.shape[0]
    inverse = 1.0 / jnp.sum(totals[...], 0)[:, :group]
    for i in range(parts):
        first = pl.multiple_of(lax.rem(at[0] + i, parts) * block, 64)
        w_hat = w_own[pl.ds(first, block)]
        raw = None
        for units, places, row in ((unit, place, 0), (unit_2, place_2, 1)):
            grad = grad_of(
                w_hat, units[...], places[...], first, inverse[row : row + 1]
            )
            term = jnp.dot(grad, units[...], preferred_element_type=F32)
            raw = term if raw is None else raw + term
        if i == 0:
            mine[...] = raw
            source = mine
        else:
            sent[i - 1] = raw.astype(BF16)
            source = sent.at[i - 1]
        copies.append(pltpu.make_async_copy(source, outs[i], sems.at[i]))
        copies[-1].start()
    for copy in copies:
        copy.wait()


def project_kernel(parts, at, picked, *refs):
    found, (out, picks_ref, sem) = refs[:parts], refs[parts:]
    block = out.shape[0]
    rows = pl.ds(pl.multiple_of(at[0] * block, 64), block)
    copy = pltpu.make_async_copy(picked.at[rows], picks_ref, sem)
    copy.start()
    raw = found[0][...]
    for piece in found[1:]:
        raw = raw + piece[...].astype(F32)
    copy.wait()
    picks = picks_ref[...].astype(F32)
    inv_norm = lax.rsqrt(jnp.sum(picks * picks, 1, keepdims=True) + EPSILON)
    w_unit = picks * inv_norm
    along = jnp.sum(w_unit * raw, 1, keepdims=True)
    out[...] = ((raw - w_unit * along) * inv_norm).astype(BF16)


def own_kernel(batch, at, inputs, sums, gain, bias, grad_unit, totals, terms, loss):
    n = inputs.shape[0]
    total = jnp.sum(sums[...], 0)
    normed, unit_f, scale, inv_std = head(
        inputs[...], total, gain[...], bias[...], batch
    )
    pull = grad_unit[...]
    radial = jnp.sum(unit_f * pull, 1, keepdims=True)
    shifts = (pull - unit_f * radial) * scale
    share = inv_std * gain[...]
    terms[0:n] = shifts * share
    terms[n : 2 * n] = normed * (share / batch)
    terms[2 * n : 3 * n] = jnp.broadcast_to(share / batch, (n, share.shape[1]))
    own = jnp.sum(totals[...], 0)[0:1]
    shape = (n, own.shape[1])
    ahead = lax.broadcasted_iota(jnp.int32, shape, 1) - lax.broadcasted_iota(
        jnp.int32, shape, 0
    )
    found = [
        jnp.sum(jnp.where(ahead == at[k], own, 0.0), 1, keepdims=True) for k in (0, 1)
    ]
    values = jnp.log(found[0]) - found[1]
    square = (n, n)
    same = lax.broadcasted_iota(jnp.int32, square, 0) == lax.broadcasted_iota(
        jnp.int32, square, 1
    )
    loss[...] = jnp.sum(jnp.where(same, values, 0.0), 0, keepdims=True)


def final_kernel(parts, at, terms, ends, *refs):
    found, (emb, grad, gain_grad, bias_grad) = refs[:parts], refs[parts:]
    block = found[0].shape[0]
    n = emb.shape[0]
    both = jnp.sum(ends[...], 0)
    bias_grad[...] = both[0:1]
    gain_grad[...] = both[1:2]
    emb[...] = (
        terms[0:n] - terms[2 * n : 3 * n] * both[0:1] - terms[n : 2 * n] * both[1:2]
    )
    for by, piece in enumerate(found):
        where = lax.rem(at[0] - by + parts, parts) * block
        grad[pl.ds(pl.multiple_of(where, 64), block)] = piece[...]


def body(embeddings, bn_gain, bn_bias, centres, sample_rows, label_shard, label_slot):
    nx, nz, nc, nr = (lax.axis_size(a) for a in ("x", "z", "core", "rep"))
    ix, iz, ic, ir = (lax.axis_index(a) for a in ("x", "z", "core", "rep"))
    rows_dev, width = embeddings.shape
    slots = sample_rows.shape[1]
    batch = rows_dev * nx * nz * nc * nr
    line_rows = nz * rows_dev
    group = nx * line_rows
    held = nc * slots
    quarter = slots // nr
    at = ir.astype(jnp.int32).reshape(1)
    gain, bias = bn_gain[None], bn_bias[None]

    picked = centres.at[sample_rows[0]].get(mode="promise_in_bounds")
    picks = picked.astype(F32)
    inv_norm = lax.rsqrt(jnp.sum(picks * picks, 1, keepdims=True) + EPSILON)
    w_own = (picks * inv_norm).astype(BF16)

    line = spread(embeddings, "z").reshape(line_rows, width)
    line, w_own = lax.optimization_barrier((line, w_own))
    rows = spread(line, "x").reshape(group, width)
    rows_f = rows.astype(F32)
    sums = spread(
        jnp.stack([jnp.sum(rows_f, 0), jnp.sum(rows_f * rows_f, 0)]), ("core", "rep")
    )
    w_other = shift(w_own, "core", 1)

    def of_core(labels, core):
        lines = labels.reshape(nx * nz, nc, rows_dev)
        return lax.dynamic_index_in_dim(lines, core, 1).reshape(1, group)

    owner, slot = of_core(label_shard, ic), of_core(label_slot, ic)
    chip = (ix * nz + iz) * nc
    place = jnp.where(
        owner == chip + ic, slot, jnp.where(owner == chip + 1 - ic, slot + slots, -1)
    )
    place_2 = jnp.where(
        of_core(label_shard, 1 - ic) == chip + ic, of_core(label_slot, 1 - ic), -1
    )

    unit, stats = call(
        lambda *refs: exp_kernel(batch, *refs),
        [VM] * 7,
        [VM] * 2,
        [
            jax.ShapeDtypeStruct((group, width), BF16),
            jax.ShapeDtypeStruct((nx * nc, 2, group), F32),
        ],
        2 * held * group * width,
        2 * held * width,
        held * group,
    )(rows, sums, gain, bias, place, w_own, w_other)
    unit_2 = shift(unit, "core", 1)

    stats = lax.all_to_all(stats, ("x", "core"), 0, 0)
    totals = call(
        lambda *refs: total_kernel(nx, *refs),
        [SM, VM],
        VM,
        jax.ShapeDtypeStruct((nz, nc, group + line_rows), F32),
        16 * group,
        64 * group,
        grant=SMALL,
    )(jnp.stack([ix, ic]).astype(jnp.int32), stats)
    totals, unit_2, place_2 = lax.optimization_barrier((totals, unit_2, place_2))
    totals = lax.all_to_all(totals, "z", 0, 0)

    pull = call(
        lambda *refs: pull_kernel(batch, *refs),
        [VM] * 9,
        VM,
        jax.ShapeDtypeStruct((nx, line_rows + PAD, width), BF16),
        4 * held * group * width,
        2 * held * width,
        held * group,
    )(rows, sums, gain, bias, place, totals, unit, w_own, w_other)

    piece = jax.ShapeDtypeStruct((quarter, width), BF16)
    mine, *sent = call(
        lambda *refs: raw_kernel(nr, *refs),
        [SM] + [VM] * 6 + [HB],
        [HO] * nr,
        [jax.ShapeDtypeStruct((quarter, width), F32)] + [piece] * (nr - 1),
        4 * held * group * width,
        2 * held * width,
        held * group,
        [
            pltpu.VMEM((quarter, width), F32),
            pltpu.VMEM((nr - 1, quarter, width), BF16),
            pltpu.SemaphoreType.DMA((nr,)),
        ],
    )(at, place, place_2, totals, unit, unit_2, w_own, pull)
    came = [shift(sent[by - 1], "rep", by) for by in range(1, nr)]
    grad = call(
        lambda *refs: project_kernel(nr, *refs),
        [SM, HB] + [VM] * nr,
        VM,
        piece,
        20 * quarter * width,
        14 * quarter * width,
        0,
        [pltpu.VMEM((quarter, width), BF16), pltpu.SemaphoreType.DMA],
        grant=SMALL,
    )(at, picked, mine, *came)
    pull = lax.all_to_all(pull, "x", 0, 0)
    pull, mine = lax.optimization_barrier((pull, mine))
    lanes = min(width, 128)
    tall = (rows_dev + 4) * (width // lanes)
    pull = call(
        lambda *refs: mid_kernel(rows_dev, *refs),
        [VM],
        VM,
        jax.ShapeDtypeStruct((nz, tall, lanes), BF16),
        nx * line_rows * width,
        2 * nx * line_rows * width,
        grant=SMALL,
    )(pull)
    pull = lax.all_to_all(pull, "z", 0, 0)
    grad_unit, ends = call(
        lambda *refs: home_kernel(rows_dev, *refs),
        [VM],
        [VM] * 2,
        [
            jax.ShapeDtypeStruct((rows_dev, width), F32),
            jax.ShapeDtypeStruct((nc * nr, 2, width), F32),
        ],
        nz * tall * lanes,
        2 * nz * tall * lanes,
        grant=SMALL,
    )(pull)
    ends = lax.all_to_all(ends, ("core", "rep"), 0, 0)

    own = jnp.stack([(ix * nz + iz) * rows_dev, group + iz * rows_dev])
    terms, row_loss = call(
        lambda *refs: own_kernel(batch, *refs),
        [SM] + [VM] * 6,
        [VM] * 2,
        [
            jax.ShapeDtypeStruct((3 * rows_dev, width), F32),
            jax.ShapeDtypeStruct((1, rows_dev), F32),
        ],
        40 * rows_dev * width,
        40 * rows_dev * width,
        grant=SMALL,
    )(own.astype(jnp.int32), embeddings, sums, gain, bias, grad_unit, totals)
    emb_grad, centre_grad, gain_grad, bias_grad = call(
        lambda *refs: final_kernel(nr, *refs),
        [SM] + [VM] * (2 + nr),
        [VM] * 4,
        [
            jax.ShapeDtypeStruct((rows_dev, width), F32),
            jax.ShapeDtypeStruct((slots, width), BF16),
            jax.ShapeDtypeStruct((1, width), F32),
            jax.ShapeDtypeStruct((1, width), F32),
        ],
        slots * width,
        4 * slots * width,
        grant=SMALL,
    )(at, terms, ends, grad, *[shift(grad, "rep", by) for by in range(1, nr)])
    return (row_loss[0], emb_grad, centre_grad, gain_grad[0], bias_grad[0])


def solution(mesh):
    shards, replicas = mesh.devices.shape
    split = (4, shards // 8, 2, replicas)
    fine = Mesh(mesh.devices.reshape(split), ("x", "z", "core", "rep"))
    cen = ("x", "z", "core")
    every = cen + ("rep",)
    return jax.shard_map(
        body,
        mesh=fine,
        in_specs=(
            P(every, None),
            P(),
            P(),
            P(cen, None),
            P(cen, None),
            P(None, "rep", None),
            P(None, "rep", None),
        ),
        out_specs=(P(every), P(every, None), P(cen, None), P(), P()),
        check_vma=False,
    )
```

```python
import math

import jax
import jax.numpy as jnp
from jax import lax
from jax.experimental import pallas as pl
from jax.experimental.pallas import tpu as pltpu
from jax.sharding import Mesh, PartitionSpec as P

LOGIT_SCALE = 64.0
MARGIN = 0.4
EPSILON = 1e-05
SHRINK = math.exp(-LOGIT_SCALE * MARGIN)
F32 = jnp.float32
BF16 = jnp.bfloat16
LARGE = 60 * 1024 * 1024
SMALL = 20 * 1024 * 1024
PAD = 16


def spread(block, axes):
    copies = jnp.broadcast_to(block[None], (lax.axis_size(axes),) + block.shape)
    return lax.all_to_all(copies, axes, 0, 0)


def shift(block, axis, by):
    n = lax.axis_size(axis)
    return lax.ppermute(block, axis, [(i, (i + by) % n) for i in range(n)])


def head(inputs, sums, gain, bias, batch_total):
    mean = sums[0:1] / batch_total
    inv_std = lax.rsqrt(sums[1:2] / batch_total - mean * mean + EPSILON)
    normed = (inputs.astype(F32) - mean) * inv_std
    shifted = normed * gain + bias
    scale = lax.rsqrt(jnp.sum(shifted * shifted, 1, keepdims=True) + EPSILON)
    return normed, shifted * scale, scale, inv_std


VM = pl.BlockSpec(memory_space=pltpu.VMEM)
SM = pl.BlockSpec(memory_space=pltpu.SMEM)
HB = pl.BlockSpec(memory_space=pl.ANY)
HO = pl.BlockSpec(memory_space=pltpu.HBM)


def call(kernel, ins, outs, shapes, flops, size, exps=0, scratch=(), grant=LARGE):
    return pl.pallas_call(
        kernel,
        in_specs=ins,
        out_specs=outs,
        out_shape=shapes,
        scratch_shapes=list(scratch),
        compiler_params=pltpu.CompilerParams(vmem_limit_bytes=grant),
        cost_estimate=pl.CostEstimate(
            flops=flops, bytes_accessed=size, transcendentals=exps
        ),
    )


def hits(place, block, count, first):
    return place == lax.broadcasted_iota(jnp.int32, (block, count), 0) + first


def cosine_of(w_hat, unit, place, first):
    cosine = lax.dot_general(
        w_hat, unit, (((1,), (1,)), ((), ())), preferred_element_type=F32
    )
    return cosine, hits(place, w_hat.shape[0], unit.shape[0], first)


def grad_of(w_hat, unit, place, first, inverse):
    cosine, target = cosine_of(w_hat, unit, place, first)
    share = jnp.exp(LOGIT_SCALE * cosine) * inverse
    return jnp.where(target, share * SHRINK - 1.0, share).astype(BF16)


def blocks_of(w_own, w_other):
    block = w_own.shape[0] // 2
    for i in range(4):
        source = w_own if i < 2 else w_other
        yield source[(i % 2) * block : (i % 2 + 1) * block], i * block


def exp_kernel(batch, rows, sums, gain, bias, place, w_own, w_other, unit, stats):
    total = jnp.sum(sums[...], 0)
    units = head(rows[...], total, gain[...], bias[...], batch)[1].astype(BF16)
    unit[...] = units
    exps = hit = None
    for w_hat, first in blocks_of(w_own, w_other):
        cosine, target = cosine_of(w_hat, units, place[...], first)
        term = jnp.exp(LOGIT_SCALE * cosine)
        term = jnp.sum(jnp.where(target, term * SHRINK, term), 0, keepdims=True)
        other = jnp.sum(jnp.where(target, cosine, 0.0), 0, keepdims=True)
        exps = term if exps is None else exps + term
        hit = other if hit is None else hit + other
    hit = jnp.where(place[...] >= 0, LOGIT_SCALE * hit - LOGIT_SCALE * MARGIN, 0.0)
    both = jnp.concatenate([exps, hit], 0)
    for p in range(stats.shape[0]):
        stats[p] = both


def pull_kernel(
    batch, rows, sums, gain, bias, place, totals, unit, w_own, w_other, packed
):
    units = unit[...]
    inverse = 1.0 / jnp.sum(totals[...], 0)[0:1, : units.shape[0]]
    pull = None
    for w_hat, first in blocks_of(w_own, w_other):
        grad = grad_of(w_hat, units, place[...], first, inverse)
        term = lax.dot_general(
            grad, w_hat, (((0,), (0,)), ((), ())), preferred_element_type=F32
        )
        pull = term if pull is None else pull + term
    total = jnp.sum(sums[...], 0)
    normed, unit_f, scale, _ = head(rows[...], total, gain[...], bias[...], batch)
    radial = jnp.sum(unit_f * pull, 1, keepdims=True)
    shifts = (pull - unit_f * radial) * scale
    bias_part = jnp.sum(shifts, 0, keepdims=True)
    gain_part = jnp.sum(shifts * normed, 0, keepdims=True)
    tail = tail_of(bias_part, gain_part)
    parts = packed.shape[0]
    n = pull.shape[0] // parts
    for p in range(parts):
        packed[p, :n] = pull[p * n : (p + 1) * n].astype(BF16)
        packed[p, n:] = tail


def tail_of(bias_part, gain_part):
    pieces = split(bias_part, 3) + split(gain_part, 3)
    fill = jnp.zeros((PAD - 6, bias_part.shape[1]), F32)
    return jnp.concatenate(pieces + [fill], 0).astype(BF16)


def sums_of(tail):
    return jnp.concatenate(
        [jnp.sum(tail[k : k + 3], 0, keepdims=True) for k in (0, 3)], 0
    )


def split(value, count):
    pieces = []
    for _ in range(count):
        piece = value.astype(BF16).astype(F32)
        value = value - piece
        pieces.append(piece)
    return pieces


def total_kernel(lines, at, arrived, out):
    group = arrived.shape[2]
    n = group // lines
    place = at[0] * n if n % 128 else pl.multiple_of(at[0] * n, 128)
    own = other = hit = 0.0
    for x in range(lines):
        own = own + arrived[2 * x + at[1], 0:1]
        other = other + arrived[2 * x + 1 - at[1], 0:1]
        hit = hit + arrived[2 * x + at[1], 1:2, pl.ds(place, n)]
    both = jnp.concatenate(
        [
            jnp.concatenate([own, hit], 1),
            jnp.concatenate([other, jnp.zeros_like(hit)], 1),
        ],
        0,
    )
    for p in range(out.shape[0]):
        out[p] = both


def mid_kernel(rows_dev, arrived, packed):
    lines, _, lane = packed.shape
    total = jnp.sum(arrived[...].astype(F32), 0)
    width = total.shape[1]
    cuts = [slice(k, k + lane) for k in range(0, width, lane)]
    ends = sums_of(total[lines * rows_dev :])
    rows = split(ends[0:1], 2) + split(ends[1:2], 2)
    tail = [row[:, cut] for row in rows for cut in cuts]
    for p in range(lines):
        piece = total[p * rows_dev : (p + 1) * rows_dev]
        packed[p] = jnp.concatenate([piece[:, c] for c in cuts] + tail, 0).astype(BF16)


def home_kernel(rows_dev, arrived, grad, ends):
    total = jnp.sum(arrived[...].astype(F32), 0)
    lane = total.shape[1]
    n = grad.shape[1] // lane
    grad[...] = jnp.concatenate(
        [total[k * rows_dev : (k + 1) * rows_dev] for k in range(n)], 1
    )
    tail = total[n * rows_dev :]
    rows = []
    for v in range(2):
        both = tail[2 * v * n : (2 * v + 1) * n] + tail[(2 * v + 1) * n : (2 * v + 2) * n]
        rows.append(jnp.concatenate([both[k : k + 1] for k in range(n)], 1))
    both = jnp.concatenate(rows, 0)
    for p in range(ends.shape[0]):
        ends[p] = both


def raw_kernel(parts, at, place, place_2, totals, unit, unit_2, w_own, _, *refs):
    outs, (mine, sent, sems) = refs[:parts], refs[parts:]
    block = mine.shape[0]
    copies = []
    group = unit.shape[0]
    inverse = 1.0 / jnp.sum(totals[...], 0)[:, :group]
    for i in range(parts):
        first = pl.multiple_of(lax.rem(at[0] + i, parts) * block, 64)
        w_hat = w_own[pl.ds(first, block)]
        raw = None
        for units, places, row in ((unit, place, 0), (unit_2, place_2, 1)):
            grad = grad_of(
                w_hat, units[...], places[...], first, inverse[row : row + 1]
            )
            term = jnp.dot(grad, units[...], preferred_element_type=F32)
            raw = term if raw is None else raw + term
        if i == 0:
            mine[...] = raw
            source = mine
        else:
            sent[i - 1] = raw.astype(BF16)
            source = sent.at[i - 1]
        copies.append(pltpu.make_async_copy(source, outs[i], sems.at[i]))
        copies[-1].start()
    for copy in copies:
        copy.wait()


def project_kernel(parts, at, picked, *refs):
    found, (out, picks_ref, sem) = refs[:parts], refs[parts:]
    block = out.shape[0]
    rows = pl.ds(pl.multiple_of(at[0] * block, 64), block)
    copy = pltpu.make_async_copy(picked.at[rows], picks_ref, sem)
    copy.start()
    raw = found[0][...]
    for piece in found[1:]:
        raw = raw + piece[...].astype(F32)
    copy.wait()
    picks = picks_ref[...].astype(F32)
    inv_norm = lax.rsqrt(jnp.sum(picks * picks, 1, keepdims=True) + EPSILON)
    w_unit = picks * inv_norm
    along = jnp.sum(w_unit * raw, 1, keepdims=True)
    out[...] = ((raw - w_unit * along) * inv_norm).astype(BF16)


def own_kernel(batch, at, inputs, sums, gain, bias, grad_unit, totals, terms, loss):
    n = inputs.shape[0]
    total = jnp.sum(sums[...], 0)
    normed, unit_f, scale, inv_std = head(
        inputs[...], total, gain[...], bias[...], batch
    )
    pull = grad_unit[...]
    radial = jnp.sum(unit_f * pull, 1, keepdims=True)
    shifts = (pull - unit_f * radial) * scale
    share = inv_std * gain[...]
    terms[0:n] = shifts * share
    terms[n : 2 * n] = normed * (share / batch)
    terms[2 * n : 3 * n] = jnp.broadcast_to(share / batch, (n, share.shape[1]))
    own = jnp.sum(totals[...], 0)[0:1]
    shape = (n, own.shape[1])
    ahead = lax.broadcasted_iota(jnp.int32, shape, 1) - lax.broadcasted_iota(
        jnp.int32, shape, 0
    )
    found = [
        jnp.sum(jnp.where(ahead == at[k], own, 0.0), 1, keepdims=True) for k in (0, 1)
    ]
    values = jnp.log(found[0]) - found[1]
    square = (n, n)
    same = lax.broadcasted_iota(jnp.int32, square, 0) == lax.broadcasted_iota(
        jnp.int32, square, 1
    )
    loss[...] = jnp.sum(jnp.where(same, values, 0.0), 0, keepdims=True)


def final_kernel(terms, ends, emb, gain_grad, bias_grad):
    n = emb.shape[0]
    both = jnp.sum(ends[...], 0)
    bias_grad[...] = both[0:1]
    gain_grad[...] = both[1:2]
    emb[...] = (
        terms[0:n] - terms[2 * n : 3 * n] * both[0:1] - terms[n : 2 * n] * both[1:2]
    )


def body(embeddings, bn_gain, bn_bias, centres, sample_rows, label_shard, label_slot):
    nx, nz, nc, nr = (lax.axis_size(a) for a in ("x", "z", "core", "rep"))
    ix, iz, ic, ir = (lax.axis_index(a) for a in ("x", "z", "core", "rep"))
    rows_dev, width = embeddings.shape
    slots = sample_rows.shape[1]
    batch = rows_dev * nx * nz * nc * nr
    line_rows = nz * rows_dev
    group = nx * line_rows
    held = nc * slots
    quarter = slots // nr
    at = ir.astype(jnp.int32).reshape(1)
    gain, bias = bn_gain[None], bn_bias[None]

    picked = centres.at[sample_rows[0]].get(mode="promise_in_bounds")
    picks = picked.astype(F32)
    inv_norm = lax.rsqrt(jnp.sum(picks * picks, 1, keepdims=True) + EPSILON)
    w_own = (picks * inv_norm).astype(BF16)

    line = spread(embeddings, "z").reshape(line_rows, width)
    line, w_own = lax.optimization_barrier((line, w_own))
    rows = spread(line, "x").reshape(group, width)
    rows_f = rows.astype(F32)
    sums = spread(
        jnp.stack([jnp.sum(rows_f, 0), jnp.sum(rows_f * rows_f, 0)]), ("core", "rep")
    )
    w_other = shift(w_own, "core", 1)

    def of_core(labels, core):
        lines = labels.reshape(nx * nz, nc, rows_dev)
        return lax.dynamic_index_in_dim(lines, core, 1).reshape(1, group)

    owner, slot = of_core(label_shard, ic), of_core(label_slot, ic)
    chip = (ix * nz + iz) * nc
    place = jnp.where(
        owner == chip + ic, slot, jnp.where(owner == chip + 1 - ic, slot + slots, -1)
    )
    place_2 = jnp.where(
        of_core(label_shard, 1 - ic) == chip + ic, of_core(label_slot, 1 - ic), -1
    )

    unit, stats = call(
        lambda *refs: exp_kernel(batch, *refs),
        [VM] * 7,
        [VM] * 2,
        [
            jax.ShapeDtypeStruct((group, width), BF16),
            jax.ShapeDtypeStruct((nx * nc, 2, group), F32),
        ],
        2 * held * group * width,
        2 * held * width,
        held * group,
    )(rows, sums, gain, bias, place, w_own, w_other)
    unit_2 = shift(unit, "core", 1)

    stats = lax.all_to_all(stats, ("x", "core"), 0, 0)
    totals = call(
        lambda *refs: total_kernel(nx, *refs),
        [SM, VM],
        VM,
        jax.ShapeDtypeStruct((nz, nc, group + line_rows), F32),
        16 * group,
        64 * group,
        grant=SMALL,
    )(jnp.stack([ix, ic]).astype(jnp.int32), stats)
    totals, unit_2, place_2 = lax.optimization_barrier((totals, unit_2, place_2))
    totals = lax.all_to_all(totals, "z", 0, 0)

    pull = call(
        lambda *refs: pull_kernel(batch, *refs),
        [VM] * 9,
        VM,
        jax.ShapeDtypeStruct((nx, line_rows + PAD, width), BF16),
        4 * held * group * width,
        2 * held * width,
        held * group,
    )(rows, sums, gain, bias, place, totals, unit, w_own, w_other)

    piece = jax.ShapeDtypeStruct((quarter, width), BF16)
    mine, *sent = call(
        lambda *refs: raw_kernel(nr, *refs),
        [SM] + [VM] * 6 + [HB],
        [HO] * nr,
        [jax.ShapeDtypeStruct((quarter, width), F32)] + [piece] * (nr - 1),
        4 * held * group * width,
        2 * held * width,
        held * group,
        [
            pltpu.VMEM((quarter, width), F32),
            pltpu.VMEM((nr - 1, quarter, width), BF16),
            pltpu.SemaphoreType.DMA((nr,)),
        ],
    )(at, place, place_2, totals, unit, unit_2, w_own, pull)
    came = [shift(sent[by - 1], "rep", by) for by in range(1, nr)]
    grad = call(
        lambda *refs: project_kernel(nr, *refs),
        [SM, HB] + [VM] * nr,
        VM,
        piece,
        20 * quarter * width,
        14 * quarter * width,
        0,
        [pltpu.VMEM((quarter, width), BF16), pltpu.SemaphoreType.DMA],
        grant=SMALL,
    )(at, picked, mine, *came)
    pull = lax.all_to_all(pull, "x", 0, 0)
    pull, mine = lax.optimization_barrier((pull, mine))
    lanes = min(width, 128)
    tall = (rows_dev + 4) * (width // lanes)
    pull = call(
        lambda *refs: mid_kernel(rows_dev, *refs),
        [VM],
        VM,
        jax.ShapeDtypeStruct((nz, tall, lanes), BF16),
        nx * line_rows * width,
        2 * nx * line_rows * width,
        grant=SMALL,
    )(pull)
    pull = lax.all_to_all(pull, "z", 0, 0)
    grad_unit, ends = call(
        lambda *refs: home_kernel(rows_dev, *refs),
        [VM],
        [VM] * 2,
        [
            jax.ShapeDtypeStruct((rows_dev, width), F32),
            jax.ShapeDtypeStruct((nc * nr, 2, width), F32),
        ],
        nz * tall * lanes,
        2 * nz * tall * lanes,
        grant=SMALL,
    )(pull)
    ends = lax.all_to_all(ends, ("core", "rep"), 0, 0)

    own = jnp.stack([(ix * nz + iz) * rows_dev, group + iz * rows_dev])
    terms, row_loss = call(
        lambda *refs: own_kernel(batch, *refs),
        [SM] + [VM] * 6,
        [VM] * 2,
        [
            jax.ShapeDtypeStruct((3 * rows_dev, width), F32),
            jax.ShapeDtypeStruct((1, rows_dev), F32),
        ],
        40 * rows_dev * width,
        40 * rows_dev * width,
        grant=SMALL,
    )(own.astype(jnp.int32), embeddings, sums, gain, bias, grad_unit, totals)
    emb_grad, gain_grad, bias_grad = call(
        final_kernel,
        [VM] * 2,
        [VM] * 3,
        [
            jax.ShapeDtypeStruct((rows_dev, width), F32),
            jax.ShapeDtypeStruct((1, width), F32),
            jax.ShapeDtypeStruct((1, width), F32),
        ],
        8 * rows_dev * width,
        16 * rows_dev * width,
        grant=SMALL,
    )(terms, ends)
    centre_grad = lax.all_gather(grad, "rep", axis=0, tiled=True)
    return (row_loss[0], emb_grad, centre_grad, gain_grad[0], bias_grad[0])


def solution(mesh):
    shards, replicas = mesh.devices.shape
    split = (4, shards // 8, 2, replicas)
    fine = Mesh(mesh.devices.reshape(split), ("x", "z", "core", "rep"))
    cen = ("x", "z", "core")
    every = cen + ("rep",)
    return jax.shard_map(
        body,
        mesh=fine,
        in_specs=(
            P(every, None),
            P(),
            P(),
            P(cen, None),
            P(cen, None),
            P(None, "rep", None),
            P(None, "rep", None),
        ),
        out_specs=(P(every), P(every, None), P(cen, None), P(), P()),
        check_vma=False,
    )
```

```python
import math

import jax
import jax.numpy as jnp
from jax import lax
from jax.experimental import pallas as pl
from jax.experimental.pallas import tpu as pltpu
from jax.sharding import Mesh, PartitionSpec as P

LOGIT_SCALE = 64.0
MARGIN = 0.4
EPSILON = 1e-05
SHRINK = math.exp(-LOGIT_SCALE * MARGIN)
F32 = jnp.float32
BF16 = jnp.bfloat16
LARGE = 60 * 1024 * 1024
SMALL = 20 * 1024 * 1024
PAD = 16


def spread(block, axes):
    copies = jnp.broadcast_to(block[None], (lax.axis_size(axes),) + block.shape)
    return lax.all_to_all(copies, axes, 0, 0)


def shift(block, axis, by):
    n = lax.axis_size(axis)
    return lax.ppermute(block, axis, [(i, (i + by) % n) for i in range(n)])


def head(inputs, sums, gain, bias, batch_total):
    mean = sums[0:1] / batch_total
    inv_std = lax.rsqrt(sums[1:2] / batch_total - mean * mean + EPSILON)
    normed = (inputs.astype(F32) - mean) * inv_std
    shifted = normed * gain + bias
    scale = lax.rsqrt(jnp.sum(shifted * shifted, 1, keepdims=True) + EPSILON)
    return normed, shifted * scale, scale, inv_std


VM = pl.BlockSpec(memory_space=pltpu.VMEM)
SM = pl.BlockSpec(memory_space=pltpu.SMEM)
HB = pl.BlockSpec(memory_space=pl.ANY)
HO = pl.BlockSpec(memory_space=pltpu.HBM)


def call(kernel, ins, outs, shapes, flops, size, exps=0, scratch=(), grant=LARGE):
    return pl.pallas_call(
        kernel,
        in_specs=ins,
        out_specs=outs,
        out_shape=shapes,
        scratch_shapes=list(scratch),
        compiler_params=pltpu.CompilerParams(vmem_limit_bytes=grant),
        cost_estimate=pl.CostEstimate(
            flops=flops, bytes_accessed=size, transcendentals=exps
        ),
    )


def hits(place, block, count, first):
    return place == lax.broadcasted_iota(jnp.int32, (block, count), 0) + first


def cosine_of(w_hat, unit, place, first):
    cosine = lax.dot_general(
        w_hat, unit, (((1,), (1,)), ((), ())), preferred_element_type=F32
    )
    return cosine, hits(place, w_hat.shape[0], unit.shape[0], first)


def grad_of(w_hat, unit, place, first, inverse):
    cosine, target = cosine_of(w_hat, unit, place, first)
    share = jnp.exp(LOGIT_SCALE * cosine) * inverse
    return jnp.where(target, share * SHRINK - 1.0, share).astype(BF16)


def blocks_of(w_own, w_other):
    block = w_own.shape[0] // 2
    for i in range(4):
        source = w_own if i < 2 else w_other
        yield source[(i % 2) * block : (i % 2 + 1) * block], i * block


def exp_kernel(batch, rows, sums, gain, bias, place, w_own, w_other, unit, stats):
    total = jnp.sum(sums[...], 0)
    units = head(rows[...], total, gain[...], bias[...], batch)[1].astype(BF16)
    unit[...] = units
    exps = hit = None
    for w_hat, first in blocks_of(w_own, w_other):
        cosine, target = cosine_of(w_hat, units, place[...], first)
        term = jnp.exp(LOGIT_SCALE * cosine)
        term = jnp.sum(jnp.where(target, term * SHRINK, term), 0, keepdims=True)
        other = jnp.sum(jnp.where(target, cosine, 0.0), 0, keepdims=True)
        exps = term if exps is None else exps + term
        hit = other if hit is None else hit + other
    hit = jnp.where(place[...] >= 0, LOGIT_SCALE * hit - LOGIT_SCALE * MARGIN, 0.0)
    both = jnp.concatenate([exps, hit], 0)
    for p in range(stats.shape[0]):
        stats[p] = both


def pull_kernel(
    batch, rows, sums, gain, bias, place, totals, unit, w_own, w_other, packed
):
    units = unit[...]
    inverse = 1.0 / jnp.sum(totals[...], 0)[0:1, : units.shape[0]]
    pull = None
    for w_hat, first in blocks_of(w_own, w_other):
        grad = grad_of(w_hat, units, place[...], first, inverse)
        term = lax.dot_general(
            grad, w_hat, (((0,), (0,)), ((), ())), preferred_element_type=F32
        )
        pull = term if pull is None else pull + term
    total = jnp.sum(sums[...], 0)
    normed, unit_f, scale, _ = head(rows[...], total, gain[...], bias[...], batch)
    radial = jnp.sum(unit_f * pull, 1, keepdims=True)
    shifts = (pull - unit_f * radial) * scale
    bias_part = jnp.sum(shifts, 0, keepdims=True)
    gain_part = jnp.sum(shifts * normed, 0, keepdims=True)
    tail = tail_of(bias_part, gain_part)
    parts = packed.shape[0]
    n = pull.shape[0] // parts
    for p in range(parts):
        packed[p, :n] = pull[p * n : (p + 1) * n].astype(BF16)
        packed[p, n:] = tail


def tail_of(bias_part, gain_part):
    pieces = split(bias_part, 3) + split(gain_part, 3)
    fill = jnp.zeros((PAD - 6, bias_part.shape[1]), F32)
    return jnp.concatenate(pieces + [fill], 0).astype(BF16)


def sums_of(tail):
    return jnp.concatenate(
        [jnp.sum(tail[k : k + 3], 0, keepdims=True) for k in (0, 3)], 0
    )


def split(value, count):
    pieces = []
    for _ in range(count):
        piece = value.astype(BF16).astype(F32)
        value = value - piece
        pieces.append(piece)
    return pieces


def total_kernel(lines, at, arrived, out):
    group = arrived.shape[2]
    n = group // lines
    place = at[0] * n if n % 128 else pl.multiple_of(at[0] * n, 128)
    own = other = hit = 0.0
    for x in range(lines):
        own = own + arrived[2 * x + at[1], 0:1]
        other = other + arrived[2 * x + 1 - at[1], 0:1]
        hit = hit + arrived[2 * x + at[1], 1:2, pl.ds(place, n)]
    both = jnp.concatenate(
        [
            jnp.concatenate([own, hit], 1),
            jnp.concatenate([other, jnp.zeros_like(hit)], 1),
        ],
        0,
    )
    for p in range(out.shape[0]):
        out[p] = both


def mid_kernel(rows_dev, arrived, packed):
    lines, _, lane = packed.shape
    total = jnp.sum(arrived[...].astype(F32), 0)
    width = total.shape[1]
    cuts = [slice(k, k + lane) for k in range(0, width, lane)]
    ends = sums_of(total[lines * rows_dev :])
    rows = split(ends[0:1], 2) + split(ends[1:2], 2)
    tail = [row[:, cut] for row in rows for cut in cuts]
    for p in range(lines):
        piece = total[p * rows_dev : (p + 1) * rows_dev]
        packed[p] = jnp.concatenate([piece[:, c] for c in cuts] + tail, 0).astype(BF16)


def home_kernel(rows_dev, arrived, grad, ends):
    total = jnp.sum(arrived[...].astype(F32), 0)
    lane = total.shape[1]
    n = grad.shape[1] // lane
    grad[...] = jnp.concatenate(
        [total[k * rows_dev : (k + 1) * rows_dev] for k in range(n)], 1
    )
    tail = total[n * rows_dev :]
    rows = []
    for v in range(2):
        both = tail[2 * v * n : (2 * v + 1) * n] + tail[(2 * v + 1) * n : (2 * v + 2) * n]
        rows.append(jnp.concatenate([both[k : k + 1] for k in range(n)], 1))
    both = jnp.concatenate(rows, 0)
    for p in range(ends.shape[0]):
        ends[p] = both


def raw_kernel(parts, at, place, place_2, totals, unit, unit_2, w_own, _, *refs):
    outs, (mine, sent, sems) = refs[:parts], refs[parts:]
    block = mine.shape[0]
    copies = []
    group = unit.shape[0]
    inverse = 1.0 / jnp.sum(totals[...], 0)[:, :group]
    for i in range(parts):
        first = pl.multiple_of(lax.rem(at[0] + i, parts) * block, 64)
        w_hat = w_own[pl.ds(first, block)]
        raw = None
        for units, places, row in ((unit, place, 0), (unit_2, place_2, 1)):
            grad = grad_of(
                w_hat, units[...], places[...], first, inverse[row : row + 1]
            )
            term = jnp.dot(grad, units[...], preferred_element_type=F32)
            raw = term if raw is None else raw + term
        if i == 0:
            mine[...] = raw
            source = mine
        else:
            sent[i - 1] = raw.astype(BF16)
            source = sent.at[i - 1]
        copies.append(pltpu.make_async_copy(source, outs[i], sems.at[i]))
        copies[-1].start()
    for copy in copies:
        copy.wait()


def project_kernel(parts, at, picked, *refs):
    found, (out, picks_ref, raw_ref, sems) = refs[:parts], refs[parts:]
    block = out.shape[0]
    rows = pl.ds(pl.multiple_of(at[0] * block, 64), block)
    copy = pltpu.make_async_copy(picked.at[rows], picks_ref, sems.at[0])
    copy.start()
    copy_2 = pltpu.make_async_copy(found[0], raw_ref, sems.at[1])
    copy_2.start()
    raw = found[1][...].astype(F32)
    for piece in found[2:]:
        raw = raw + piece[...].astype(F32)
    copy_2.wait()
    raw = raw_ref[...] + raw
    copy.wait()
    picks = picks_ref[...].astype(F32)
    inv_norm = lax.rsqrt(jnp.sum(picks * picks, 1, keepdims=True) + EPSILON)
    w_unit = picks * inv_norm
    along = jnp.sum(w_unit * raw, 1, keepdims=True)
    out[...] = ((raw - w_unit * along) * inv_norm).astype(BF16)


def own_kernel(batch, at, inputs, sums, gain, bias, grad_unit, totals, terms, loss):
    n = inputs.shape[0]
    total = jnp.sum(sums[...], 0)
    normed, unit_f, scale, inv_std = head(
        inputs[...], total, gain[...], bias[...], batch
    )
    pull = grad_unit[...]
    radial = jnp.sum(unit_f * pull, 1, keepdims=True)
    shifts = (pull - unit_f * radial) * scale
    share = inv_std * gain[...]
    terms[0:n] = shifts * share
    terms[n : 2 * n] = normed * (share / batch)
    terms[2 * n : 3 * n] = jnp.broadcast_to(share / batch, (n, share.shape[1]))
    own = jnp.sum(totals[...], 0)[0:1]
    shape = (n, own.shape[1])
    ahead = lax.broadcasted_iota(jnp.int32, shape, 1) - lax.broadcasted_iota(
        jnp.int32, shape, 0
    )
    found = [
        jnp.sum(jnp.where(ahead == at[k], own, 0.0), 1, keepdims=True) for k in (0, 1)
    ]
    values = jnp.log(found[0]) - found[1]
    square = (n, n)
    same = lax.broadcasted_iota(jnp.int32, square, 0) == lax.broadcasted_iota(
        jnp.int32, square, 1
    )
    loss[...] = jnp.sum(jnp.where(same, values, 0.0), 0, keepdims=True)


def final_kernel(parts, at, terms, ends, *refs):
    found, (emb, grad, gain_grad, bias_grad) = refs[:parts], refs[parts:]
    block = found[0].shape[0]
    n = emb.shape[0]
    both = jnp.sum(ends[...], 0)
    bias_grad[...] = both[0:1]
    gain_grad[...] = both[1:2]
    emb[...] = (
        terms[0:n] - terms[2 * n : 3 * n] * both[0:1] - terms[n : 2 * n] * both[1:2]
    )
    for by, piece in enumerate(found):
        where = lax.rem(at[0] - by + parts, parts) * block
        grad[pl.ds(pl.multiple_of(where, 64), block)] = piece[...]


def body(embeddings, bn_gain, bn_bias, centres, sample_rows, label_shard, label_slot):
    nx, nz, nc, nr = (lax.axis_size(a) for a in ("x", "z", "core", "rep"))
    ix, iz, ic, ir = (lax.axis_index(a) for a in ("x", "z", "core", "rep"))
    rows_dev, width = embeddings.shape
    slots = sample_rows.shape[1]
    batch = rows_dev * nx * nz * nc * nr
    line_rows = nz * rows_dev
    group = nx * line_rows
    held = nc * slots
    quarter = slots // nr
    at = ir.astype(jnp.int32).reshape(1)
    gain, bias = bn_gain[None], bn_bias[None]

    picked = centres.at[sample_rows[0]].get(mode="promise_in_bounds")
    picks = picked.astype(F32)
    inv_norm = lax.rsqrt(jnp.sum(picks * picks, 1, keepdims=True) + EPSILON)
    w_own = (picks * inv_norm).astype(BF16)

    line = spread(embeddings, "z").reshape(line_rows, width)
    line, w_own = lax.optimization_barrier((line, w_own))
    rows = spread(line, "x").reshape(group, width)
    rows_f = rows.astype(F32)
    sums = spread(
        jnp.stack([jnp.sum(rows_f, 0), jnp.sum(rows_f * rows_f, 0)]), ("core", "rep")
    )
    w_other = shift(w_own, "core", 1)

    def of_core(labels, core):
        lines = labels.reshape(nx * nz, nc, rows_dev)
        return lax.dynamic_index_in_dim(lines, core, 1).reshape(1, group)

    owner, slot = of_core(label_shard, ic), of_core(label_slot, ic)
    chip = (ix * nz + iz) * nc
    place = jnp.where(
        owner == chip + ic, slot, jnp.where(owner == chip + 1 - ic, slot + slots, -1)
    )
    place_2 = jnp.where(
        of_core(label_shard, 1 - ic) == chip + ic, of_core(label_slot, 1 - ic), -1
    )

    unit, stats = call(
        lambda *refs: exp_kernel(batch, *refs),
        [VM] * 7,
        [VM] * 2,
        [
            jax.ShapeDtypeStruct((group, width), BF16),
            jax.ShapeDtypeStruct((nx * nc, 2, group), F32),
        ],
        2 * held * group * width,
        2 * held * width,
        held * group,
    )(rows, sums, gain, bias, place, w_own, w_other)
    unit_2 = shift(unit, "core", 1)

    stats = lax.all_to_all(stats, ("x", "core"), 0, 0)
    totals = call(
        lambda *refs: total_kernel(nx, *refs),
        [SM, VM],
        VM,
        jax.ShapeDtypeStruct((nz, nc, group + line_rows), F32),
        16 * group,
        64 * group,
        grant=SMALL,
    )(jnp.stack([ix, ic]).astype(jnp.int32), stats)
    totals, unit_2, place_2 = lax.optimization_barrier((totals, unit_2, place_2))
    totals = lax.all_to_all(totals, "z", 0, 0)

    pull = call(
        lambda *refs: pull_kernel(batch, *refs),
        [VM] * 9,
        VM,
        jax.ShapeDtypeStruct((nx, line_rows + PAD, width), BF16),
        4 * held * group * width,
        2 * held * width,
        held * group,
    )(rows, sums, gain, bias, place, totals, unit, w_own, w_other)

    piece = jax.ShapeDtypeStruct((quarter, width), BF16)
    mine, *sent = call(
        lambda *refs: raw_kernel(nr, *refs),
        [SM] + [VM] * 6 + [HB],
        [HO] * nr,
        [jax.ShapeDtypeStruct((quarter, width), F32)] + [piece] * (nr - 1),
        4 * held * group * width,
        2 * held * width,
        held * group,
        [
            pltpu.VMEM((quarter, width), F32),
            pltpu.VMEM((nr - 1, quarter, width), BF16),
            pltpu.SemaphoreType.DMA((nr,)),
        ],
    )(at, place, place_2, totals, unit, unit_2, w_own, pull)
    came = [shift(sent[by - 1], "rep", by) for by in range(1, nr)]
    grad = call(
        lambda *refs: project_kernel(nr, *refs),
        [SM, HB, HB] + [VM] * (nr - 1),
        VM,
        piece,
        20 * quarter * width,
        14 * quarter * width,
        0,
        [
            pltpu.VMEM((quarter, width), BF16),
            pltpu.VMEM((quarter, width), F32),
            pltpu.SemaphoreType.DMA((2,)),
        ],
        grant=SMALL,
    )(at, picked, mine, *came)
    pull = lax.all_to_all(pull, "x", 0, 0)
    pull, mine = lax.optimization_barrier((pull, mine))
    lanes = min(width, 128)
    tall = (rows_dev + 4) * (width // lanes)
    pull = call(
        lambda *refs: mid_kernel(rows_dev, *refs),
        [VM],
        VM,
        jax.ShapeDtypeStruct((nz, tall, lanes), BF16),
        nx * line_rows * width,
        2 * nx * line_rows * width,
        grant=SMALL,
    )(pull)
    pull = lax.all_to_all(pull, "z", 0, 0)
    grad_unit, ends = call(
        lambda *refs: home_kernel(rows_dev, *refs),
        [VM],
        [VM] * 2,
        [
            jax.ShapeDtypeStruct((rows_dev, width), F32),
            jax.ShapeDtypeStruct((nc * nr, 2, width), F32),
        ],
        nz * tall * lanes,
        2 * nz * tall * lanes,
        grant=SMALL,
    )(pull)
    ends = lax.all_to_all(ends, ("core", "rep"), 0, 0)

    own = jnp.stack([(ix * nz + iz) * rows_dev, group + iz * rows_dev])
    terms, row_loss = call(
        lambda *refs: own_kernel(batch, *refs),
        [SM] + [VM] * 6,
        [VM] * 2,
        [
            jax.ShapeDtypeStruct((3 * rows_dev, width), F32),
            jax.ShapeDtypeStruct((1, rows_dev), F32),
        ],
        40 * rows_dev * width,
        40 * rows_dev * width,
        grant=SMALL,
    )(own.astype(jnp.int32), embeddings, sums, gain, bias, grad_unit, totals)
    emb_grad, centre_grad, gain_grad, bias_grad = call(
        lambda *refs: final_kernel(nr, *refs),
        [SM] + [VM] * (2 + nr),
        [VM] * 4,
        [
            jax.ShapeDtypeStruct((rows_dev, width), F32),
            jax.ShapeDtypeStruct((slots, width), BF16),
            jax.ShapeDtypeStruct((1, width), F32),
            jax.ShapeDtypeStruct((1, width), F32),
        ],
        slots * width,
        4 * slots * width,
        grant=SMALL,
    )(at, terms, ends, grad, *[shift(grad, "rep", by) for by in range(1, nr)])
    return (row_loss[0], emb_grad, centre_grad, gain_grad[0], bias_grad[0])


def solution(mesh):
    shards, replicas = mesh.devices.shape
    split = (4, shards // 8, 2, replicas)
    fine = Mesh(mesh.devices.reshape(split), ("x", "z", "core", "rep"))
    cen = ("x", "z", "core")
    every = cen + ("rep",)
    return jax.shard_map(
        body,
        mesh=fine,
        in_specs=(
            P(every, None),
            P(),
            P(),
            P(cen, None),
            P(cen, None),
            P(None, "rep", None),
            P(None, "rep", None),
        ),
        out_specs=(P(every), P(every, None), P(cen, None), P(), P()),
        check_vma=False,
    )
```

```python
import math

import jax
import jax.numpy as jnp
from jax import lax
from jax.experimental import pallas as pl
from jax.experimental.pallas import tpu as pltpu
from jax.sharding import Mesh, PartitionSpec as P

LOGIT_SCALE = 64.0
MARGIN = 0.4
EPSILON = 1e-05
SHRINK = math.exp(-LOGIT_SCALE * MARGIN)
F32 = jnp.float32
BF16 = jnp.bfloat16
LARGE = 60 * 1024 * 1024
SMALL = 20 * 1024 * 1024
PAD = 16


def spread(block, axes):
    copies = jnp.broadcast_to(block[None], (lax.axis_size(axes),) + block.shape)
    return lax.all_to_all(copies, axes, 0, 0)


def shift(block, axis, by):
    n = lax.axis_size(axis)
    return lax.ppermute(block, axis, [(i, (i + by) % n) for i in range(n)])


def head(inputs, sums, gain, bias, batch_total):
    mean = sums[0:1] / batch_total
    inv_std = lax.rsqrt(sums[1:2] / batch_total - mean * mean + EPSILON)
    normed = (inputs.astype(F32) - mean) * inv_std
    shifted = normed * gain + bias
    scale = lax.rsqrt(jnp.sum(shifted * shifted, 1, keepdims=True) + EPSILON)
    return normed, shifted * scale, scale, inv_std


VM = pl.BlockSpec(memory_space=pltpu.VMEM)
SM = pl.BlockSpec(memory_space=pltpu.SMEM)
HB = pl.BlockSpec(memory_space=pl.ANY)
HO = pl.BlockSpec(memory_space=pltpu.HBM)


def call(kernel, ins, outs, shapes, flops, size, exps=0, scratch=(), grant=LARGE):
    return pl.pallas_call(
        kernel,
        in_specs=ins,
        out_specs=outs,
        out_shape=shapes,
        scratch_shapes=list(scratch),
        compiler_params=pltpu.CompilerParams(vmem_limit_bytes=grant),
        cost_estimate=pl.CostEstimate(
            flops=flops, bytes_accessed=size, transcendentals=exps
        ),
    )


def hits(place, block, count, first):
    return place == lax.broadcasted_iota(jnp.int32, (block, count), 0) + first


def cosine_of(w_hat, unit, place, first):
    cosine = lax.dot_general(
        w_hat, unit, (((1,), (1,)), ((), ())), preferred_element_type=F32
    )
    return cosine, hits(place, w_hat.shape[0], unit.shape[0], first)


def grad_of(w_hat, unit, place, first, inverse):
    cosine, target = cosine_of(w_hat, unit, place, first)
    share = jnp.exp(LOGIT_SCALE * cosine) * inverse
    return jnp.where(target, share * SHRINK - 1.0, share).astype(BF16)


def blocks_of(w_own, w_other):
    block = w_own.shape[0] // 2
    for i in range(4):
        source = w_own if i < 2 else w_other
        yield source[(i % 2) * block : (i % 2 + 1) * block], i * block


def exp_kernel(batch, rows, sums, gain, bias, place, w_own, w_other, unit, stats):
    total = jnp.sum(sums[...], 0)
    units = head(rows[...], total, gain[...], bias[...], batch)[1].astype(BF16)
    unit[...] = units
    exps = hit = None
    for w_hat, first in blocks_of(w_own, w_other):
        cosine, target = cosine_of(w_hat, units, place[...], first)
        term = jnp.exp(LOGIT_SCALE * cosine)
        term = jnp.sum(jnp.where(target, term * SHRINK, term), 0, keepdims=True)
        other = jnp.sum(jnp.where(target, cosine, 0.0), 0, keepdims=True)
        exps = term if exps is None else exps + term
        hit = other if hit is None else hit + other
    hit = jnp.where(place[...] >= 0, LOGIT_SCALE * hit - LOGIT_SCALE * MARGIN, 0.0)
    both = jnp.concatenate([exps, hit], 0)
    for p in range(stats.shape[0]):
        stats[p] = both


def pull_kernel(
    batch, rows, sums, gain, bias, place, totals, unit, w_own, w_other, packed
):
    units = unit[...]
    inverse = 1.0 / jnp.sum(totals[...], 0)[0:1, : units.shape[0]]
    pull = None
    for w_hat, first in blocks_of(w_own, w_other):
        grad = grad_of(w_hat, units, place[...], first, inverse)
        term = lax.dot_general(
            grad, w_hat, (((0,), (0,)), ((), ())), preferred_element_type=F32
        )
        pull = term if pull is None else pull + term
    total = jnp.sum(sums[...], 0)
    normed, unit_f, scale, _ = head(rows[...], total, gain[...], bias[...], batch)
    radial = jnp.sum(unit_f * pull, 1, keepdims=True)
    shifts = (pull - unit_f * radial) * scale
    bias_part = jnp.sum(shifts, 0, keepdims=True)
    gain_part = jnp.sum(shifts * normed, 0, keepdims=True)
    tail = tail_of(bias_part, gain_part)
    parts = packed.shape[0]
    n = pull.shape[0] // parts
    for p in range(parts):
        packed[p, :n] = pull[p * n : (p + 1) * n].astype(BF16)
        packed[p, n:] = tail


def tail_of(bias_part, gain_part):
    pieces = split(bias_part, 3) + split(gain_part, 3)
    fill = jnp.zeros((PAD - 6, bias_part.shape[1]), F32)
    return jnp.concatenate(pieces + [fill], 0).astype(BF16)


def sums_of(tail):
    return jnp.concatenate(
        [jnp.sum(tail[k : k + 3], 0, keepdims=True) for k in (0, 3)], 0
    )


def split(value, count):
    pieces = []
    for _ in range(count):
        piece = value.astype(BF16).astype(F32)
        value = value - piece
        pieces.append(piece)
    return pieces


def total_kernel(lines, at, arrived, out):
    group = arrived.shape[2]
    n = group // lines
    place = at[0] * n if n % 128 else pl.multiple_of(at[0] * n, 128)
    own = other = hit = 0.0
    for x in range(lines):
        own = own + arrived[2 * x + at[1], 0:1]
        other = other + arrived[2 * x + 1 - at[1], 0:1]
        hit = hit + arrived[2 * x + at[1], 1:2, pl.ds(place, n)]
    both = jnp.concatenate(
        [
            jnp.concatenate([own, hit], 1),
            jnp.concatenate([other, jnp.zeros_like(hit)], 1),
        ],
        0,
    )
    for p in range(out.shape[0]):
        out[p] = both


def mid_kernel(rows_dev, arrived, packed):
    lines, _, lane = packed.shape
    total = jnp.sum(arrived[...].astype(F32), 0)
    width = total.shape[1]
    cuts = [slice(k, k + lane) for k in range(0, width, lane)]
    ends = sums_of(total[lines * rows_dev :])
    rows = split(ends[0:1], 2) + split(ends[1:2], 2)
    tail = [row[:, cut] for row in rows for cut in cuts]
    for p in range(lines):
        piece = total[p * rows_dev : (p + 1) * rows_dev]
        packed[p] = jnp.concatenate([piece[:, c] for c in cuts] + tail, 0).astype(BF16)


def home_kernel(rows_dev, arrived, grad, ends):
    total = jnp.sum(arrived[...].astype(F32), 0)
    lane = total.shape[1]
    n = grad.shape[1] // lane
    grad[...] = jnp.concatenate(
        [total[k * rows_dev : (k + 1) * rows_dev] for k in range(n)], 1
    )
    tail = total[n * rows_dev :]
    rows = []
    for v in range(2):
        both = tail[2 * v * n : (2 * v + 1) * n] + tail[(2 * v + 1) * n : (2 * v + 2) * n]
        rows.append(jnp.concatenate([both[k : k + 1] for k in range(n)], 1))
    both = jnp.concatenate(rows, 0)
    for p in range(ends.shape[0]):
        ends[p] = both


def raw_kernel(parts, at, place, place_2, totals, unit, unit_2, w_own, _, *refs):
    outs, (mine, sent, sems) = refs[:parts], refs[parts:]
    block = mine.shape[0]
    copies = []
    group = unit.shape[0]
    inverse = 1.0 / jnp.sum(totals[...], 0)[:, :group]
    for i in range(parts):
        first = pl.multiple_of(lax.rem(at[0] + i, parts) * block, 64)
        w_hat = w_own[pl.ds(first, block)]
        raw = None
        for units, places, row in ((unit, place, 0), (unit_2, place_2, 1)):
            grad = grad_of(
                w_hat, units[...], places[...], first, inverse[row : row + 1]
            )
            term = jnp.dot(grad, units[...], preferred_element_type=F32)
            raw = term if raw is None else raw + term
        if i == 0:
            mine[...] = raw
            source = mine
        else:
            sent[i - 1] = raw.astype(BF16)
            source = sent.at[i - 1]
        copies.append(pltpu.make_async_copy(source, outs[i], sems.at[i]))
        copies[-1].start()
    for copy in copies:
        copy.wait()


def project_kernel(parts, at, picked, *refs):
    found, (out, picks_ref, sem) = refs[:parts], refs[parts:]
    block = out.shape[0]
    rows = pl.ds(pl.multiple_of(at[0] * block, 64), block)
    copy = pltpu.make_async_copy(picked.at[rows], picks_ref, sem)
    copy.start()
    raw = found[0][...]
    for piece in found[1:]:
        raw = raw + piece[...].astype(F32)
    copy.wait()
    picks = picks_ref[...].astype(F32)
    inv_norm = lax.rsqrt(jnp.sum(picks * picks, 1, keepdims=True) + EPSILON)
    w_unit = picks * inv_norm
    along = jnp.sum(w_unit * raw, 1, keepdims=True)
    out[...] = ((raw - w_unit * along) * inv_norm).astype(BF16)


def own_kernel(batch, at, inputs, sums, gain, bias, grad_unit, totals, terms, loss):
    n = inputs.shape[0]
    total = jnp.sum(sums[...], 0)
    normed, unit_f, scale, inv_std = head(
        inputs[...], total, gain[...], bias[...], batch
    )
    pull = grad_unit[...]
    radial = jnp.sum(unit_f * pull, 1, keepdims=True)
    shifts = (pull - unit_f * radial) * scale
    share = inv_std * gain[...]
    terms[0:n] = shifts * share
    terms[n : 2 * n] = normed * (share / batch)
    terms[2 * n : 3 * n] = jnp.broadcast_to(share / batch, (n, share.shape[1]))
    own = jnp.sum(totals[...], 0)[0:1]
    shape = (n, own.shape[1])
    ahead = lax.broadcasted_iota(jnp.int32, shape, 1) - lax.broadcasted_iota(
        jnp.int32, shape, 0
    )
    found = [
        jnp.sum(jnp.where(ahead == at[k], own, 0.0), 1, keepdims=True) for k in (0, 1)
    ]
    values = jnp.log(found[0]) - found[1]
    square = (n, n)
    same = lax.broadcasted_iota(jnp.int32, square, 0) == lax.broadcasted_iota(
        jnp.int32, square, 1
    )
    loss[...] = jnp.sum(jnp.where(same, values, 0.0), 0, keepdims=True)


def final_kernel(parts, at, terms, ends, *refs):
    found, (emb, grad, gain_grad, bias_grad) = refs[:parts], refs[parts:]
    block = found[0].shape[0]
    n = emb.shape[0]
    both = jnp.sum(ends[...], 0)
    bias_grad[...] = both[0:1]
    gain_grad[...] = both[1:2]
    emb[...] = (
        terms[0:n] - terms[2 * n : 3 * n] * both[0:1] - terms[n : 2 * n] * both[1:2]
    )
    for by, piece in enumerate(found):
        where = lax.rem(at[0] - by + parts, parts) * block
        grad[pl.ds(pl.multiple_of(where, 64), block)] = piece[...]


def body(embeddings, bn_gain, bn_bias, centres, sample_rows, label_shard, label_slot):
    nx, nz, nc, nr = (lax.axis_size(a) for a in ("x", "z", "core", "rep"))
    ix, iz, ic, ir = (lax.axis_index(a) for a in ("x", "z", "core", "rep"))
    rows_dev, width = embeddings.shape
    slots = sample_rows.shape[1]
    batch = rows_dev * nx * nz * nc * nr
    line_rows = nz * rows_dev
    group = nx * line_rows
    held = nc * slots
    quarter = slots // nr
    at = ir.astype(jnp.int32).reshape(1)
    gain, bias = bn_gain[None], bn_bias[None]

    picked = centres.at[sample_rows[0]].get(mode="promise_in_bounds")
    picks = picked.astype(F32)
    inv_norm = lax.rsqrt(jnp.sum(picks * picks, 1, keepdims=True) + EPSILON)
    w_own = (picks * inv_norm).astype(BF16)

    line = spread(embeddings, "z").reshape(line_rows, width)
    line, w_own = lax.optimization_barrier((line, w_own))
    rows = spread(line, "x").reshape(group, width)
    rows_f = rows.astype(F32)
    sums = spread(
        jnp.stack([jnp.sum(rows_f, 0), jnp.sum(rows_f * rows_f, 0)]), ("core", "rep")
    )
    w_other = shift(w_own, "core", 1)

    def of_core(labels, core):
        lines = labels.reshape(nx * nz, nc, rows_dev)
        return lax.dynamic_index_in_dim(lines, core, 1).reshape(1, group)

    owner, slot = of_core(label_shard, ic), of_core(label_slot, ic)
    chip = (ix * nz + iz) * nc
    place = jnp.where(
        owner == chip + ic, slot, jnp.where(owner == chip + 1 - ic, slot + slots, -1)
    )
    place_2 = jnp.where(
        of_core(label_shard, 1 - ic) == chip + ic, of_core(label_slot, 1 - ic), -1
    )

    unit, stats = call(
        lambda *refs: exp_kernel(batch, *refs),
        [VM] * 7,
        [VM] * 2,
        [
            jax.ShapeDtypeStruct((group, width), BF16),
            jax.ShapeDtypeStruct((nx * nc, 2, group), F32),
        ],
        2 * held * group * width,
        2 * held * width,
        held * group,
    )(rows, sums, gain, bias, place, w_own, w_other)
    unit_2 = shift(unit, "core", 1)

    stats = lax.all_to_all(stats, ("x", "core"), 0, 0)
    totals = call(
        lambda *refs: total_kernel(nx, *refs),
        [SM, VM],
        VM,
        jax.ShapeDtypeStruct((nz, nc, group + line_rows), F32),
        16 * group,
        64 * group,
        grant=SMALL,
    )(jnp.stack([ix, ic]).astype(jnp.int32), stats)
    totals, unit_2, place_2 = lax.optimization_barrier((totals, unit_2, place_2))
    totals = lax.all_to_all(totals, "z", 0, 0)

    pull = call(
        lambda *refs: pull_kernel(batch, *refs),
        [VM] * 9,
        VM,
        jax.ShapeDtypeStruct((nx, line_rows + PAD, width), BF16),
        4 * held * group * width,
        2 * held * width,
        held * group,
    )(rows, sums, gain, bias, place, totals, unit, w_own, w_other)

    piece = jax.ShapeDtypeStruct((quarter, width), BF16)
    mine, *sent = call(
        lambda *refs: raw_kernel(nr, *refs),
        [SM] + [VM] * 6 + [HB],
        [HO] * nr,
        [jax.ShapeDtypeStruct((quarter, width), F32)] + [piece] * (nr - 1),
        4 * held * group * width,
        2 * held * width,
        held * group,
        [
            pltpu.VMEM((quarter, width), F32),
            pltpu.VMEM((nr - 1, quarter, width), BF16),
            pltpu.SemaphoreType.DMA((nr,)),
        ],
    )(at, place, place_2, totals, unit, unit_2, w_own, pull)
    far_first = sorted(range(1, nr), key=lambda by: -min(by, nr - by))
    came = [shift(sent[by - 1], "rep", by) for by in far_first]
    grad = call(
        lambda *refs: project_kernel(nr, *refs),
        [SM, HB] + [VM] * nr,
        VM,
        piece,
        20 * quarter * width,
        14 * quarter * width,
        0,
        [pltpu.VMEM((quarter, width), BF16), pltpu.SemaphoreType.DMA],
        grant=SMALL,
    )(at, picked, mine, *came)
    pull = lax.all_to_all(pull, "x", 0, 0)
    pull, mine = lax.optimization_barrier((pull, mine))
    lanes = min(width, 128)
    tall = (rows_dev + 4) * (width // lanes)
    pull = call(
        lambda *refs: mid_kernel(rows_dev, *refs),
        [VM],
        VM,
        jax.ShapeDtypeStruct((nz, tall, lanes), BF16),
        nx * line_rows * width,
        2 * nx * line_rows * width,
        grant=SMALL,
    )(pull)
    pull = lax.all_to_all(pull, "z", 0, 0)
    grad_unit, ends = call(
        lambda *refs: home_kernel(rows_dev, *refs),
        [VM],
        [VM] * 2,
        [
            jax.ShapeDtypeStruct((rows_dev, width), F32),
            jax.ShapeDtypeStruct((nc * nr, 2, width), F32),
        ],
        nz * tall * lanes,
        2 * nz * tall * lanes,
        grant=SMALL,
    )(pull)
    ends = lax.all_to_all(ends, ("core", "rep"), 0, 0)

    own = jnp.stack([(ix * nz + iz) * rows_dev, group + iz * rows_dev])
    terms, row_loss = call(
        lambda *refs: own_kernel(batch, *refs),
        [SM] + [VM] * 6,
        [VM] * 2,
        [
            jax.ShapeDtypeStruct((3 * rows_dev, width), F32),
            jax.ShapeDtypeStruct((1, rows_dev), F32),
        ],
        40 * rows_dev * width,
        40 * rows_dev * width,
        grant=SMALL,
    )(own.astype(jnp.int32), embeddings, sums, gain, bias, grad_unit, totals)
    emb_grad, centre_grad, gain_grad, bias_grad = call(
        lambda *refs: final_kernel(nr, *refs),
        [SM] + [VM] * (2 + nr),
        [VM] * 4,
        [
            jax.ShapeDtypeStruct((rows_dev, width), F32),
            jax.ShapeDtypeStruct((slots, width), BF16),
            jax.ShapeDtypeStruct((1, width), F32),
            jax.ShapeDtypeStruct((1, width), F32),
        ],
        slots * width,
        4 * slots * width,
        grant=SMALL,
    )(at, terms, ends, grad, *[shift(grad, "rep", by) for by in range(1, nr)])
    return (row_loss[0], emb_grad, centre_grad, gain_grad[0], bias_grad[0])


def solution(mesh):
    shards, replicas = mesh.devices.shape
    split = (4, shards // 8, 2, replicas)
    fine = Mesh(mesh.devices.reshape(split), ("x", "z", "core", "rep"))
    cen = ("x", "z", "core")
    every = cen + ("rep",)
    return jax.shard_map(
        body,
        mesh=fine,
        in_specs=(
            P(every, None),
            P(),
            P(),
            P(cen, None),
            P(cen, None),
            P(None, "rep", None),
            P(None, "rep", None),
        ),
        out_specs=(P(every), P(every, None), P(cen, None), P(), P()),
        check_vma=False,
    )
```

```python
import math

import jax
import jax.numpy as jnp
from jax import lax
from jax.experimental import pallas as pl
from jax.experimental.pallas import tpu as pltpu
from jax.sharding import Mesh, PartitionSpec as P

LOGIT_SCALE = 64.0
MARGIN = 0.4
EPSILON = 1e-05
SHRINK = math.exp(-LOGIT_SCALE * MARGIN)
F32 = jnp.float32
BF16 = jnp.bfloat16
LARGE = 60 * 1024 * 1024
SMALL = 20 * 1024 * 1024
PAD = 16


def spread(block, axes):
    copies = jnp.broadcast_to(block[None], (lax.axis_size(axes),) + block.shape)
    return lax.all_to_all(copies, axes, 0, 0)


def shift(block, axis, by):
    n = lax.axis_size(axis)
    return lax.ppermute(block, axis, [(i, (i + by) % n) for i in range(n)])


def head(inputs, sums, gain, bias, batch_total):
    mean = sums[0:1] / batch_total
    inv_std = lax.rsqrt(sums[1:2] / batch_total - mean * mean + EPSILON)
    normed = (inputs.astype(F32) - mean) * inv_std
    shifted = normed * gain + bias
    scale = lax.rsqrt(jnp.sum(shifted * shifted, 1, keepdims=True) + EPSILON)
    return normed, shifted * scale, scale, inv_std


VM = pl.BlockSpec(memory_space=pltpu.VMEM)
SM = pl.BlockSpec(memory_space=pltpu.SMEM)
HB = pl.BlockSpec(memory_space=pl.ANY)
HO = pl.BlockSpec(memory_space=pltpu.HBM)


def call(kernel, ins, outs, shapes, flops, size, exps=0, scratch=(), grant=LARGE):
    return pl.pallas_call(
        kernel,
        in_specs=ins,
        out_specs=outs,
        out_shape=shapes,
        scratch_shapes=list(scratch),
        compiler_params=pltpu.CompilerParams(vmem_limit_bytes=grant),
        cost_estimate=pl.CostEstimate(
            flops=flops, bytes_accessed=size, transcendentals=exps
        ),
    )


def hits(place, block, count, first):
    return place == lax.broadcasted_iota(jnp.int32, (block, count), 0) + first


def cosine_of(w_hat, unit, place, first):
    cosine = lax.dot_general(
        w_hat, unit, (((1,), (1,)), ((), ())), preferred_element_type=F32
    )
    return cosine, hits(place, w_hat.shape[0], unit.shape[0], first)


def grad_of(w_hat, unit, place, first, inverse):
    cosine, target = cosine_of(w_hat, unit, place, first)
    share = jnp.exp(LOGIT_SCALE * cosine) * inverse
    return jnp.where(target, share * SHRINK - 1.0, share).astype(BF16)


def blocks_of(w_own, w_other):
    block = w_own.shape[0] // 2
    for i in range(4):
        source = w_own if i < 2 else w_other
        yield source[(i % 2) * block : (i % 2 + 1) * block], i * block


def exp_kernel(batch, rows, sums, gain, bias, place, w_own, w_other, unit, stats):
    total = jnp.sum(sums[...], 0)
    units = head(rows[...], total, gain[...], bias[...], batch)[1].astype(BF16)
    unit[...] = units
    exps = hit = None
    for w_hat, first in blocks_of(w_own, w_other):
        cosine, target = cosine_of(w_hat, units, place[...], first)
        term = jnp.exp(LOGIT_SCALE * cosine)
        term = jnp.sum(jnp.where(target, term * SHRINK, term), 0, keepdims=True)
        other = jnp.sum(jnp.where(target, cosine, 0.0), 0, keepdims=True)
        exps = term if exps is None else exps + term
        hit = other if hit is None else hit + other
    hit = jnp.where(place[...] >= 0, LOGIT_SCALE * hit - LOGIT_SCALE * MARGIN, 0.0)
    both = jnp.concatenate([exps, hit], 0)
    for p in range(stats.shape[0]):
        stats[p] = both


def pull_kernel(
    batch, rows, sums, gain, bias, place, totals, unit, w_own, w_other, packed
):
    units = unit[...]
    inverse = 1.0 / jnp.sum(totals[...], 0)[0:1, : units.shape[0]]
    pull = None
    for w_hat, first in blocks_of(w_own, w_other):
        grad = grad_of(w_hat, units, place[...], first, inverse)
        term = lax.dot_general(
            grad, w_hat, (((0,), (0,)), ((), ())), preferred_element_type=F32
        )
        pull = term if pull is None else pull + term
    total = jnp.sum(sums[...], 0)
    normed, unit_f, scale, _ = head(rows[...], total, gain[...], bias[...], batch)
    radial = jnp.sum(unit_f * pull, 1, keepdims=True)
    shifts = (pull - unit_f * radial) * scale
    bias_part = jnp.sum(shifts, 0, keepdims=True)
    gain_part = jnp.sum(shifts * normed, 0, keepdims=True)
    tail = tail_of(bias_part, gain_part)
    parts = packed.shape[0]
    n = pull.shape[0] // parts
    for p in range(parts):
        packed[p, :n] = pull[p * n : (p + 1) * n].astype(BF16)
        packed[p, n:] = tail


def tail_of(bias_part, gain_part):
    pieces = split(bias_part, 3) + split(gain_part, 3)
    fill = jnp.zeros((PAD - 6, bias_part.shape[1]), F32)
    return jnp.concatenate(pieces + [fill], 0).astype(BF16)


def sums_of(tail):
    return jnp.concatenate(
        [jnp.sum(tail[k : k + 3], 0, keepdims=True) for k in (0, 3)], 0
    )


def split(value, count):
    pieces = []
    for _ in range(count):
        piece = value.astype(BF16).astype(F32)
        value = value - piece
        pieces.append(piece)
    return pieces


def total_kernel(lines, at, arrived, out):
    group = arrived.shape[2]
    n = group // lines
    place = at[0] * n if n % 128 else pl.multiple_of(at[0] * n, 128)
    own = other = hit = 0.0
    for x in range(lines):
        own = own + arrived[2 * x + at[1], 0:1]
        other = other + arrived[2 * x + 1 - at[1], 0:1]
        hit = hit + arrived[2 * x + at[1], 1:2, pl.ds(place, n)]
    both = jnp.concatenate(
        [
            jnp.concatenate([own, hit], 1),
            jnp.concatenate([other, jnp.zeros_like(hit)], 1),
        ],
        0,
    )
    for p in range(out.shape[0]):
        out[p] = both


def mid_kernel(rows_dev, arrived, packed):
    lines, _, lane = packed.shape
    total = jnp.sum(arrived[...].astype(F32), 0)
    width = total.shape[1]
    cuts = [slice(k, k + lane) for k in range(0, width, lane)]
    ends = sums_of(total[lines * rows_dev :])
    rows = split(ends[0:1], 2) + split(ends[1:2], 2)
    tail = [row[:, cut] for row in rows for cut in cuts]
    for p in range(lines):
        piece = total[p * rows_dev : (p + 1) * rows_dev]
        packed[p] = jnp.concatenate([piece[:, c] for c in cuts] + tail, 0).astype(BF16)


def home_kernel(rows_dev, arrived, grad, ends):
    total = jnp.sum(arrived[...].astype(F32), 0)
    lane = total.shape[1]
    n = grad.shape[1] // lane
    grad[...] = jnp.concatenate(
        [total[k * rows_dev : (k + 1) * rows_dev] for k in range(n)], 1
    )
    tail = total[n * rows_dev :]
    rows = []
    for v in range(2):
        both = tail[2 * v * n : (2 * v + 1) * n] + tail[(2 * v + 1) * n : (2 * v + 2) * n]
        rows.append(jnp.concatenate([both[k : k + 1] for k in range(n)], 1))
    both = jnp.concatenate(rows, 0)
    for p in range(ends.shape[0]):
        ends[p] = both


def raw_kernel(parts, at, place, place_2, totals, unit, unit_2, w_own, _, *refs):
    outs, (mine, sent, sems) = refs[:parts], refs[parts:]
    block = mine.shape[0]
    copies = []
    group = unit.shape[0]
    inverse = 1.0 / jnp.sum(totals[...], 0)[:, :group]
    for i in range(parts):
        first = pl.multiple_of(lax.rem(at[0] + i, parts) * block, 64)
        w_hat = w_own[pl.ds(first, block)]
        raw = None
        for units, places, row in ((unit, place, 0), (unit_2, place_2, 1)):
            grad = grad_of(
                w_hat, units[...], places[...], first, inverse[row : row + 1]
            )
            term = jnp.dot(grad, units[...], preferred_element_type=F32)
            raw = term if raw is None else raw + term
        if i == 0:
            mine[...] = raw
            source = mine
        else:
            sent[i - 1] = raw.astype(BF16)
            source = sent.at[i - 1]
        copies.append(pltpu.make_async_copy(source, outs[i], sems.at[i]))
        copies[-1].start()
    for copy in copies:
        copy.wait()


def project_kernel(parts, at, picked, *refs):
    found, (out, picks_ref, sem) = refs[:parts], refs[parts:]
    block = out.shape[0]
    rows = pl.ds(pl.multiple_of(at[0] * block, 64), block)
    copy = pltpu.make_async_copy(picked.at[rows], picks_ref, sem)
    copy.start()
    raw = found[0][...]
    for piece in found[1:]:
        raw = raw + piece[...].astype(F32)
    copy.wait()
    picks = picks_ref[...].astype(F32)
    inv_norm = lax.rsqrt(jnp.sum(picks * picks, 1, keepdims=True) + EPSILON)
    w_unit = picks * inv_norm
    along = jnp.sum(w_unit * raw, 1, keepdims=True)
    out[...] = ((raw - w_unit * along) * inv_norm).astype(BF16)


def own_kernel(batch, at, inputs, sums, gain, bias, grad_unit, totals, terms, loss):
    n = inputs.shape[0]
    total = jnp.sum(sums[...], 0)
    normed, unit_f, scale, inv_std = head(
        inputs[...], total, gain[...], bias[...], batch
    )
    pull = grad_unit[...]
    radial = jnp.sum(unit_f * pull, 1, keepdims=True)
    shifts = (pull - unit_f * radial) * scale
    share = inv_std * gain[...]
    terms[0:n] = shifts * share
    terms[n : 2 * n] = normed * (share / batch)
    terms[2 * n : 3 * n] = jnp.broadcast_to(share / batch, (n, share.shape[1]))
    own = jnp.sum(totals[...], 0)[0:1]
    shape = (n, own.shape[1])
    ahead = lax.broadcasted_iota(jnp.int32, shape, 1) - lax.broadcasted_iota(
        jnp.int32, shape, 0
    )
    found = [
        jnp.sum(jnp.where(ahead == at[k], own, 0.0), 1, keepdims=True) for k in (0, 1)
    ]
    values = jnp.log(found[0]) - found[1]
    square = (n, n)
    same = lax.broadcasted_iota(jnp.int32, square, 0) == lax.broadcasted_iota(
        jnp.int32, square, 1
    )
    loss[...] = jnp.sum(jnp.where(same, values, 0.0), 0, keepdims=True)


def final_kernel(parts, at, terms, ends, *refs):
    found, (emb, grad, gain_grad, bias_grad) = refs[:parts], refs[parts:]
    block = found[0].shape[0]
    n = emb.shape[0]
    both = jnp.sum(ends[...], 0)
    bias_grad[...] = both[0:1]
    gain_grad[...] = both[1:2]
    emb[...] = (
        terms[0:n] - terms[2 * n : 3 * n] * both[0:1] - terms[n : 2 * n] * both[1:2]
    )
    for by, piece in enumerate(found):
        where = lax.rem(at[0] - by + parts, parts) * block
        grad[pl.ds(pl.multiple_of(where, 64), block)] = piece[...]


def body(embeddings, bn_gain, bn_bias, centres, sample_rows, label_shard, label_slot):
    nx, nz, nc, nr = (lax.axis_size(a) for a in ("x", "z", "core", "rep"))
    ix, iz, ic, ir = (lax.axis_index(a) for a in ("x", "z", "core", "rep"))
    rows_dev, width = embeddings.shape
    slots = sample_rows.shape[1]
    batch = rows_dev * nx * nz * nc * nr
    line_rows = nz * rows_dev
    group = nx * line_rows
    held = nc * slots
    quarter = slots // nr
    at = ir.astype(jnp.int32).reshape(1)
    gain, bias = bn_gain[None], bn_bias[None]

    picked = centres.at[sample_rows[0]].get(mode="promise_in_bounds")
    picks = picked.astype(F32)
    inv_norm = lax.rsqrt(jnp.sum(picks * picks, 1, keepdims=True) + EPSILON)
    w_own = (picks * inv_norm).astype(BF16)

    line = spread(embeddings, "z").reshape(line_rows, width)
    line, w_own = lax.optimization_barrier((line, w_own))
    rows = spread(line, "x").reshape(group, width)
    rows_f = rows.astype(F32)
    sums = spread(
        jnp.stack([jnp.sum(rows_f, 0), jnp.sum(rows_f * rows_f, 0)]), ("core", "rep")
    )
    w_other = shift(w_own, "core", 1)

    def of_core(labels, core):
        lines = labels.reshape(nx * nz, nc, rows_dev)
        return lax.dynamic_index_in_dim(lines, core, 1).reshape(1, group)

    owner, slot = of_core(label_shard, ic), of_core(label_slot, ic)
    chip = (ix * nz + iz) * nc
    place = jnp.where(
        owner == chip + ic, slot, jnp.where(owner == chip + 1 - ic, slot + slots, -1)
    )
    place_2 = jnp.where(
        of_core(label_shard, 1 - ic) == chip + ic, of_core(label_slot, 1 - ic), -1
    )

    unit, stats = call(
        lambda *refs: exp_kernel(batch, *refs),
        [VM] * 7,
        [VM] * 2,
        [
            jax.ShapeDtypeStruct((group, width), BF16),
            jax.ShapeDtypeStruct((nx * nc, 2, group), F32),
        ],
        2 * held * group * width,
        2 * held * width,
        held * group,
    )(rows, sums, gain, bias, place, w_own, w_other)
    unit_2 = shift(unit, "core", 1)

    stats = lax.all_to_all(stats, ("x", "core"), 0, 0)
    totals = call(
        lambda *refs: total_kernel(nx, *refs),
        [SM, VM],
        VM,
        jax.ShapeDtypeStruct((nz, nc, group + line_rows), F32),
        16 * group,
        64 * group,
        grant=SMALL,
    )(jnp.stack([ix, ic]).astype(jnp.int32), stats)
    totals, unit_2, place_2 = lax.optimization_barrier((totals, unit_2, place_2))
    totals = lax.all_to_all(totals, "z", 0, 0)

    pull = call(
        lambda *refs: pull_kernel(batch, *refs),
        [VM] * 9,
        VM,
        jax.ShapeDtypeStruct((nx, line_rows + PAD, width), BF16),
        4 * held * group * width,
        2 * held * width,
        held * group,
    )(rows, sums, gain, bias, place, totals, unit, w_own, w_other)

    piece = jax.ShapeDtypeStruct((quarter, width), BF16)
    mine, *sent = call(
        lambda *refs: raw_kernel(nr, *refs),
        [SM] + [VM] * 6 + [HB],
        [HO] * nr,
        [jax.ShapeDtypeStruct((quarter, width), F32)] + [piece] * (nr - 1),
        4 * held * group * width,
        2 * held * width,
        held * group,
        [
            pltpu.VMEM((quarter, width), F32),
            pltpu.VMEM((nr - 1, quarter, width), BF16),
            pltpu.SemaphoreType.DMA((nr,)),
        ],
    )(at, place, place_2, totals, unit, unit_2, w_own, pull)
    far_first = sorted(range(1, nr), key=lambda by: -min(by, nr - by))
    came = [shift(sent[by - 1], "rep", by) for by in far_first]
    grad = call(
        lambda *refs: project_kernel(nr, *refs),
        [SM, HB] + [VM] * nr,
        VM,
        piece,
        20 * quarter * width,
        14 * quarter * width,
        0,
        [pltpu.VMEM((quarter, width), BF16), pltpu.SemaphoreType.DMA],
        grant=SMALL,
    )(at, picked, mine, *came)
    pull = lax.all_to_all(pull, "x", 0, 0)
    pull, mine = lax.optimization_barrier((pull, mine))
    lanes = min(width, 128)
    tall = (rows_dev + 4) * (width // lanes)
    pull = call(
        lambda *refs: mid_kernel(rows_dev, *refs),
        [VM],
        VM,
        jax.ShapeDtypeStruct((nz, tall, lanes), BF16),
        nx * line_rows * width,
        2 * nx * line_rows * width,
        grant=SMALL,
    )(pull)
    pull = lax.all_to_all(pull, "z", 0, 0)
    grad_unit, ends = call(
        lambda *refs: home_kernel(rows_dev, *refs),
        [VM],
        [VM] * 2,
        [
            jax.ShapeDtypeStruct((rows_dev, width), F32),
            jax.ShapeDtypeStruct((nc * nr, 2, width), F32),
        ],
        nz * tall * lanes,
        2 * nz * tall * lanes,
        grant=SMALL,
    )(pull)
    ends = lax.all_to_all(ends, ("core", "rep"), 0, 0)

    own = jnp.stack([(ix * nz + iz) * rows_dev, group + iz * rows_dev])
    terms, row_loss = call(
        lambda *refs: own_kernel(batch, *refs),
        [SM] + [VM] * 6,
        [VM] * 2,
        [
            jax.ShapeDtypeStruct((3 * rows_dev, width), F32),
            jax.ShapeDtypeStruct((1, rows_dev), F32),
        ],
        40 * rows_dev * width,
        40 * rows_dev * width,
        grant=SMALL,
    )(own.astype(jnp.int32), embeddings, sums, gain, bias, grad_unit, totals)
    moved = {by: shift(grad, "rep", by) for by in reversed(far_first)}
    emb_grad, centre_grad, gain_grad, bias_grad = call(
        lambda *refs: final_kernel(nr, *refs),
        [SM] + [VM] * (2 + nr),
        [VM] * 4,
        [
            jax.ShapeDtypeStruct((rows_dev, width), F32),
            jax.ShapeDtypeStruct((slots, width), BF16),
            jax.ShapeDtypeStruct((1, width), F32),
            jax.ShapeDtypeStruct((1, width), F32),
        ],
        slots * width,
        4 * slots * width,
        grant=SMALL,
    )(at, terms, ends, grad, *[moved[by] for by in range(1, nr)])
    return (row_loss[0], emb_grad, centre_grad, gain_grad[0], bias_grad[0])


def solution(mesh):
    shards, replicas = mesh.devices.shape
    split = (4, shards // 8, 2, replicas)
    fine = Mesh(mesh.devices.reshape(split), ("x", "z", "core", "rep"))
    cen = ("x", "z", "core")
    every = cen + ("rep",)
    return jax.shard_map(
        body,
        mesh=fine,
        in_specs=(
            P(every, None),
            P(),
            P(),
            P(cen, None),
            P(cen, None),
            P(None, "rep", None),
            P(None, "rep", None),
        ),
        out_specs=(P(every), P(every, None), P(cen, None), P(), P()),
        check_vma=False,
    )
```
